32 devices in a mesh: dp: 8 (over z, core), fsdp: 4 (over y, x).
Axes of the slice: x: 2, y: 2, z: 4, core: 2. Of those that a mesh axis runs over, the one named last changes fastest.
Arguments:
- inputs: bfloat16 [8, 2, 1024, 2048], P('dp', None, 'fsdp'), may hold values from -6 to 6
- cotangent: bfloat16 [8, 2, 1024, 2048], P('dp', None, 'fsdp'), may hold values from -6 to 6
- lengths: int32 [8, 2], replicated, may hold values from 512 to 1024, as said below
- dealing: int32 [2, 8], replicated, may hold values from 0 to 7, as said below
- query_weight: bfloat16 [2048, 2048], P('dp', 'fsdp'), may hold values from -0.125 to 0.125
- key_weight: bfloat16 [2048, 512], P('dp', 'fsdp'), may hold values from -0.125 to 0.125
- value_weight: bfloat16 [2048, 512], P('dp', 'fsdp'), may hold values from -0.125 to 0.125
- output_weight: bfloat16 [2048, 2048], P('fsdp', 'dp'), may hold values from -0.375 to 0.375
- gate_weight: bfloat16 [2048, 8192], P('dp', 'fsdp'), may hold values from -0.125 to 0.125
- up_weight: bfloat16 [2048, 8192], P('dp', 'fsdp'), may hold values from -0.125 to 0.125
- down_weight: bfloat16 [8192, 2048], P('fsdp', 'dp'), may hold values from -0.0625 to 0.0625
- adapter_down_weights: bfloat16 [2048, 32], P(('dp', 'fsdp')), may hold values from -0.125 to 0.125
- adapter_up_query_output: bfloat16 [2048, 16], P(('dp', 'fsdp')), may hold values from -2 to 2
- adapter_up_key_value: bfloat16 [512, 16], P(('dp', 'fsdp')), may hold values from -2 to 2
- query_feature_weights: bfloat16 [2048, 64], P(('dp', 'fsdp')), may hold values from -0.75 to 0.75
- key_feature_weights: bfloat16 [512, 64], P(('dp', 'fsdp')), may hold values from -0.75 to 0.75
- norm_gain_weights: bfloat16 [2048, 2], P(('dp', 'fsdp')), may hold values from 0.5 to 1.5
Outputs:
- output: bfloat16 [8, 2, 1024, 2048], P('dp', None, 'fsdp')
- input_grad: bfloat16 [8, 2, 1024, 2048], P('dp', None, 'fsdp')
- lora_in_grad: float32 [2048, 32], P(('dp', 'fsdp'))
- lora_up_d_grad: float32 [2048, 16], P(('dp', 'fsdp'))
- lora_up_kv_grad: float32 [512, 16], P(('dp', 'fsdp'))
- fmap_q_grad: float32 [2048, 64], P(('dp', 'fsdp'))
- fmap_k_grad: float32 [512, 64], P(('dp', 'fsdp'))
- norm_gains_grad: float32 [2048, 2], P(('dp', 'fsdp'))
The draws below stay inside these ranges and needn't reach their ends.
Inputs may be any that keep to these rules, and one draw needn't show every extreme that they name: Each row of dealing is a permutation of the groups. A sequence fills the first lengths[i, m] positions of its block; the rest is padding.
All inputs are finite; a program needn't handle non-finite values.
Results may differ from the reference program's by a relative error of at most 0.018.
Values may be sent and summed in bfloat16 or wider, within the bound.
No kernel may reach another device: no remote copies, remote signals or barrier semaphores. Data moves between devices by JAX's collectives and lax.ppermute only.
A program may use at most 896 MiB of HBM per device.

```python
import math
import jax
import jax.numpy as jnp
from jax import lax

MODEL_WIDTH = 2048
H = 32
KEY_VALUE_HEADS = 8
HEAD_SIZE = 64
FF = 8192
ADAPTER_RANK = 8
WIN = 64
MICRO = 2
GROUPS = 8
BLOCK = 1024
LOW_LEN = 512


def dealing_and_lengths(key):
    perm_keys = jax.random.split(jax.random.fold_in(key, 101), MICRO)
    dealing = jnp.stack([jax.random.permutation(perm_keys[micro_index], GROUPS) for micro_index in range(MICRO)]).astype(jnp.int32)
    base_len = jax.random.randint(jax.random.fold_in(key, 103), (GROUPS, MICRO), LOW_LEN, BLOCK + 1)
    picked = jax.random.randint(jax.random.fold_in(key, 107), (GROUPS,), 0, MICRO)
    short_group = jax.random.randint(jax.random.fold_in(key, 109), (), 0, GROUPS)
    targets = jnp.transpose(dealing)
    micro_ids = jnp.arange(MICRO, dtype=jnp.int32)[None, :]
    full_mask = picked[targets] == micro_ids
    short_mask = (targets == short_group) & jnp.logical_not(full_mask)
    lengths = jnp.where(full_mask, BLOCK, jnp.where(short_mask, LOW_LEN, base_len))
    return (dealing, lengths.astype(jnp.int32))


def draw_dealing(key, part):
    return dealing_and_lengths(key)[0]


def draw_lengths(key, part):
    return dealing_and_lengths(key)[1]


def shard_levels(stream_key, dims, shards, low, high):
    def one(axis_at, parts):
        steps = jax.random.uniform(jax.random.fold_in(jax.random.fold_in(stream_key, 6), axis_at), (parts,), jnp.float32, low / len(shards), high / len(shards))
        return jnp.repeat(jnp.exp(steps), dims[axis_at] // parts).reshape((-1,) + (1,) * (len(dims) - axis_at - 1))

    level = one(*shards[0])
    for cut in shards[1:]:
        level = level * one(*cut)
    return level


def noise(own_key, extent, deviation, limit, pieces=(), held_as=jnp.bfloat16):
    values = deviation * jax.random.normal(own_key, extent, jnp.float32)
    if pieces:
        values = values * shard_levels(own_key, extent, pieces, -0.22, 0.18)
    return jnp.clip(values, -limit, limit).astype(held_as)


def setup_inputs(seed: int = 0) -> dict:
    splits = jax.random.split(jax.random.key(seed), 18)
    return {
        "inputs": noise(splits[0], (GROUPS, MICRO, BLOCK, MODEL_WIDTH), 1.0, 6.0, ((0, 8), (2, 4))),
        "cotangent": noise(splits[1], (GROUPS, MICRO, BLOCK, MODEL_WIDTH), 1.0, 6.0, ((0, 8), (2, 4))),
        "lengths": draw_lengths(jax.random.fold_in(splits[17], 71), 0),
        "dealing": draw_dealing(jax.random.fold_in(splits[17], 71), 0),
        "query_weight": noise(splits[4], (MODEL_WIDTH, MODEL_WIDTH), MODEL_WIDTH ** -0.5, 0.125, ((0, 8), (1, 4))),
        "key_weight": noise(splits[5], (MODEL_WIDTH, KEY_VALUE_HEADS * HEAD_SIZE), MODEL_WIDTH ** -0.5, 0.125, ((0, 8), (1, 4))),
        "value_weight": noise(splits[6], (MODEL_WIDTH, KEY_VALUE_HEADS * HEAD_SIZE), MODEL_WIDTH ** -0.5, 0.125, ((0, 8), (1, 4))),
        "output_weight": noise(splits[7], (MODEL_WIDTH, MODEL_WIDTH), (MODEL_WIDTH // 8) ** -0.5, 0.375, ((0, 4), (1, 8))),
        "gate_weight": noise(splits[8], (MODEL_WIDTH, FF), MODEL_WIDTH ** -0.5, 0.125, ((0, 8), (1, 4))),
        "up_weight": noise(splits[9], (MODEL_WIDTH, FF), MODEL_WIDTH ** -0.5, 0.125, ((0, 8), (1, 4))),
        "down_weight": noise(splits[10], (FF, MODEL_WIDTH), FF ** -0.5, 0.0625, ((0, 4), (1, 8))),
        "adapter_down_weights": noise(splits[11], (MODEL_WIDTH, 4 * ADAPTER_RANK), MODEL_WIDTH ** -0.5, 0.125, ((0, 32),)),
        "adapter_up_query_output": noise(splits[12], (MODEL_WIDTH, 2 * ADAPTER_RANK), ADAPTER_RANK ** -0.5, 2.0, ((0, 32),)),
        "adapter_up_key_value": noise(splits[13], (KEY_VALUE_HEADS * HEAD_SIZE, 2 * ADAPTER_RANK), ADAPTER_RANK ** -0.5, 2.0, ((0, 32),)),
        "query_feature_weights": noise(splits[14], (H * HEAD_SIZE, HEAD_SIZE), HEAD_SIZE ** -0.5, 0.75, ((0, 32),)),
        "key_feature_weights": noise(splits[15], (KEY_VALUE_HEADS * HEAD_SIZE, HEAD_SIZE), HEAD_SIZE ** -0.5, 0.75, ((0, 32),)),
        "norm_gain_weights": jnp.clip(1.0 + 0.1 * jax.random.normal(splits[16], (MODEL_WIDTH, 2), jnp.float32), 0.5, 1.5).astype(jnp.bfloat16),
    }


EPSILON = 1e-05
ROPE_BASE = 500000.0
EXACT_PRECISION = lax.Precision.HIGHEST

@jax.custom_vjp
def low(v):
    return lax.optimization_barrier(v.astype(jnp.bfloat16)).astype(jnp.float32)

@jax.custom_vjp
def rank_backward_pass(v):
    return v

def low_keep(v):
    return (low(v), None)

def low_pass(kept, grad):
    return (grad,)

def back_keep(v):
    return (v, None)

def back_low(kept, grad):
    return (low(grad),)
low.defvjp(low_keep, low_pass)
rank_backward_pass.defvjp(back_keep, back_low)

def forward_and_backward(value):
    return low(rank_backward_pass(value))

def matrix_product(left_side, right_side):
    return jnp.dot(left_side, right_side, precision=EXACT_PRECISION, preferred_element_type=jnp.float32)

def rope_tables(positions):
    half_size = HEAD_SIZE // 2
    frequencies = jnp.exp(-(2.0 * jnp.arange(half_size, dtype=jnp.float32) / HEAD_SIZE) * math.log(ROPE_BASE))
    angles = positions.astype(jnp.float32)[:, None] * frequencies[None, :]
    return (jnp.cos(angles), jnp.sin(angles))

def rotate(heads, cosine, sine_part):
    half_size = heads.shape[-1] // 2
    front_half = heads[..., :half_size]
    back_half = heads[..., half_size:]
    cos_rows = cosine[:, None, :]
    sin_rows = sine_part[:, None, :]
    return jnp.concatenate([front_half * cos_rows - back_half * sin_rows, back_half * cos_rows + front_half * sin_rows], axis=-1)

def rms_scale(value_rows):
    return lax.rsqrt(lax.optimization_barrier(jnp.mean(value_rows * value_rows, axis=-1, keepdims=True)) + EPSILON)

def attention_masks(query_pos, key_pos):
    distance = query_pos[:, None] - key_pos[None, :]
    key_valid = (key_pos >= 0)[None, :]
    window_mask = (distance >= 0) & (distance < WIN) & key_valid
    band_mask = (key_pos[None, :] // WIN == query_pos[:, None] // WIN - 1) & (distance >= WIN) & key_valid
    return (window_mask, band_mask)

def attention(q_rot, k_rot, value_rows, q_feat, k_feat):
    total_rows = q_rot.shape[0]
    repeat = H // KEY_VALUE_HEADS
    span_count = total_rows // WIN
    key_spans = k_feat.reshape(span_count, WIN, KEY_VALUE_HEADS, 2 * HEAD_SIZE)
    contrib = jnp.einsum('cwgf,cwgd->cgfd', key_spans, value_rows.reshape(span_count, WIN, KEY_VALUE_HEADS, HEAD_SIZE), precision=EXACT_PRECISION)
    running = jnp.cumsum(contrib, axis=0)
    states = jnp.concatenate([jnp.zeros((2, KEY_VALUE_HEADS, 2 * HEAD_SIZE, HEAD_SIZE), jnp.float32), running[:-2]], axis=0)
    norm_running = jnp.cumsum(lax.optimization_barrier(jnp.sum(key_spans, axis=1)), axis=0)
    norm_states = jnp.concatenate([jnp.zeros((2, KEY_VALUE_HEADS, 2 * HEAD_SIZE), jnp.float32), norm_running[:-2]], axis=0)
    key_pad = jnp.concatenate([jnp.zeros((WIN, KEY_VALUE_HEADS, HEAD_SIZE), jnp.float32), k_rot], axis=0)
    value_pad = jnp.concatenate([jnp.zeros((WIN, KEY_VALUE_HEADS, HEAD_SIZE), jnp.float32), value_rows], axis=0)
    feat_pad = jnp.concatenate([jnp.zeros((WIN, KEY_VALUE_HEADS, 2 * HEAD_SIZE), jnp.float32), k_feat], axis=0)
    block_rows = math.gcd(total_rows, 512)

    def one_block(block_index):
        start_row = (block_index * block_rows).astype(jnp.int32)
        query_block_rows = lax.dynamic_slice_in_dim(q_rot, start_row, block_rows, 0).reshape(block_rows, KEY_VALUE_HEADS, repeat, HEAD_SIZE)
        query_feature_block = lax.dynamic_slice_in_dim(q_feat, start_row, block_rows, 0).reshape(block_rows, KEY_VALUE_HEADS, repeat, 2 * HEAD_SIZE)
        key_block_rows = lax.dynamic_slice_in_dim(key_pad, start_row, block_rows + WIN, 0)
        value_block_rows = lax.dynamic_slice_in_dim(value_pad, start_row, block_rows + WIN, 0)
        key_feature_block = lax.dynamic_slice_in_dim(feat_pad, start_row, block_rows + WIN, 0)
        query_pos = start_row + jnp.arange(block_rows, dtype=jnp.int32)
        key_pos = start_row - WIN + jnp.arange(block_rows + WIN, dtype=jnp.int32)
        window_mask, band_mask = attention_masks(query_pos, key_pos)
        score_matrix = rank_backward_pass(jnp.einsum('yzpo,nzo->zpyn', query_block_rows, key_block_rows, precision=EXACT_PRECISION) / math.sqrt(HEAD_SIZE))
        linear_attention = rank_backward_pass(jnp.einsum('zbpj,qbj->bpzq', query_feature_block, key_feature_block, precision=EXACT_PRECISION))
        weight_matrix = jnp.where(window_mask, jnp.exp(score_matrix), 0.0) + jnp.where(band_mask, linear_attention, 0.0)
        first_span = (start_row // WIN).astype(jnp.int32)
        state_block = lax.dynamic_slice_in_dim(states, first_span, block_rows // WIN, 0)
        norm_block = lax.dynamic_slice_in_dim(norm_states, first_span, block_rows // WIN, 0)
        qf_spans = query_feature_block.reshape(block_rows // WIN, WIN, KEY_VALUE_HEADS, repeat, 2 * HEAD_SIZE)
        state_numerator = jnp.einsum('cwgrf,cgfd->cwgrd', qf_spans, state_block, precision=EXACT_PRECISION).reshape(block_rows, KEY_VALUE_HEADS, repeat, HEAD_SIZE)
        state_den = jnp.einsum('cwgrf,cgf->grcw', qf_spans, norm_block, precision=EXACT_PRECISION).reshape(KEY_VALUE_HEADS, repeat, block_rows)
        softmax_divisor = lax.optimization_barrier(jnp.sum(weight_matrix, axis=-1)) + state_den
        rank_weights = low(weight_matrix / softmax_divisor[..., None])
        combined_heads = jnp.einsum('qxlm,mqo->lqxo', rank_weights, value_block_rows, precision=EXACT_PRECISION) + state_numerator / jnp.transpose(softmax_divisor, (2, 0, 1))[..., None]
        return combined_heads.reshape(block_rows, H, HEAD_SIZE)
    block_outs = lax.map(jax.checkpoint(one_block), jnp.arange(total_rows // block_rows, dtype=jnp.int32))
    return block_outs.reshape(total_rows, H, HEAD_SIZE)

def one_sequence(sequence_tokens, length, trainable_weights, frozen):
    query_weight, key_weight, value_weight, output_weight, gate_weight, up_weight, down_weight = frozen
    adapter_down_weights, adapter_up_query_output, adapter_up_key_value, query_feature_weights, key_feature_weights, norm_gain_weights = trainable_weights
    total_rows = sequence_tokens.shape[0]
    positions = jnp.arange(total_rows, dtype=jnp.int32)
    cosine, sine_part = rope_tables(positions)
    normalized_attention_input = low(sequence_tokens * rms_scale(sequence_tokens) * norm_gain_weights[:, 0])
    adapter_rank_inputs = forward_and_backward(matrix_product(normalized_attention_input, adapter_down_weights[:, :3 * ADAPTER_RANK]))
    query_rows = rank_backward_pass(matrix_product(normalized_attention_input, query_weight) + matrix_product(adapter_rank_inputs[:, :ADAPTER_RANK], adapter_up_query_output[:, :ADAPTER_RANK].T))
    key_projected = rank_backward_pass(matrix_product(normalized_attention_input, key_weight) + matrix_product(adapter_rank_inputs[:, ADAPTER_RANK:2 * ADAPTER_RANK], adapter_up_key_value[:, :ADAPTER_RANK].T))
    value_rows = forward_and_backward(matrix_product(normalized_attention_input, value_weight) + matrix_product(adapter_rank_inputs[:, 2 * ADAPTER_RANK:3 * ADAPTER_RANK], adapter_up_key_value[:, ADAPTER_RANK:].T))
    q_rot = low(rotate(query_rows.reshape(total_rows, H, HEAD_SIZE), cosine, sine_part))
    k_rot = low(rotate(key_projected.reshape(total_rows, KEY_VALUE_HEADS, HEAD_SIZE), cosine, sine_part))
    q_map = rank_backward_pass(jnp.einsum('thd,hde->the', q_rot, query_feature_weights.reshape(H, HEAD_SIZE, HEAD_SIZE), precision=EXACT_PRECISION))
    k_map = rank_backward_pass(jnp.einsum('thd,hde->the', k_rot, key_feature_weights.reshape(KEY_VALUE_HEADS, HEAD_SIZE, HEAD_SIZE), precision=EXACT_PRECISION))
    q_feat = low(jnp.concatenate([jax.nn.softmax(q_map, axis=-1), jax.nn.softmax(-q_map, axis=-1)], axis=-1))
    k_feat = low(jnp.concatenate([jax.nn.softmax(k_map, axis=-1), jax.nn.softmax(-k_map, axis=-1)], axis=-1))
    combined_heads = attention(q_rot, k_rot, value_rows.reshape(total_rows, KEY_VALUE_HEADS, HEAD_SIZE), q_feat, k_feat)
    combined_rank_rows = forward_and_backward(combined_heads.reshape(total_rows, H * HEAD_SIZE))
    output_rank_rows = forward_and_backward(matrix_product(combined_rank_rows, adapter_down_weights[:, 3 * ADAPTER_RANK:]))
    middle_sum = sequence_tokens + rank_backward_pass(matrix_product(combined_rank_rows, output_weight) + matrix_product(output_rank_rows, adapter_up_query_output[:, ADAPTER_RANK:].T))
    normed_two = low(middle_sum * rms_scale(middle_sum) * norm_gain_weights[:, 1])
    gate_proj = rank_backward_pass(matrix_product(normed_two, gate_weight))
    up_proj = rank_backward_pass(matrix_product(normed_two, up_weight))
    hidden = low(jax.nn.silu(gate_proj) * up_proj)
    result = middle_sum + rank_backward_pass(matrix_product(hidden, down_weight))
    return jnp.where((positions < length)[:, None], result, 0.0)

def reference(inputs, cotangent, lengths, dealing, query_weight, key_weight, value_weight, output_weight, gate_weight, up_weight, down_weight, adapter_down_weights, adapter_up_query_output, adapter_up_key_value, query_feature_weights, key_feature_weights, norm_gain_weights):
    frozen = tuple((weight_matrix.astype(jnp.float32) for weight_matrix in (query_weight, key_weight, value_weight, output_weight, gate_weight, up_weight, down_weight)))
    trainable_weights = tuple((weight_matrix.astype(jnp.float32) for weight_matrix in (adapter_down_weights, adapter_up_query_output, adapter_up_key_value, query_feature_weights, key_feature_weights, norm_gain_weights)))
    inverse = jnp.argsort(dealing, axis=1).astype(jnp.int32)
    dealt_rows = jnp.stack([inputs[inverse[micro_index], micro_index] for micro_index in range(MICRO)], axis=1)
    dealt_len = jnp.stack([lengths[inverse[micro_index], micro_index] for micro_index in range(MICRO)], axis=1)
    flat_inputs = dealt_rows.reshape(GROUPS * MICRO, BLOCK, MODEL_WIDTH).astype(jnp.float32)
    flat_len = dealt_len.reshape(GROUPS * MICRO).astype(jnp.int32)

    def sequence_fn(sequence_tokens, length, weights):
        return one_sequence(sequence_tokens, length, weights, frozen)

    def forward(sequences, weights):

        def scan_step(carry_value, seq_item):
            return (carry_value, jax.checkpoint(sequence_fn)(seq_item[0], seq_item[1], weights))
        unused_carry, results = lax.scan(scan_step, jnp.zeros((), jnp.float32), (sequences, flat_len))
        return results
    outputs, pullback = jax.vjp(forward, flat_inputs, trainable_weights)
    grad_inputs, grad_train = pullback(cotangent.reshape(GROUPS * MICRO, BLOCK, MODEL_WIDTH).astype(jnp.float32))
    output = outputs.reshape(GROUPS, MICRO, BLOCK, MODEL_WIDTH).astype(jnp.bfloat16)
    grad_dealt = grad_inputs.reshape(GROUPS, MICRO, BLOCK, MODEL_WIDTH)
    input_grad = jnp.stack([grad_dealt[dealing[micro_index], micro_index] for micro_index in range(MICRO)], axis=1).astype(jnp.bfloat16)
    return (output, input_grad, grad_train[0], grad_train[1], grad_train[2], grad_train[3], grad_train[4], grad_train[5])
```

```python
import functools
import math

import jax
import jax.numpy as jnp
from jax import lax
from jax.experimental import pallas as pl
from jax.experimental.pallas import tpu as pltpu
from jax.sharding import PartitionSpec as P

H = 32
KEY_VALUE_HEADS = 8
REPEAT = H // KEY_VALUE_HEADS
HEAD_SIZE = 64
ADAPTER_RANK = 8
WIN = 64
AUG = 80
RANK_LANES = 128

EPSILON = 1e-05
ROPE_BASE = 500000.0
F32 = jnp.float32
BF16 = jnp.bfloat16
MIB = 1024 * 1024


def dot(a, b):
    return lax.dot_general(a, b, (((1,), (0,)), ((), ())), preferred_element_type=F32)


def dot_nt(a, b):
    return lax.dot_general(a, b, (((1,), (1,)), ((), ())), preferred_element_type=F32)


def params(mib, semantics=("arbitrary",)):
    return pltpu.CompilerParams(vmem_limit_bytes=mib * MIB, dimension_semantics=semantics)


def cost(flops, bytes_accessed, transcendentals=0):
    return pl.CostEstimate(
        flops=int(flops), bytes_accessed=int(bytes_accessed), transcendentals=int(transcendentals)
    )


def whole(shape):
    return pl.BlockSpec(shape, lambda *_: (0,) * len(shape))


def rope_tables_t(positions):
    half_size = HEAD_SIZE // 2
    frequencies = jnp.exp(
        -(2.0 * jnp.arange(half_size, dtype=F32) / HEAD_SIZE) * math.log(ROPE_BASE)
    )
    angles = frequencies[:, None] * positions.astype(F32)[None, :]
    return jnp.cos(angles), jnp.sin(angles)


def rotate_t(head, cos_t, sin_t):
    a, b = head[:32], head[32:]
    return jnp.concatenate([a * cos_t - b * sin_t, b * cos_t + a * sin_t], axis=0)


def rotate_back_t(head, cos_t, sin_t):
    a, b = head[:32], head[32:]
    return jnp.concatenate([a * cos_t + b * sin_t, b * cos_t - a * sin_t], axis=0)


def half_softmax_t(scores):
    e = jnp.exp(scores - jnp.max(scores, axis=0, keepdims=True))
    return e * (1.0 / jnp.sum(e, axis=0, keepdims=True))


def features_t(mapped):
    return jnp.concatenate([half_softmax_t(mapped[:64]), half_softmax_t(mapped[64:])], axis=0)


def features_back_t(e, f):
    ef = e * f
    t1 = jnp.sum(ef[:64], axis=0, keepdims=True)
    t2 = jnp.sum(ef[64:], axis=0, keepdims=True)
    return (ef[:64] - e[:64] * t1) - (ef[64:] - e[64:] * t2)


def project(h1_ref, u_ref, w_ref, b_ref, depth):
    total = dot(u_ref[...], b_ref[0])
    for j in range(w_ref.shape[0]):
        total += dot(h1_ref[:, j * depth : (j + 1) * depth], w_ref[j, 0])
    return total


def kv_kernel(kv_heads, micro, depth, h1_ref, u_ref, w_ref, b_ref, cos_ref, sin_ref, f_ref,
              n_ref, tot_ref):
    rows = h1_ref.shape[0] // micro
    kv_t = project(h1_ref, u_ref, w_ref, b_ref, depth).T
    cos_t, sin_t = cos_ref[...], sin_ref[...]
    width = kv_heads * HEAD_SIZE
    for g in range(kv_heads):
        kr = rotate_t(kv_t[g * 64 : (g + 1) * 64], cos_t, sin_t).astype(BF16)
        v = kv_t[width + g * 64 : width + (g + 1) * 64].astype(BF16)
        pk = features_t(dot(f_ref[g], kr)).astype(BF16)
        natural = (
            jnp.concatenate([pk.astype(F32), kr.astype(F32), v.astype(F32)], axis=0).T
        ).astype(BF16)
        v_aug = jnp.concatenate([v, jnp.ones((AUG - 64, v.shape[1]), BF16)], axis=0)
        for m in range(micro):
            part = natural[m * rows : (m + 1) * rows]
            n_ref[g, m] = part
            tot_ref[g, m] = dot(v_aug[:, m * rows : (m + 1) * rows], part[:, :128]).astype(BF16)


def q_kernel(heads, depth, h1_ref, u_ref, w_ref, b_ref, cos_ref, sin_ref, f_ref, qr_ref, pq_ref):
    q_t = project(h1_ref, u_ref, w_ref, b_ref, depth).T
    cos_t, sin_t = cos_ref[...], sin_ref[...]
    for h in range(heads):
        qr = rotate_t(q_t[h * 64 : (h + 1) * 64], cos_t, sin_t).astype(BF16)
        qr_ref[h * 64 : (h + 1) * 64] = qr
        pq_ref[h * 128 : (h + 1) * 128] = features_t(dot(f_ref[h], qr)).astype(BF16)


def pair_masks(has_prev):
    lane = lax.broadcasted_iota(jnp.int32, (64, REPEAT * 128), 1)
    row = lax.broadcasted_iota(jnp.int32, (64, REPEAT * 128), 0)
    low = (lane % 128) < 64
    ahead = row - lane % 64
    value = jnp.where(low, ahead - 1, -ahead)
    hidden = jnp.where(low, (1 - has_prev) * 1024, 0)
    return low, value >= 0, value - hidden >= 0


def heads_side(ref, size, start):
    return jnp.concatenate(
        [ref[h * size : (h + 1) * size, start : start + 128] for h in range(REPEAT)], axis=1
    )


def attend_kernel(micro, prev_ref, n_ref, halo_ref, base_ref, qr_ref, pq_ref,
                  o_ref, ot_ref, den_ref, s_ref):
    rows = n_ref.shape[2]
    low, mask_a, mask_first = pair_masks(prev_ref[0])
    low_row = (lax.broadcasted_iota(jnp.int32, (1, REPEAT * 128), 1) % 128) < 64
    key_lane = lax.broadcasted_iota(jnp.int32, (AUG, 128), 1) < 64
    for m in range(micro):
        ext = jnp.concatenate([halo_ref[0, m], n_ref[0, m]], axis=0)
        ext_t = ext.astype(F32).T.astype(BF16)
        v_aug_all = jnp.concatenate([ext_t[192:256], jnp.ones((AUG - 64, rows + WIN), BF16)], axis=0)
        running = base_ref[0, m]
        for p in range(rows // 128):
            start = m * rows + p * 128
            r0 = p * 128
            qr4 = heads_side(qr_ref, 64, start)
            pq4 = heads_side(pq_ref, 128, start)
            pk = ext[r0 : r0 + 128, :128]
            kr = ext[r0 : r0 + 192, 128:192]
            v_aug = v_aug_all[:, r0 : r0 + 128]
            zero = jnp.zeros_like(v_aug)
            spans = dot(
                jnp.concatenate(
                    [jnp.where(key_lane, v_aug, zero), jnp.where(key_lane, zero, v_aug)], axis=0
                ),
                pk,
            )
            if p == 0:
                running = running - spans[:AUG]
            state = jnp.concatenate([running, running + spans[:AUG]], axis=0).astype(BF16)
            running = running + spans[:AUG] + spans[AUG:]
            s_ref[0, m, p] = state
            from_state = dot(state, pq4)
            scores = dot(kr, qr4) * (1.0 / math.sqrt(HEAD_SIZE))
            linear = dot(pk, pq4)
            exp_a = jnp.exp(jnp.where(low, scores[:64], scores[128:]))
            exp_b = jnp.exp(scores[64:128])
            mask = mask_first if p == 0 else mask_a
            w_a = jnp.where(mask, exp_a, jnp.where(low, linear[:64], 0.0))
            w_b = jnp.where(mask_a, jnp.where(low, 0.0, linear[64:]), exp_b)
            den = (
                jnp.sum(w_a, axis=0, keepdims=True)
                + jnp.sum(w_b, axis=0, keepdims=True)
                + jnp.where(low_row, from_state[64:65], from_state[AUG + 64 : AUG + 65])
            )
            inv = 1.0 / den
            p_a = w_a * inv
            weights = jnp.concatenate(
                [jnp.where(low, p_a, 0.0), w_b * inv, jnp.where(low, 0.0, p_a)], axis=0
            ).astype(BF16)
            out = (
                dot(ext_t[192:256, r0 : r0 + 192], weights)
                + jnp.where(low, from_state[:64], from_state[AUG : AUG + 64]) * inv
            )
            for h in range(REPEAT):
                den_ref[0, h : h + 1, start : start + 128] = den[:, h * 128 : (h + 1) * 128]
            out_t = jnp.concatenate(
                [out[:, h * 128 : (h + 1) * 128] for h in range(REPEAT)], axis=0
            )
            ot_ref[:, start : start + 128] = out_t.astype(BF16)
            o_ref[start : start + 128, :] = out_t.T.astype(BF16)


def attend_back_kernel(micro, prev_ref, n_ref, halo_ref, s_ref, qr_ref, pq_ref, go_ref, ot_ref,
                       den_ref, f_ref, cos_ref, sin_ref,
                       gq_ref, df_ref, gn_ref, gs_ref, gqr_ref, gmq_ref):
    rows = n_ref.shape[2]
    low, mask_a, mask_first = pair_masks(prev_ref[0])
    low_aug = (lax.broadcasted_iota(jnp.int32, (AUG, REPEAT * 128), 1) % 128) < 64
    low_feat = (lax.broadcasted_iota(jnp.int32, (128, REPEAT * 128), 1) % 128) < 64
    scale = 1.0 / math.sqrt(HEAD_SIZE)
    for m in range(micro):
        ext = jnp.concatenate([halo_ref[0, m], n_ref[0, m]], axis=0)
        ext_t = ext.astype(F32).T.astype(BF16)
        tail = None
        for p in range(rows // 128):
            start = m * rows + p * 128
            r0 = p * 128
            qr4 = heads_side(qr_ref, 64, start)
            pq4 = heads_side(pq_ref, 128, start)
            go4 = heads_side(go_ref, 64, start)
            o4 = heads_side(ot_ref, 64, start)
            den = jnp.concatenate(
                [den_ref[0, h : h + 1, start : start + 128] for h in range(REPEAT)], axis=1
            )
            inv = 1.0 / den
            pk = ext[r0 : r0 + 128, :128]
            kr = ext[r0 : r0 + 192, 128:192]
            v = ext[r0 : r0 + 192, 192:256]
            go_f = go4.astype(F32)
            delta = jnp.sum(go_f * o4.astype(F32), axis=0, keepdims=True)
            scores = dot(kr, qr4) * scale
            linear = dot(pk, pq4)
            g_p = dot(v, go4)
            mask = mask_first if p == 0 else mask_a
            exp_a = jnp.exp(jnp.where(low, scores[:64], scores[128:]))
            exp_b = jnp.exp(scores[64:128])
            p_a = jnp.where(mask, exp_a, jnp.where(low, linear[:64], 0.0)) * inv
            p_b = jnp.where(mask_a, jnp.where(low, 0.0, linear[64:]), exp_b) * inv
            weights = jnp.concatenate(
                [jnp.where(low, p_a, 0.0), p_b, jnp.where(low, 0.0, p_a)], axis=0
            ).astype(BF16)
            gw_a = (jnp.where(low, g_p[:64], g_p[128:]) - delta) * inv
            gw_b = (g_p[64:128] - delta) * inv
            gs_a = jnp.where(mask, gw_a * exp_a, 0.0)
            gs_b = jnp.where(mask_a, 0.0, gw_b * exp_b)
            g_scores = jnp.concatenate(
                [jnp.where(low, gs_a, 0.0), gs_b, jnp.where(low, 0.0, gs_a)], axis=0
            ).astype(BF16)
            g_linear = jnp.concatenate(
                [
                    jnp.where(mask_a, 0.0, jnp.where(low, gw_a, 0.0)),
                    jnp.where(mask_a, jnp.where(low, 0.0, gw_b), 0.0),
                ],
                axis=0,
            ).astype(BF16)
            go_aug = jnp.concatenate(
                [go_f * inv, -delta * inv, jnp.zeros((AUG - 65, REPEAT * 128), F32)], axis=0
            )
            go_aug_b = go_aug.astype(BF16)
            gqr = dot(ext_t[128:192, r0 : r0 + 192], g_scores) * scale
            state_t = s_ref[0, m, p].astype(F32).T.astype(BF16)
            gpq = dot(ext_t[:128, r0 : r0 + 128], g_linear) + jnp.where(
                low_feat, dot(state_t[:, :AUG], go_aug_b), dot(state_t[:, AUG:], go_aug_b)
            )
            zero = jnp.zeros_like(go_aug_b)
            gs_ref[0, m, p] = dot_nt(
                jnp.concatenate(
                    [jnp.where(low_aug, go_aug_b, zero), jnp.where(low_aug, zero, go_aug_b)], axis=0
                ),
                pq4,
            )
            g_pk = dot_nt(g_linear, pq4)
            g_kr = dot_nt(g_scores, qr4) * scale
            g_v = dot_nt(weights, go4)
            g_keys = jnp.concatenate(
                [
                    jnp.concatenate([g_pk, jnp.zeros((64, 128), F32)], axis=0),
                    g_kr,
                    g_v,
                ],
                axis=1,
            )
            if tail is None:
                gn_ref[0, m, 0:64] = g_keys[:64]
            else:
                gn_ref[0, m, r0 : r0 + 64] = g_keys[:64] + tail
            gn_ref[0, m, r0 + 64 : r0 + 128] = g_keys[64:128]
            tail = g_keys[128:]
            if p == rows // 128 - 1:
                gn_ref[0, m, rows : rows + 64] = tail
            pq_f = pq4.astype(F32)
            gmq = features_back_t(pq_f, gpq).astype(BF16)
            for h in range(REPEAT):
                gqr_ref[h * 64 : (h + 1) * 64, start : start + 128] = gqr[:, h * 128 : (h + 1) * 128]
                gmq_ref[h * 64 : (h + 1) * 64, start : start + 128] = gmq[:, h * 128 : (h + 1) * 128]
    cos_t, sin_t = cos_ref[...], sin_ref[...]
    grads = []
    for h in range(REPEAT):
        sl = slice(h * 64, (h + 1) * 64)
        gmq = gmq_ref[sl]
        df_ref[0, sl] = dot_nt(qr_ref[sl], gmq)
        grads.append(rotate_back_t(gqr_ref[sl] + dot(f_ref[h], gmq), cos_t, sin_t))
    gq_ref[0] = jnp.concatenate(grads, axis=0).T.astype(BF16)


def kv_back_kernel(kv_heads, micro, gn_ref, ghalo_ref, n_ref, gs_ref, next_ref, f_ref, cos_ref,
                   sin_ref, gkv_ref, df_ref):
    rows = n_ref.shape[2]
    spans = rows // WIN
    cos_t, sin_t = cos_ref[...], sin_ref[...]
    keys, values = [], []
    unit = (lax.broadcasted_iota(jnp.int32, (64, AUG - 64), 1) == 0).astype(BF16)
    for g in range(kv_heads):
        parts = []
        for m in range(micro):
            natural = n_ref[g, m]
            later = [None] * spans
            later[spans - 1] = next_ref[g, m, 1]
            later[spans - 2] = next_ref[g, m, 0]
            for c in range(spans - 3, -1, -1):
                later[c] = later[c + 1] + gs_ref[g, m, (c + 2) // 2, ((c + 2) % 2) * AUG : ((c + 2) % 2 + 1) * AUG]
            for c in range(spans):
                part = natural[c * 64 : (c + 1) * 64]
                grad = gn_ref[g, m, 64 + c * 64 : 128 + c * 64]
                if c == spans - 1:
                    grad = grad + ghalo_ref[g, m].astype(F32)
                big = later[c].astype(BF16)
                g_pk = dot(jnp.concatenate([part[:, 192:256], unit], axis=1), big)
                g_v = dot_nt(part[:, :128], big[:64])
                parts.append(
                    grad + jnp.concatenate([g_pk, jnp.zeros((64, 64), F32), g_v], axis=1)
                )
        grad_t = jnp.concatenate(parts, axis=0).T
        nat_t = jnp.concatenate([n_ref[g, m, :, :192] for m in range(micro)], axis=0).astype(F32).T
        gmk = features_back_t(nat_t[:128], grad_t[:128]).astype(BF16)
        df_ref[0, g * 64 : (g + 1) * 64] = dot_nt(nat_t[128:].astype(BF16), gmk)
        keys.append(rotate_back_t(grad_t[128:192] + dot(f_ref[g], gmk), cos_t, sin_t))
        values.append(grad_t[192:256])
    gkv_ref[0] = jnp.concatenate(keys + values, axis=0).T.astype(BF16)


def out_kernel(shards, depth, o_ref, w_ref, ao_ref, bo_ref, x_ref, gain_ref,
               x2_ref, h2_ref, uo_ref, r2_ref, x2_all, sq_ref):
    j = pl.program_id(0)
    last = pl.num_programs(0) - 1

    @pl.when(j == 0)
    def _():
        uo_ref[...] = dot(o_ref[...], ao_ref[...]).astype(BF16)
        sq_ref[...] = jnp.zeros_like(sq_ref)

    total = dot_nt(uo_ref[...], bo_ref[...])
    halves = w_ref.shape[3] // depth
    for f in range(shards):
        for a in range(halves):
            e0 = (f * halves + a) * depth
            total += dot(o_ref[:, e0 : e0 + depth], w_ref[0, f, :, a * depth : (a + 1) * depth])
    x2 = x_ref[...].astype(F32) + total
    x2_ref[...] = x2
    x2_all[j] = x2
    sq_ref[...] += jnp.sum(x2 * x2, axis=1, keepdims=True)

    @pl.when(j == last)
    def _():
        width = depth * x2_all.shape[0]
        r2 = lax.rsqrt(sq_ref[...] * (1.0 / width) + EPSILON)
        r2_ref[...] = r2
        for i in range(x2_all.shape[0]):
            cols = slice(i * depth, (i + 1) * depth)
            h2_ref[:, cols] = (x2_all[i] * r2 * gain_ref[:, cols]).astype(BF16)


def go_kernel(depth, gb_ref, w_ref, ao_ref, guo_ref, go_ref):
    groups = w_ref.shape[0]
    halves = w_ref.shape[3] // depth
    low_rank = dot_nt(ao_ref[...], guo_ref[...])
    for a in range(halves):
        total = low_rank[a * depth : (a + 1) * depth]
        for j in range(groups):
            total += dot_nt(
                w_ref[j, 0, :, a * depth : (a + 1) * depth], gb_ref[:, j * depth : (j + 1) * depth]
            )
        go_ref[a * depth : (a + 1) * depth] = total.astype(BF16)


def gx_kernel(shards, depth, gq_ref, gkv_ref, wq_ref, wkv_ref, gu_ref, a_ref, x_ref, x_all_ref,
              gx2_ref, r1_ref, gain_ref, gx_ref, dg_ref, gh_all, dot_ref):
    j = pl.program_id(0)
    last = pl.num_programs(0) - 1

    @pl.when(j == 0)
    def _():
        dot_ref[...] = jnp.zeros_like(dot_ref)

    total = dot_nt(gu_ref[...], a_ref[...])
    for f in range(shards):
        total += dot_nt(gq_ref[f], wq_ref[0, f])
        total += dot_nt(gkv_ref[f], wkv_ref[0, f])
    gh_all[j] = total
    hx = total * x_ref[...].astype(F32)
    dg_ref[...] = jnp.sum(hx * r1_ref[...], axis=0, keepdims=True)
    dot_ref[...] += jnp.sum(hx * gain_ref[0], axis=1, keepdims=True)

    @pl.when(j == last)
    def _():
        count = gh_all.shape[0]
        r1 = r1_ref[...]
        back = r1 * r1 * r1 * dot_ref[...] * (1.0 / (count * depth))
        for i in range(count):
            cols = slice(i * depth, (i + 1) * depth)
            gx_ref[:, cols] = (
                gx2_ref[:, cols]
                + r1 * gain_ref[i] * gh_all[i]
                - x_all_ref[:, cols].astype(F32) * back
            ).astype(BF16)


def ffn_kernel(depth, h2_ref, gy_ref, wg_ref, wu_ref, wd_ref, out_ref, gh_ref, out_acc, gh_acc):
    j = pl.program_id(1)
    last = pl.num_programs(1) - 1
    groups = wd_ref.shape[0]
    gate = dot(h2_ref[...], wg_ref[...])
    up = dot(h2_ref[...], wu_ref[...])
    g_hid = dot_nt(gy_ref[:, :depth], wd_ref[0])
    for i in range(1, groups):
        g_hid += dot_nt(gy_ref[:, i * depth : (i + 1) * depth], wd_ref[i])
    sig = 1.0 / (1.0 + jnp.exp(-gate))
    silu = gate * sig
    hid = (silu * up).astype(BF16)
    g_gate = (g_hid * up * sig * (1.0 + gate * (1.0 - sig))).astype(BF16)
    g_up = (g_hid * silu).astype(BF16)
    g_h2 = dot_nt(g_gate, wg_ref[...]) + dot_nt(g_up, wu_ref[...])

    @pl.when(j == 0)
    def _():
        gh_acc[...] = g_h2
        for i in range(groups):
            out_acc[:, i * depth : (i + 1) * depth] = dot(hid, wd_ref[i])

    @pl.when(j > 0)
    def _():
        gh_acc[...] += g_h2
        for i in range(groups):
            out_acc[:, i * depth : (i + 1) * depth] += dot(hid, wd_ref[i])

    @pl.when(j == last)
    def _():
        gh_ref[...] = gh_acc[...].astype(BF16)
        out_ref[...] = out_acc[...].astype(BF16)


def ffn(h2, gy, wg, wu, wd):
    total, width = h2.shape
    hidden = wg.shape[1]
    groups, _, depth = wd.shape
    row_tile = min(512, total)
    hid_tile = min(512, hidden)
    grid = (total // row_tile, hidden // hid_tile)
    return pl.pallas_call(
        functools.partial(ffn_kernel, depth),
        grid=grid,
        in_specs=[
            pl.BlockSpec((row_tile, width), lambda r, j: (r, 0)),
            pl.BlockSpec((row_tile, width), lambda r, j: (r, 0)),
            pl.BlockSpec((width, hid_tile), lambda r, j: (0, j)),
            pl.BlockSpec((width, hid_tile), lambda r, j: (0, j)),
            pl.BlockSpec((groups, hid_tile, depth), lambda r, j: (0, j, 0)),
        ],
        out_specs=[
            pl.BlockSpec((row_tile, width), lambda r, j: (r, 0)),
            pl.BlockSpec((row_tile, width), lambda r, j: (r, 0)),
        ],
        out_shape=[jax.ShapeDtypeStruct((total, width), BF16)] * 2,
        scratch_shapes=[pltpu.VMEM((row_tile, width), F32)] * 2,
        compiler_params=params(58, ("arbitrary", "arbitrary")),
        cost_estimate=cost(12 * total * width * hidden, 2 * (4 * total * width + 3 * grid[0] * width * hidden)),
        name="feed_forward",
    )(h2, gy, wg, wu, wd)


def shift_sum(array, axis_name, size, direction):
    total = None
    for step in range(1, size):
        if direction > 0:
            perm = [(i, i + step) for i in range(size - step)]
        else:
            perm = [(i + step, i) for i in range(size - step)]
        moved = lax.ppermute(array, axis_name, perm).astype(F32)
        total = moved if total is None else total + moved
    return total


def deal(rows, order):
    micro, count, width = rows.shape
    groups = order.shape[1]
    pieces = rows.reshape(micro, groups, count // groups, width).transpose(1, 0, 2, 3)
    spread = lax.all_to_all(pieces, "dp", split_axis=0, concat_axis=0, tiled=True)
    ordered = jnp.stack(
        [
            jnp.stack([lax.dynamic_index_in_dim(spread, order[m, j], 0, keepdims=False)[m] for m in range(micro)])
            for j in range(groups)
        ]
    )
    settled = lax.all_to_all(ordered, "dp", split_axis=0, concat_axis=0, tiled=True)
    return settled.transpose(1, 0, 2, 3).reshape(micro, count, width)


def shards(
    inputs, cotangent, lengths, dealing, wq, wk, wv, wo, wg, wu, wd,
    down_ad, up_qo, up_kv, fmap_q, fmap_k, gains,
):
    n_dp = lax.axis_size("dp")
    n_f = lax.axis_size("fsdp")
    group = lax.axis_index("dp")
    quarter = lax.axis_index("fsdp")
    micro, rows, width = inputs.shape[1:]
    total = micro * rows
    depth = wq.shape[0]
    q_cols, k_cols = wq.shape[1], wk.shape[1]
    kv_heads = k_cols // HEAD_SIZE
    heads = q_cols // HEAD_SIZE
    halves = wo.shape[0] // depth
    n_all = n_dp * n_f
    x = inputs[0].reshape(total, width)

    small_parts = [down_ad, up_qo, up_kv, fmap_q, fmap_k, gains]
    flat = jnp.concatenate([part.reshape(-1) for part in small_parts])
    pack_cols = 2 * q_cols + 2 * k_cols
    small_rows = -(-flat.shape[0] // pack_cols)
    small_rows = -(-small_rows // 16) * 16
    flat = jnp.pad(flat, (0, small_rows * pack_cols - flat.shape[0])).reshape(small_rows, pack_cols)
    wo_side = jnp.concatenate([wo[a * depth : (a + 1) * depth] for a in range(halves)], axis=1)
    packed = jnp.concatenate([jnp.concatenate([wq, wo_side, wk, wv], axis=1), flat], axis=0)
    gathered = lax.all_gather(packed, ("dp", "fsdp"), axis=0, tiled=False)
    gathered = gathered.reshape(n_dp, n_f, depth + small_rows, pack_cols)
    small = gathered[:, :, depth:].reshape(n_all, small_rows * pack_cols)
    at = 0
    fetched = []
    for part in small_parts:
        fetched.append(
            small[:, at : at + part.size].reshape((n_all * part.shape[0],) + part.shape[1:])
        )
        at += part.size
    down_ad, up_qo, up_kv, fmap_q, fmap_k, gains = fetched
    gain_one = gains[:, 0].astype(F32)
    gain_two = gains[:, 1].astype(F32)

    wg_all = lax.all_gather(wg, "dp", axis=0, tiled=True)
    wu_all = lax.all_gather(wu, "dp", axis=0, tiled=True)
    wd_all = lax.all_gather(wd, "dp", axis=0, tiled=False)

    cot = deal(cotangent[0], dealing)
    positions = quarter * rows + jnp.arange(rows, dtype=jnp.int32)
    seq_len = lax.dynamic_index_in_dim(lengths, group, 0, keepdims=False)
    valid = positions[None, :] < seq_len[:, None]
    gy = jnp.where(valid[:, :, None], cot, jnp.zeros_like(cot)).reshape(total, width)
    gy_all = lax.all_gather(gy, "fsdp", axis=0, tiled=True)

    xf = x.astype(F32)
    r1 = lax.rsqrt(jnp.mean(xf * xf, axis=-1, keepdims=True) + EPSILON)
    h1 = (xf * r1 * gain_one).astype(BF16)
    rank = ADAPTER_RANK
    lanes = RANK_LANES
    a_qkv = jnp.pad(down_ad[:, : 3 * rank], ((0, 0), (0, lanes - 3 * rank)))
    a_o = jnp.pad(down_ad[:, 3 * rank :], ((0, 0), (0, lanes - rank)))
    u = dot(h1, a_qkv).astype(BF16)
    b_q = up_qo[:, :rank].reshape(n_f, q_cols, rank)
    b_k = up_kv[:, :rank].reshape(n_f, k_cols, rank)
    b_v = up_kv[:, rank:].reshape(n_f, k_cols, rank)
    b_o = jnp.pad(up_qo[:, rank:], ((0, 0), (0, lanes - rank)))

    def placed(block, at):
        return jnp.pad(block.transpose(0, 2, 1), ((0, 0), (at, lanes - at - rank), (0, 0)))

    b_q_t = placed(b_q, 0)
    b_kv_t = jnp.concatenate([placed(b_k, rank), placed(b_v, 2 * rank)], axis=2)
    fq = fmap_q.reshape(H, HEAD_SIZE, HEAD_SIZE)
    fk = fmap_k.reshape(KEY_VALUE_HEADS, HEAD_SIZE, HEAD_SIZE)
    fq_t = jnp.concatenate([fq.transpose(0, 2, 1), -fq.transpose(0, 2, 1)], axis=1)
    fk_t = jnp.concatenate([fk.transpose(0, 2, 1), -fk.transpose(0, 2, 1)], axis=1)
    cos_t, sin_t = rope_tables_t(jnp.tile(positions, micro))
    spans = rows // WIN
    pairs = rows // 128
    w_rows = depth + small_rows

    kv_natural, totals = pl.pallas_call(
        functools.partial(kv_kernel, kv_heads, micro, depth),
        grid=(n_f,),
        in_specs=[
            whole((total, width)),
            whole((total, lanes)),
            pl.BlockSpec((n_dp, 1, depth, 2 * k_cols), lambda f: (0, f, 0, q_cols // k_cols)),
            pl.BlockSpec((1, lanes, 2 * k_cols), lambda f: (f, 0, 0)),
            whole((32, total)),
            whole((32, total)),
            pl.BlockSpec((kv_heads, 128, 64), lambda f: (f, 0, 0)),
        ],
        out_specs=[
            pl.BlockSpec((kv_heads, micro, rows, 256), lambda f: (f, 0, 0, 0)),
            pl.BlockSpec((kv_heads, micro, AUG, 128), lambda f: (f, 0, 0, 0)),
        ],
        out_shape=[
            jax.ShapeDtypeStruct((KEY_VALUE_HEADS, micro, rows, 256), BF16),
            jax.ShapeDtypeStruct((KEY_VALUE_HEADS, micro, AUG, 128), BF16),
        ],
        compiler_params=params(40),
        cost_estimate=cost(4 * total * width * k_cols * n_f, 2 * (total * width + 2 * width * k_cols * n_f), 128 * 8 * total),
        name="key_value",
    )(h1, u, gathered, b_kv_t, cos_t, sin_t, fk_t)

    forward_one = [(i, i + 1) for i in range(n_f - 1)]
    backward_one = [(i + 1, i) for i in range(n_f - 1)]
    halo = lax.ppermute(kv_natural[:, :, rows - WIN :], "fsdp", forward_one)
    base = shift_sum(totals, "fsdp", n_f, 1)

    q_rot, q_feat = pl.pallas_call(
        functools.partial(q_kernel, heads, depth),
        grid=(n_f,),
        in_specs=[
            whole((total, width)),
            whole((total, lanes)),
            pl.BlockSpec((n_dp, 1, depth, q_cols), lambda f: (0, f, 0, 0)),
            pl.BlockSpec((1, lanes, q_cols), lambda f: (f, 0, 0)),
            whole((32, total)),
            whole((32, total)),
            pl.BlockSpec((heads, 128, 64), lambda f: (f, 0, 0)),
        ],
        out_specs=[
            pl.BlockSpec((q_cols, total), lambda f: (f, 0)),
            pl.BlockSpec((2 * q_cols, total), lambda f: (f, 0)),
        ],
        out_shape=[
            jax.ShapeDtypeStruct((H * 64, total), BF16),
            jax.ShapeDtypeStruct((H * 128, total), BF16),
        ],
        compiler_params=params(40),
        cost_estimate=cost(2 * total * width * q_cols * n_f, 2 * (total * width + width * q_cols * n_f + 3 * total * 2048), 128 * 32 * total),
        name="query",
    )(h1, u, gathered, b_q_t, cos_t, sin_t, fq_t)

    has_prev = (quarter > 0).astype(jnp.int32).reshape(1)
    g4 = REPEAT * 64
    prev_spec = pl.BlockSpec(memory_space=pltpu.SMEM)
    n_spec = pl.BlockSpec((1, micro, rows, 256), lambda g: (g, 0, 0, 0))
    halo_spec = pl.BlockSpec((1, micro, WIN, 256), lambda g: (g, 0, 0, 0))
    state_spec = pl.BlockSpec((1, micro, pairs, 2 * AUG, 128), lambda g: (g, 0, 0, 0, 0))
    head_spec = pl.BlockSpec((g4, total), lambda g: (g, 0))
    feat_spec = pl.BlockSpec((2 * g4, total), lambda g: (g, 0))
    den_spec = pl.BlockSpec((1, 8, total), lambda g: (g, 0, 0))
    attend_flops = H * total * 2 * (192 * 64 + 128 * 128 + 160 * 128 + 192 * 64)
    o, o_t, den, states = pl.pallas_call(
        functools.partial(attend_kernel, micro),
        grid=(KEY_VALUE_HEADS,),
        in_specs=[
            prev_spec,
            n_spec,
            halo_spec,
            pl.BlockSpec((1, micro, AUG, 128), lambda g: (g, 0, 0, 0)),
            head_spec,
            feat_spec,
        ],
        out_specs=[pl.BlockSpec((total, g4), lambda g: (0, g)), head_spec, den_spec, state_spec],
        out_shape=[
            jax.ShapeDtypeStruct((total, H * 64), BF16),
            jax.ShapeDtypeStruct((H * 64, total), BF16),
            jax.ShapeDtypeStruct((KEY_VALUE_HEADS, 8, total), F32),
            jax.ShapeDtypeStruct((KEY_VALUE_HEADS, micro, pairs, 2 * AUG, 128), BF16),
        ],
        compiler_params=params(40),
        cost_estimate=cost(attend_flops, 14 * MIB, 128 * H * total),
        name="attend",
    )(has_prev, kv_natural, halo, base, q_rot, q_feat)

    x2, h2, uo, r2 = pl.pallas_call(
        functools.partial(out_kernel, n_f, depth),
        grid=(n_dp,),
        in_specs=[
            whole((total, H * 64)),
            pl.BlockSpec((1, n_f, depth, q_cols), lambda j: (j, 0, 0, 1)),
            whole((H * 64, lanes)),
            pl.BlockSpec((depth, lanes), lambda j: (j, 0)),
            pl.BlockSpec((total, depth), lambda j: (0, j)),
            whole((1, width)),
        ],
        out_specs=[
            pl.BlockSpec((total, depth), lambda j: (0, j)),
            whole((total, width)),
            whole((total, lanes)),
            whole((total, 1)),
        ],
        out_shape=[
            jax.ShapeDtypeStruct((total, width), F32),
            jax.ShapeDtypeStruct((total, width), BF16),
            jax.ShapeDtypeStruct((total, lanes), BF16),
            jax.ShapeDtypeStruct((total, 1), F32),
        ],
        scratch_shapes=[pltpu.VMEM((n_dp, total, depth), F32), pltpu.VMEM((total, 1), F32)],
        compiler_params=params(40),
        cost_estimate=cost(2 * total * width * H * 64, 20 * MIB),
        name="output_projection",
    )(o, gathered, a_o, b_o, x, gain_two.reshape(1, width))

    h2_all = lax.all_gather(h2, "fsdp", axis=0, tiled=True)
    down_part, gh2_part = ffn(h2_all, gy_all, wg_all, wu_all, wd_all)

    def scatter(part):
        moved = lax.all_to_all(
            part.reshape(n_f, total, width), "fsdp", split_axis=0, concat_axis=0, tiled=True
        )
        return jnp.sum(moved.astype(F32), axis=0)

    gh2 = scatter(gh2_part)
    result = x2 + scatter(down_part)
    result = jnp.where(valid.reshape(total, 1), result, 0.0).astype(BF16)
    inverse = jnp.argsort(dealing, axis=1).astype(jnp.int32)
    output = deal(result.reshape(micro, rows, width), inverse)

    dg2 = jnp.sum(gh2 * x2 * r2, axis=0)
    gx2 = (
        gy.astype(F32)
        + r2 * gain_two * gh2
        - x2 * r2**3 * jnp.mean(gain_two * gh2 * x2, axis=-1, keepdims=True)
    )
    gb = gx2.astype(BF16)
    guo = dot(gb, b_o).astype(BF16)
    d_bo = lax.dot_general(gb, uo[:, :rank], (((0,), (0,)), ((), ())), preferred_element_type=F32)

    go_t = pl.pallas_call(
        functools.partial(go_kernel, depth),
        grid=(n_f,),
        in_specs=[
            whole((total, width)),
            pl.BlockSpec((n_dp, 1, depth, q_cols), lambda f: (0, f, 0, 1)),
            pl.BlockSpec((q_cols, lanes), lambda f: (f, 0)),
            whole((total, lanes)),
        ],
        out_specs=pl.BlockSpec((q_cols, total), lambda f: (f, 0)),
        out_shape=jax.ShapeDtypeStruct((H * 64, total), BF16),
        compiler_params=params(40),
        cost_estimate=cost(2 * total * width * H * 64, 12 * MIB),
        name="output_projection_back",
    )(gb, gathered, a_o, guo)
    d_ao = dot(o_t, guo[:, :rank])

    gq, d_fq, g_keys, g_states = pl.pallas_call(
        functools.partial(attend_back_kernel, micro),
        grid=(KEY_VALUE_HEADS,),
        in_specs=[
            prev_spec,
            n_spec,
            halo_spec,
            state_spec,
            head_spec,
            feat_spec,
            head_spec,
            head_spec,
            den_spec,
            pl.BlockSpec((REPEAT, 64, 64), lambda g: (g, 0, 0)),
            whole((32, total)),
            whole((32, total)),
        ],
        out_specs=[
            pl.BlockSpec((1, total, g4), lambda g: (g * g4 // q_cols, 0, g % (q_cols // g4))),
            pl.BlockSpec((1, g4, 64), lambda g: (g, 0, 0)),
            pl.BlockSpec((1, micro, rows + WIN, 256), lambda g: (g, 0, 0, 0)),
            state_spec,
        ],
        out_shape=[
            jax.ShapeDtypeStruct((n_f, total, q_cols), BF16),
            jax.ShapeDtypeStruct((KEY_VALUE_HEADS, g4, 64), F32),
            jax.ShapeDtypeStruct((KEY_VALUE_HEADS, micro, rows + WIN, 256), F32),
            jax.ShapeDtypeStruct((KEY_VALUE_HEADS, micro, pairs, 2 * AUG, 128), F32),
        ],
        scratch_shapes=[pltpu.VMEM((g4, total), F32), pltpu.VMEM((g4, total), BF16)],
        compiler_params=params(50),
        cost_estimate=cost(3 * attend_flops, 24 * MIB, 128 * H * total),
        name="attend_back",
    )(has_prev, kv_natural, halo, states, q_rot, q_feat, go_t, o_t, den, fq, cos_t, sin_t)

    g_halo = lax.ppermute(g_keys[:, :, :WIN].astype(BF16), "fsdp", backward_one)
    g_total = jnp.sum(g_states[:, :, :, :AUG] + g_states[:, :, :, AUG:], axis=2)
    g_first = g_states[:, :, 0, :AUG]
    g_next = shift_sum(g_total.astype(BF16), "fsdp", n_f, -1)
    g_first_next = lax.ppermute(g_first.astype(BF16), "fsdp", backward_one).astype(F32)
    g_later = jnp.stack([g_next, g_next - g_first_next], axis=2)

    gkv, d_fk = pl.pallas_call(
        functools.partial(kv_back_kernel, kv_heads, micro),
        grid=(n_f,),
        in_specs=[
            pl.BlockSpec((kv_heads, micro, rows + WIN, 256), lambda f: (f, 0, 0, 0)),
            pl.BlockSpec((kv_heads, micro, WIN, 256), lambda f: (f, 0, 0, 0)),
            pl.BlockSpec((kv_heads, micro, rows, 256), lambda f: (f, 0, 0, 0)),
            pl.BlockSpec((kv_heads, micro, pairs, 2 * AUG, 128), lambda f: (f, 0, 0, 0, 0)),
            pl.BlockSpec((kv_heads, micro, 2, AUG, 128), lambda f: (f, 0, 0, 0, 0)),
            pl.BlockSpec((kv_heads, 64, 64), lambda f: (f, 0, 0)),
            whole((32, total)),
            whole((32, total)),
        ],
        out_specs=[
            pl.BlockSpec((1, total, 2 * k_cols), lambda f: (f, 0, 0)),
            pl.BlockSpec((1, k_cols, 64), lambda f: (f, 0, 0)),
        ],
        out_shape=[
            jax.ShapeDtypeStruct((n_f, total, 2 * k_cols), BF16),
            jax.ShapeDtypeStruct((n_f, k_cols, 64), F32),
        ],
        compiler_params=params(40),
        cost_estimate=cost(8 * total * 128 * 128, 8 * MIB),
        name="key_value_back",
    )(g_keys, g_halo, kv_natural, g_states, g_later, fk, cos_t, sin_t)

    gk, gv = gkv[:, :, :k_cols], gkv[:, :, k_cols:]

    def ranks(grad, up):
        return jnp.einsum("fte,fer->tr", grad, up, preferred_element_type=F32)

    def outer(grad, at):
        out = jnp.einsum("fte,tr->fer", grad, u[:, at : at + rank], preferred_element_type=F32)
        return out.reshape(-1, rank)

    gu = jnp.concatenate([ranks(gq, b_q), ranks(gk, b_k), ranks(gv, b_v)], axis=1).astype(BF16)
    d_bq, d_bk, d_bv = outer(gq, 0), outer(gk, rank), outer(gv, 2 * rank)
    d_qkv = lax.dot_general(h1, gu, (((0,), (0,)), ((), ())), preferred_element_type=F32)
    gu = jnp.pad(gu, ((0, 0), (0, lanes - 3 * rank)))

    gx, dg1 = pl.pallas_call(
        functools.partial(gx_kernel, n_f, depth),
        grid=(n_dp,),
        in_specs=[
            whole((n_f, total, q_cols)),
            whole((n_f, total, 2 * k_cols)),
            pl.BlockSpec((1, n_f, depth, q_cols), lambda j: (j, 0, 0, 0)),
            pl.BlockSpec((1, n_f, depth, 2 * k_cols), lambda j: (j, 0, 0, q_cols // k_cols)),
            whole((total, lanes)),
            pl.BlockSpec((depth, lanes), lambda j: (j, 0)),
            pl.BlockSpec((total, depth), lambda j: (0, j)),
            whole((total, width)),
            whole((total, width)),
            whole((total, 1)),
            whole((n_dp, 1, depth)),
        ],
        out_specs=[whole((total, width)), pl.BlockSpec((1, depth), lambda j: (0, j))],
        out_shape=[
            jax.ShapeDtypeStruct((total, width), BF16),
            jax.ShapeDtypeStruct((1, width), F32),
        ],
        scratch_shapes=[pltpu.VMEM((n_dp, total, depth), F32), pltpu.VMEM((total, 1), F32)],
        compiler_params=params(56),
        cost_estimate=cost(2 * total * width * 3072, 30 * MIB),
        name="input_gradient",
    )(gq, gkv, gathered, gathered, gu, a_qkv, x, x, gx2, r1, gain_one.reshape(n_dp, 1, depth))

    grads = [
        jnp.concatenate([d_qkv, d_ao], axis=1),
        jnp.concatenate([d_bq, d_bo], axis=1),
        jnp.concatenate([d_bk, d_bv], axis=1),
        d_fq.reshape(H * 64, 64),
        d_fk.reshape(KEY_VALUE_HEADS * 64, 64),
        jnp.stack([dg1[0], dg2], axis=1),
    ]
    flat = jnp.concatenate([grad.reshape(n_all, -1) for grad in grads], axis=1)
    columns = flat.shape[1]
    padded = -(-columns // 1024) * 1024
    flat = jnp.pad(flat, ((0, 0), (0, padded - columns))).reshape(n_all, padded // 128, 128)
    moved = lax.all_to_all(flat, ("dp", "fsdp"), split_axis=0, concat_axis=0, tiled=True)
    mine = jnp.sum(moved, axis=0).reshape(-1)
    shares = []
    at = 0
    for grad in grads:
        size = grad.size // n_all
        shares.append(mine[at : at + size].reshape(grad.shape[0] // n_all, grad.shape[1]))
        at += size
    return (output[None], gx.reshape(1, micro, rows, width), *shares)


def solution(mesh):
    every = ("dp", "fsdp")
    blocks = P("dp", None, "fsdp", None)
    in_specs = (
        blocks,
        blocks,
        P(),
        P(),
        P("dp", "fsdp"),
        P("dp", "fsdp"),
        P("dp", "fsdp"),
        P("fsdp", "dp"),
        P("dp", "fsdp"),
        P("dp", "fsdp"),
        P("fsdp", "dp"),
    ) + (P(every, None),) * 6
    out_specs = (blocks, blocks) + (P(every, None),) * 6
    return jax.shard_map(shards, mesh=mesh, in_specs=in_specs, out_specs=out_specs, check_vma=False)
```

```python
import functools
import math

import jax
import jax.numpy as jnp
from jax import lax
from jax.experimental import pallas as pl
from jax.experimental.pallas import tpu as pltpu
from jax.sharding import PartitionSpec as P

H = 32
KEY_VALUE_HEADS = 8
REPEAT = H // KEY_VALUE_HEADS
HEAD_SIZE = 64
ADAPTER_RANK = 8
WIN = 64
AUG = 80
RANK_LANES = 128

EPSILON = 1e-05
ROPE_BASE = 500000.0
F32 = jnp.float32
BF16 = jnp.bfloat16
MIB = 1024 * 1024
X_PAIRS = [(i, i ^ 1) for i in range(4)]
Y_PAIRS = [(i, i ^ 2) for i in range(4)]


def dot(a, b):
    return lax.dot_general(a, b, (((1,), (0,)), ((), ())), preferred_element_type=F32)


def dot_nt(a, b):
    return lax.dot_general(a, b, (((1,), (1,)), ((), ())), preferred_element_type=F32)


def params(mib, semantics=("arbitrary",)):
    return pltpu.CompilerParams(vmem_limit_bytes=mib * MIB, dimension_semantics=semantics)


def cost(flops, bytes_accessed, transcendentals=0):
    return pl.CostEstimate(
        flops=int(flops), bytes_accessed=int(bytes_accessed), transcendentals=int(transcendentals)
    )


def whole(shape):
    return pl.BlockSpec(shape, lambda *_: (0,) * len(shape))


def after(value, *others):
    return lax.optimization_barrier((value, *others))[0]


def together(*jobs):
    arguments = lax.optimization_barrier([job[1:] for job in jobs])
    return lax.optimization_barrier([job[0](*args) for job, args in zip(jobs, arguments)])


def by_x(rows):
    return lax.ppermute(rows, "fsdp", X_PAIRS)


def by_y(rows):
    return lax.ppermute(rows, "fsdp", Y_PAIRS)


def rope_tables_t(positions):
    half_size = HEAD_SIZE // 2
    frequencies = jnp.exp(
        -(2.0 * jnp.arange(half_size, dtype=F32) / HEAD_SIZE) * math.log(ROPE_BASE)
    )
    angles = frequencies[:, None] * positions.astype(F32)[None, :]
    return jnp.cos(angles), jnp.sin(angles)


def rotate_t(head, cos_t, sin_t):
    a, b = head[:32], head[32:]
    return jnp.concatenate([a * cos_t - b * sin_t, b * cos_t + a * sin_t], axis=0)


def rotate_back_t(head, cos_t, sin_t):
    a, b = head[:32], head[32:]
    return jnp.concatenate([a * cos_t + b * sin_t, b * cos_t - a * sin_t], axis=0)


def half_softmax_t(scores):
    e = jnp.exp(scores - jnp.max(scores, axis=0, keepdims=True))
    return e * (1.0 / jnp.sum(e, axis=0, keepdims=True))


def features_t(mapped):
    return jnp.concatenate([half_softmax_t(mapped[:64]), half_softmax_t(mapped[64:])], axis=0)


def features_back_t(e, f):
    ef = e * f
    t1 = jnp.sum(ef[:64], axis=0, keepdims=True)
    t2 = jnp.sum(ef[64:], axis=0, keepdims=True)
    return (ef[:64] - e[:64] * t1) - (ef[64:] - e[64:] * t2)


def block_pieces(refs, place_ref, n_dp):
    if len(refs) == 9:
        own, x_mine, y_mine, dx_mine, dy_mine, x_other, y_other, dx_other, dy_other = refs
        shard, core = place_ref[0], place_ref[1]
        half = n_dp // 2
        mine, other = core * half, (1 - core) * half
        quarter = half // 2
        return [
            (shard, [(own, 0)]),
            (shard ^ 1, [(x_mine, mine), (x_other, other)]),
            (shard ^ 2, [(y_mine, mine), (y_other, other)]),
            (
                shard ^ 3,
                [
                    (dx_mine, mine),
                    (dy_mine, mine + quarter),
                    (dx_other, other),
                    (dy_other, other + quarter),
                ],
            ),
        ]
    return [(f, [(ref, 0)]) for f, ref in enumerate(refs)]


def project(h1_ref, u_ref, pieces, low_rank, depth):
    total = dot(u_ref[...], low_rank)
    for ref, start in pieces:
        count = ref.shape[0] * depth
        if isinstance(start, int):
            columns = h1_ref[:, start * depth : start * depth + count]
        else:
            columns = h1_ref[:, pl.ds(pl.multiple_of(start * depth, depth), count)]
        total += dot(columns, ref[...].reshape(count, ref.shape[2]))
    return total


def kv_kernel(kv_heads, micro, depth, n_dp, place_ref, h1_ref, u_ref, b_ref, cos_ref, sin_ref,
              f_ref, *refs):
    *w_refs, n_ref, tot_ref, msg_ref = refs
    rows = h1_ref.shape[0] // micro
    cos_t, sin_t = cos_ref[...], sin_ref[...]
    width = kv_heads * HEAD_SIZE
    for f, pieces in block_pieces(w_refs, place_ref, n_dp):
        kv_t = project(h1_ref, u_ref, pieces, b_ref[f], depth).T
        for g in range(kv_heads):
            head = f * kv_heads + g
            kr = rotate_t(kv_t[g * 64 : (g + 1) * 64], cos_t, sin_t).astype(BF16)
            v = kv_t[width + g * 64 : width + (g + 1) * 64].astype(BF16)
            pk = features_t(dot(f_ref[head], kr)).astype(BF16)
            natural = (
                jnp.concatenate([pk.astype(F32), kr.astype(F32), v.astype(F32)], axis=0).T
            ).astype(BF16)
            v_aug = jnp.concatenate([v, jnp.ones((AUG - 64, v.shape[1]), BF16)], axis=0)
            for m in range(micro):
                part = natural[m * rows : (m + 1) * rows]
                n_ref[head, m] = part
                sums = dot(v_aug[:, m * rows : (m + 1) * rows], part[:, :128])
                tot_ref[head, m] = sums.astype(BF16)
                msg_ref[head, m, :64] = part[rows - 64 :]
                tail = jnp.concatenate([sums[48:], jnp.zeros((16, 128), F32)], axis=0)
                msg_ref[head, m, 64:] = jnp.concatenate([sums[:48], tail], axis=1).astype(BF16)


def q_kernel(heads, depth, n_dp, place_ref, h1_ref, u_ref, b_ref, cos_ref, sin_ref, f_ref, *refs):
    *w_refs, qr_ref, pq_ref = refs
    cos_t, sin_t = cos_ref[...], sin_ref[...]
    for f, pieces in block_pieces(w_refs, place_ref, n_dp):
        q_t = project(h1_ref, u_ref, pieces, b_ref[f], depth).T
        for h in range(heads):
            head = f * heads + h
            qr = rotate_t(q_t[h * 64 : (h + 1) * 64], cos_t, sin_t).astype(BF16)
            pq = features_t(dot(f_ref[head], qr)).astype(BF16)
            if isinstance(head, int):
                qr_ref[head * 64 : (head + 1) * 64] = qr
                pq_ref[head * 128 : (head + 1) * 128] = pq
            else:
                qr_ref[pl.ds(pl.multiple_of(head * 64, 64), 64)] = qr
                pq_ref[pl.ds(pl.multiple_of(head * 128, 128), 128)] = pq


def pair_masks(has_prev):
    lane = lax.broadcasted_iota(jnp.int32, (64, REPEAT * 128), 1)
    row = lax.broadcasted_iota(jnp.int32, (64, REPEAT * 128), 0)
    low = (lane % 128) < 64
    ahead = row - lane % 64
    value = jnp.where(low, ahead - 1, -ahead)
    hidden = jnp.where(low, (1 - has_prev) * 1024, 0)
    return low, value >= 0, value - hidden >= 0


def heads_side(ref, size, start):
    return jnp.concatenate(
        [ref[h * size : (h + 1) * size, start : start + 128] for h in range(REPEAT)], axis=1
    )


def attend_kernel(micro, prev_ref, n_ref, msg_ref, qr_ref, pq_ref, *refs):
    *base_refs, o_ref, ot_ref, den_ref, s_ref = refs
    rows = n_ref.shape[2]
    low, mask_a, mask_first = pair_masks(prev_ref[0])
    low_row = (lax.broadcasted_iota(jnp.int32, (1, REPEAT * 128), 1) % 128) < 64
    key_lane = lax.broadcasted_iota(jnp.int32, (AUG, 128), 1) < 64
    for m in range(micro):
        ext = jnp.concatenate([msg_ref[0, m, :64], n_ref[0, m]], axis=0)
        ext_t = ext.astype(F32).T.astype(BF16)
        near = jnp.concatenate([msg_ref[0, m, 64:112, :128], msg_ref[0, m, 64:96, 128:]], axis=0)
        v_aug_all = jnp.concatenate([ext_t[192:256], jnp.ones((AUG - 64, rows + WIN), BF16)], axis=0)
        running = near.astype(F32)
        for base_ref in base_refs:
            running += base_ref[0, m].astype(F32)
        for p in range(rows // 128):
            start = m * rows + p * 128
            r0 = p * 128
            qr4 = heads_side(qr_ref, 64, start)
            pq4 = heads_side(pq_ref, 128, start)
            pk = ext[r0 : r0 + 128, :128]
            kr = ext[r0 : r0 + 192, 128:192]
            v_aug = v_aug_all[:, r0 : r0 + 128]
            zero = jnp.zeros_like(v_aug)
            spans = dot(
                jnp.concatenate(
                    [jnp.where(key_lane, v_aug, zero), jnp.where(key_lane, zero, v_aug)], axis=0
                ),
                pk,
            )
            if p == 0:
                running = running - spans[:AUG]
            state = jnp.concatenate([running, running + spans[:AUG]], axis=0).astype(BF16)
            running = running + spans[:AUG] + spans[AUG:]
            s_ref[0, m, p] = state
            from_state = dot(state, pq4)
            scores = dot(kr, qr4) * (1.0 / math.sqrt(HEAD_SIZE))
            linear = dot(pk, pq4)
            exp_a = jnp.exp(jnp.where(low, scores[:64], scores[128:]))
            exp_b = jnp.exp(scores[64:128])
            mask = mask_first if p == 0 else mask_a
            w_a = jnp.where(mask, exp_a, jnp.where(low, linear[:64], 0.0))
            w_b = jnp.where(mask_a, jnp.where(low, 0.0, linear[64:]), exp_b)
            den = (
                jnp.sum(w_a, axis=0, keepdims=True)
                + jnp.sum(w_b, axis=0, keepdims=True)
                + jnp.where(low_row, from_state[64:65], from_state[AUG + 64 : AUG + 65])
            )
            inv = 1.0 / den
            p_a = w_a * inv
            weights = jnp.concatenate(
                [jnp.where(low, p_a, 0.0), w_b * inv, jnp.where(low, 0.0, p_a)], axis=0
            ).astype(BF16)
            out = (
                dot(ext_t[192:256, r0 : r0 + 192], weights)
                + jnp.where(low, from_state[:64], from_state[AUG : AUG + 64]) * inv
            )
            for h in range(REPEAT):
                den_ref[0, h : h + 1, start : start + 128] = den[:, h * 128 : (h + 1) * 128]
            out_t = jnp.concatenate(
                [out[:, h * 128 : (h + 1) * 128] for h in range(REPEAT)], axis=0
            )
            ot_ref[:, start : start + 128] = out_t.astype(BF16)
            o_ref[start : start + 128, :] = out_t.T.astype(BF16)


def attend_back_kernel(micro, prev_ref, n_ref, msg_ref, s_ref, qr_ref, pq_ref, go_ref, ot_ref,
                       den_ref, f_ref, cos_ref, sin_ref,
                       gq_ref, df_ref, gn_ref, gs_ref, back_ref, total_ref,
                       gqr_ref, gmq_ref):
    rows = n_ref.shape[2]
    low, mask_a, mask_first = pair_masks(prev_ref[0])
    low_aug = (lax.broadcasted_iota(jnp.int32, (AUG, REPEAT * 128), 1) % 128) < 64
    low_feat = (lax.broadcasted_iota(jnp.int32, (128, REPEAT * 128), 1) % 128) < 64
    scale = 1.0 / math.sqrt(HEAD_SIZE)
    for m in range(micro):
        ext = jnp.concatenate([msg_ref[0, m, :64], n_ref[0, m]], axis=0)
        ext_t = ext.astype(F32).T.astype(BF16)
        tail = g_sum = None
        for p in range(rows // 128):
            start = m * rows + p * 128
            r0 = p * 128
            qr4 = heads_side(qr_ref, 64, start)
            pq4 = heads_side(pq_ref, 128, start)
            go4 = heads_side(go_ref, 64, start)
            o4 = heads_side(ot_ref, 64, start)
            den = jnp.concatenate(
                [den_ref[0, h : h + 1, start : start + 128] for h in range(REPEAT)], axis=1
            )
            inv = 1.0 / den
            pk = ext[r0 : r0 + 128, :128]
            kr = ext[r0 : r0 + 192, 128:192]
            v = ext[r0 : r0 + 192, 192:256]
            go_f = go4.astype(F32)
            delta = jnp.sum(go_f * o4.astype(F32), axis=0, keepdims=True)
            scores = dot(kr, qr4) * scale
            linear = dot(pk, pq4)
            g_p = dot(v, go4)
            mask = mask_first if p == 0 else mask_a
            exp_a = jnp.exp(jnp.where(low, scores[:64], scores[128:]))
            exp_b = jnp.exp(scores[64:128])
            p_a = jnp.where(mask, exp_a, jnp.where(low, linear[:64], 0.0)) * inv
            p_b = jnp.where(mask_a, jnp.where(low, 0.0, linear[64:]), exp_b) * inv
            weights = jnp.concatenate(
                [jnp.where(low, p_a, 0.0), p_b, jnp.where(low, 0.0, p_a)], axis=0
            ).astype(BF16)
            gw_a = (jnp.where(low, g_p[:64], g_p[128:]) - delta) * inv
            gw_b = (g_p[64:128] - delta) * inv
            gs_a = jnp.where(mask, gw_a * exp_a, 0.0)
            gs_b = jnp.where(mask_a, 0.0, gw_b * exp_b)
            g_scores = jnp.concatenate(
                [jnp.where(low, gs_a, 0.0), gs_b, jnp.where(low, 0.0, gs_a)], axis=0
            ).astype(BF16)
            g_linear = jnp.concatenate(
                [
                    jnp.where(mask_a, 0.0, jnp.where(low, gw_a, 0.0)),
                    jnp.where(mask_a, jnp.where(low, 0.0, gw_b), 0.0),
                ],
                axis=0,
            ).astype(BF16)
            go_aug = jnp.concatenate(
                [go_f * inv, -delta * inv, jnp.zeros((AUG - 65, REPEAT * 128), F32)], axis=0
            )
            go_aug_b = go_aug.astype(BF16)
            gqr = dot(ext_t[128:192, r0 : r0 + 192], g_scores) * scale
            state_t = s_ref[0, m, p].astype(F32).T.astype(BF16)
            gpq = dot(ext_t[:128, r0 : r0 + 128], g_linear) + jnp.where(
                low_feat, dot(state_t[:, :AUG], go_aug_b), dot(state_t[:, AUG:], go_aug_b)
            )
            zero = jnp.zeros_like(go_aug_b)
            g_spans = dot_nt(
                jnp.concatenate(
                    [jnp.where(low_aug, go_aug_b, zero), jnp.where(low_aug, zero, go_aug_b)], axis=0
                ),
                pq4,
            )
            gs_ref[0, m, p] = g_spans
            both = g_spans[:AUG] + g_spans[AUG:]
            g_sum = both if p == 0 else g_sum + both
            if p == 0:
                back_ref[0, m, 64:, :128] = g_spans[:AUG].astype(BF16)
            g_pk = dot_nt(g_linear, pq4)
            g_kr = dot_nt(g_scores, qr4) * scale
            g_v = dot_nt(weights, go4)
            g_keys = jnp.concatenate(
                [
                    jnp.concatenate([g_pk, jnp.zeros((64, 128), F32)], axis=0),
                    g_kr,
                    g_v,
                ],
                axis=1,
            )
            if p == 0:
                back_ref[0, m, :64] = g_keys[:64].astype(BF16)
            else:
                gn_ref[0, m, r0 - 64 : r0] = g_keys[:64] + tail
            gn_ref[0, m, r0 : r0 + 64] = g_keys[64:128]
            tail = g_keys[128:]
            if p == rows // 128 - 1:
                gn_ref[0, m, rows - 64 : rows] = tail
                total_ref[0, m] = g_sum.astype(BF16)
                back_ref[0, m, 64:, 128:] = g_sum.astype(BF16)
            pq_f = pq4.astype(F32)
            gmq = features_back_t(pq_f, gpq).astype(BF16)
            for h in range(REPEAT):
                gqr_ref[h * 64 : (h + 1) * 64, start : start + 128] = gqr[:, h * 128 : (h + 1) * 128]
                gmq_ref[h * 64 : (h + 1) * 64, start : start + 128] = gmq[:, h * 128 : (h + 1) * 128]
    cos_t, sin_t = cos_ref[...], sin_ref[...]
    grads = []
    for h in range(REPEAT):
        sl = slice(h * 64, (h + 1) * 64)
        gmq = gmq_ref[sl]
        df_ref[0, sl] = dot_nt(qr_ref[sl], gmq)
        grads.append(rotate_back_t(gqr_ref[sl] + dot(f_ref[h], gmq), cos_t, sin_t))
    gq_ref[0] = jnp.concatenate(grads, axis=0).T.astype(BF16)


def kv_back_kernel(kv_heads, micro, gn_ref, back_ref, n_ref, gs_ref, f_ref, cos_ref, sin_ref,
                   u_ref, b_ref, guq_ref, h1_ref, *refs):
    *next_refs, gkv_ref, df_ref, gu_ref, db_ref, dqkv_ref, acc_ref = refs
    rows = n_ref.shape[2]
    spans = rows // WIN
    cos_t, sin_t = cos_ref[...], sin_ref[...]
    keys, values = [], []
    unit = (lax.broadcasted_iota(jnp.int32, (64, AUG - 64), 1) == 0).astype(BF16)
    for g in range(kv_heads):
        parts = []
        for m in range(micro):
            natural = n_ref[g, m]
            later = [None] * spans
            after_here = back_ref[g, m, 64:, 128:].astype(F32)
            for ref in next_refs:
                after_here += ref[g, m].astype(F32)
            later[spans - 1] = after_here - back_ref[g, m, 64:, :128].astype(F32)
            later[spans - 2] = after_here
            for c in range(spans - 3, -1, -1):
                later[c] = later[c + 1] + gs_ref[g, m, (c + 2) // 2, ((c + 2) % 2) * AUG : ((c + 2) % 2 + 1) * AUG]
            for c in range(spans):
                part = natural[c * 64 : (c + 1) * 64]
                grad = gn_ref[g, m, c * 64 : (c + 1) * 64]
                if c == spans - 1:
                    grad = grad + back_ref[g, m, :64].astype(F32)
                big = later[c].astype(BF16)
                g_pk = dot(jnp.concatenate([part[:, 192:256], unit], axis=1), big)
                g_v = dot_nt(part[:, :128], big[:64])
                parts.append(
                    grad + jnp.concatenate([g_pk, jnp.zeros((64, 64), F32), g_v], axis=1)
                )
        grad_t = jnp.concatenate(parts, axis=0).T
        nat_t = jnp.concatenate([n_ref[g, m, :, :192] for m in range(micro)], axis=0).astype(F32).T
        gmk = features_back_t(nat_t[:128], grad_t[:128]).astype(BF16)
        df_ref[0, g * 64 : (g + 1) * 64] = dot_nt(nat_t[128:].astype(BF16), gmk)
        keys.append(rotate_back_t(grad_t[128:192] + dot(f_ref[g], gmk), cos_t, sin_t))
        values.append(grad_t[192:256])
    gkv = jnp.concatenate(keys + values, axis=0).T.astype(BF16)
    gkv_ref[0] = gkv
    db_ref[...] = dot(u_ref[...].astype(F32).T[:32].astype(BF16), gkv)
    rank_grad = dot_nt(gkv, b_ref[0])

    @pl.when(pl.program_id(0) == 0)
    def _():
        acc_ref[...] = guq_ref[...] + rank_grad

    @pl.when(pl.program_id(0) > 0)
    def _():
        acc_ref[...] += rank_grad

    @pl.when(pl.program_id(0) == pl.num_programs(0) - 1)
    def _():
        gu_ref[...] = acc_ref[...].astype(BF16)
        dqkv_ref[...] = dot(acc_ref[...].T[:32].astype(BF16), h1_ref[...])


def table_kernel(heads_ref, dqkv_ref, dao_ref, dbq_ref, dbo_ref, dg1_ref, dg2_ref, out_ref):
    width = dqkv_ref.shape[1]
    gains = jnp.concatenate([dg1_ref[...], dg2_ref[...], jnp.zeros((6, width), F32)], axis=0)
    rows = jnp.concatenate(
        [dqkv_ref[:24], dao_ref[:8], dbq_ref[:8], dbo_ref[:8], gains, jnp.zeros((8, width), F32)],
        axis=0,
    )
    out_ref[...] = jnp.concatenate([heads_ref[...], rows.T], axis=1)


def out_kernel(depth, n_dp, place_ref, o_ref, ao_ref, bo_ref, x_ref, gain_ref, *refs):
    *w_refs, x2_ref, h2_ref, uo_ref, r2_ref, acc_ref = refs
    uo = dot(o_ref[...], ao_ref[...]).astype(BF16)
    uo_ref[...] = uo
    for j in range(n_dp):
        cols = slice(j * depth, (j + 1) * depth)
        acc_ref[j] = x_ref[:, cols].astype(F32) + dot_nt(uo, bo_ref[cols])
    halves = w_refs[0].shape[2] // depth
    block = halves * depth
    for f, pieces in block_pieces(w_refs, place_ref, n_dp):
        for ref, start in pieces:
            for i in range(ref.shape[0]):
                total = None
                for a in range(halves):
                    e0 = f * block + a * depth
                    if not isinstance(f, int):
                        e0 = pl.multiple_of(e0, depth)
                    term = dot(o_ref[:, pl.ds(e0, depth)], ref[i, :, a * depth : (a + 1) * depth])
                    total = term if total is None else total + term
                acc_ref[start + i] += total
    squares = 0.0
    for j in range(n_dp):
        x2 = acc_ref[j]
        x2_ref[:, j * depth : (j + 1) * depth] = x2
        squares += jnp.sum(x2 * x2, axis=1, keepdims=True)
    r2 = lax.rsqrt(squares * (1.0 / (n_dp * depth)) + EPSILON)
    r2_ref[...] = r2
    for j in range(n_dp):
        cols = slice(j * depth, (j + 1) * depth)
        h2_ref[:, cols] = (acc_ref[j] * r2 * gain_ref[:, cols]).astype(BF16)


def go_kernel(depth, gb_ref, w_ref, ao_ref, guo_ref, o_ref, go_ref, dao_ref):
    groups = w_ref.shape[1]
    halves = w_ref.shape[3] // depth
    guo = guo_ref[...]
    low_rank = dot_nt(ao_ref[...], guo)
    for a in range(halves):
        total = low_rank[a * depth : (a + 1) * depth]
        for j in range(groups):
            total += dot_nt(
                w_ref[0, j, :, a * depth : (a + 1) * depth], gb_ref[:, j * depth : (j + 1) * depth]
            )
        go_ref[a * depth : (a + 1) * depth] = total.astype(BF16)
    dao_ref[...] = dot(guo.astype(F32).T[:16].astype(BF16), o_ref[...])


def gx_query_kernel(shards, gq_ref, wq_ref, u_ref, b_ref, out_ref, gu_ref, db_ref):
    total = dot_nt(gq_ref[0], wq_ref[0, 0])
    for f in range(1, shards):
        total += dot_nt(gq_ref[f], wq_ref[f, 0])
    out_ref[...] = total

    @pl.when(pl.program_id(0) == 0)
    def _():
        u_t = u_ref[...].astype(F32).T[:32].astype(BF16)
        cols = gq_ref.shape[2]
        rank_grad = 0.0
        for f in range(shards):
            rank_grad += dot_nt(gq_ref[f], b_ref[f])
            db_ref[:, f * cols : (f + 1) * cols] = dot(u_t, gq_ref[f])
        gu_ref[...] = rank_grad


def gx_kernel(shards, depth, part_ref, gkv_ref, wkv_ref, gu_ref, a_ref, x_ref, x_all_ref,
              gx2_ref, r1_ref, gain_ref, gx_ref, dg_ref, gh_all, dot_ref):
    j = pl.program_id(0)
    last = pl.num_programs(0) - 1

    @pl.when(j == 0)
    def _():
        dot_ref[...] = jnp.zeros_like(dot_ref)

    total = part_ref[...] + dot_nt(gu_ref[...], a_ref[...])
    for f in range(shards):
        total += dot_nt(gkv_ref[f], wkv_ref[f, 0])
    gh_all[j] = total
    hx = total * x_ref[...].astype(F32)
    dg_ref[...] = jnp.sum(hx * r1_ref[...], axis=0, keepdims=True)
    dot_ref[...] += jnp.sum(hx * gain_ref[0], axis=1, keepdims=True)

    @pl.when(j == last)
    def _():
        count = gh_all.shape[0]
        r1 = r1_ref[...]
        back = r1 * r1 * r1 * dot_ref[...] * (1.0 / (count * depth))
        for i in range(count):
            cols = slice(i * depth, (i + 1) * depth)
            gx_ref[:, cols] = (
                gx2_ref[:, cols]
                + r1 * gain_ref[i] * gh_all[i]
                - x_all_ref[:, cols].astype(F32) * back
            ).astype(BF16)


def pack_attention_kernel(wq_ref, wk_ref, wv_ref, wo_ref, qkv_ref, out_ref):
    depth, q_cols = wq_ref.shape
    qkv_ref[:, :q_cols] = wq_ref[...]
    qkv_ref[:, q_cols:] = jnp.concatenate([wk_ref[...], wv_ref[...]], axis=1)
    for a in range(wo_ref.shape[0] // depth):
        out_ref[:, a * depth : (a + 1) * depth] = wo_ref[a * depth : (a + 1) * depth]


def pack_ffn_kernel(cuts, wg_ref, wu_ref, wd_ref, *refs):
    for ref, start, stop in zip(refs, cuts, cuts[1:]):
        count = stop - start
        ref[:, :count] = wg_ref[:, start:stop]
        ref[:, count : 2 * count] = wu_ref[:, start:stop]
        step = min(256, count)
        for at in range(0, count, step):
            ref[:, 2 * count + at : 2 * count + at + step] = (
                wd_ref[start + at : start + at + step].astype(F32).T.astype(BF16)
            )


def joined(refs):
    own_a, own_b, x_a, y_a, y_b, x_b = refs
    left = own_a[0].astype(F32) + x_a[0].astype(F32) + y_a[...].astype(F32)
    right = own_b[0].astype(F32) + y_b[0].astype(F32) + x_b[...].astype(F32)
    return jnp.concatenate([left, right], axis=1)


def result_kernel(count, x2_ref, valid_ref, *refs):
    *parts, out_ref = refs
    total = joined(parts) if count == 6 else parts[0][...]
    out_ref[...] = jnp.where(valid_ref[...] > 0, x2_ref[...] + total, 0.0).astype(BF16)


def mid_back_kernel(count, x2_ref, r2_ref, gain_ref, gy_ref, uo_ref, bo_ref, *refs):
    gx2_ref, gb_ref, guo_ref, dg_ref, dbo_ref = refs[-5:]
    parts = refs[:count]
    gh = joined(parts) if count == 6 else parts[0][...]
    x2, r2 = x2_ref[...], r2_ref[...]
    gx = gh * x2
    scaled = gh * gain_ref[...]
    mean = jnp.mean(scaled * x2, axis=1, keepdims=True)
    gx2 = gy_ref[...].astype(F32) + r2 * scaled - x2 * (r2 * r2 * r2 * mean)
    gx2_ref[...] = gx2
    gb = gx2.astype(BF16)
    gb_ref[...] = gb
    guo_ref[...] = dot(gb, bo_ref[...]).astype(BF16)
    dg = jnp.sum(gx * r2, axis=0, keepdims=True)
    dbo = dot(uo_ref[...].astype(F32).T[:16].astype(BF16), gb)

    @pl.when(pl.program_id(0) == 0)
    def _():
        dg_ref[...] = dg
        dbo_ref[...] = dbo

    @pl.when(pl.program_id(0) > 0)
    def _():
        dg_ref[...] += dg
        dbo_ref[...] += dbo


def load_rows(refs, rows_ref):
    if len(refs) == 1:
        rows_ref[...] = refs[0][...]
        return
    own, from_x, from_y, diagonal_x, diagonal_y = refs
    count, width = own.shape

    @pl.when(pl.program_id(0) == 0)
    def _():
        rows_ref[:count] = own[...]
        rows_ref[count:] = from_x[...]

    @pl.when(pl.program_id(0) == 1)
    def _():
        rows_ref[:count] = from_y[...]
        rows_ref[count:, : width // 2] = diagonal_x[...]
        rows_ref[count:, width // 2 :] = diagonal_y[...]


def store_rows(value_ref, refs):
    if len(refs) == 1:
        refs[0][...] = value_ref[...].astype(BF16)
        return
    send_x, keep_x, send_y, keep_y = refs
    count, half = value_ref.shape[0] // 2, value_ref.shape[1] // 2
    keep_x[0] = value_ref[:count, :half].astype(BF16)
    send_x[0] = value_ref[count:, :half].astype(BF16)
    for here, ref in enumerate((keep_y, send_y)):

        @pl.when(pl.program_id(0) == here)
        def _(ref=ref):
            ref[0] = value_ref[:count, half:].astype(BF16)
            ref[1] = value_ref[count:, half:].astype(BF16)


def ffn_kernel(pieces, carries, split, wg_ref, wu_ref, wd_ref, *refs):
    h2_refs, gy_refs = refs[:pieces], refs[pieces : 2 * pieces]
    carried = refs[2 * pieces : 2 * pieces + carries]
    *out_refs, h2_ref, gy_ref, out_acc, gh_acc = refs[2 * pieces + carries :]
    j = pl.program_id(1)

    @pl.when(j == 0)
    def _():
        load_rows(h2_refs, h2_ref)
        load_rows(gy_refs, gy_ref)

    shape = (wg_ref.shape[0] * wg_ref.shape[1], wg_ref.shape[2])
    wg, wu, wd = wg_ref[...].reshape(shape), wu_ref[...].reshape(shape), wd_ref[...].reshape(shape)
    gate = dot(h2_ref[...], wg)
    up = dot(h2_ref[...], wu)
    g_hid = dot(gy_ref[...], wd)
    sig = 1.0 / (1.0 + jnp.exp(-gate))
    silu = gate * sig
    hid = (silu * up).astype(BF16)
    g_gate = (g_hid * up * sig * (1.0 + gate * (1.0 - sig))).astype(BF16)
    g_up = (g_hid * silu).astype(BF16)

    @pl.when(j == 0)
    def _():
        out, gh = dot_nt(hid, wd), dot_nt(g_gate, wg) + dot_nt(g_up, wu)
        if carries:
            out += carried[0][...].astype(F32)
            gh += carried[1][...].astype(F32)
        out_acc[...] = out
        gh_acc[...] = gh

    @pl.when(j > 0)
    def _():
        out_acc[...] += dot_nt(hid, wd)
        gh_acc[...] += dot_nt(g_gate, wg) + dot_nt(g_up, wu)

    @pl.when(j == pl.num_programs(1) - 1)
    def _():
        half = len(out_refs) // 2
        store_rows(out_acc, out_refs[:half])
        store_rows(gh_acc, out_refs[half:])


def ffn(tile, split, h2, gy, weights, *carried):
    total = sum(part.size for part in h2) // h2[0].shape[1]
    width = h2[0].shape[1]
    groups, depth, cols = weights.shape
    tiles = cols // (3 * tile)
    pieces = len(h2)
    row_tile = total // 2
    row_spec = pl.BlockSpec((row_tile, width), lambda r, j: (r, 0))

    def weight_spec(kind):
        return pl.BlockSpec((groups, depth, tile), lambda r, j: (0, 0, kind * tiles + j))

    if pieces == 1:
        piece_specs = [row_spec]
    else:
        piece_specs = [
            pl.BlockSpec(part.shape, lambda r, j: (0, 0), pipeline_mode=pl.Buffered(1)) for part in h2
        ]
    if split and pieces > 1:
        count, half = row_tile // 2, width // 2
        moving = pl.BlockSpec((1, count, half), lambda r, j: (r, 0, 0))
        fixed = pl.BlockSpec((2, count, half), lambda r, j: (0, 0, 0))
        out_specs = [moving, moving, fixed, fixed] * 2
        out_shape = [jax.ShapeDtypeStruct((2, count, half), BF16)] * 8
    else:
        out_specs = [row_spec, row_spec]
        out_shape = [jax.ShapeDtypeStruct((total, width), BF16)] * 2
    outs = pl.pallas_call(
        functools.partial(ffn_kernel, pieces, len(carried), split),
        grid=(total // row_tile, tiles),
        in_specs=[weight_spec(0), weight_spec(1), weight_spec(2)]
        + piece_specs * 2
        + [pl.BlockSpec((row_tile, width), lambda r, j: (r, 0), pipeline_mode=pl.Buffered(1))]
        * len(carried),
        out_specs=out_specs,
        out_shape=out_shape,
        scratch_shapes=[pltpu.VMEM((row_tile, width), BF16)] * 2
        + [pltpu.VMEM((row_tile, width), F32)] * 2,
        compiler_params=params(60, ("arbitrary", "arbitrary")),
        cost_estimate=cost(4 * total * width * cols, 2 * width * cols * (total // row_tile) + 12 * total * width),
        name="feed_forward",
    )(weights, weights, weights, *h2, *gy, *carried)
    return (outs[: len(outs) // 2], outs[len(outs) // 2 :]) if split else outs


def gather_first(rows, size):
    if size != 4:
        return (lax.all_gather(rows, "fsdp", axis=0, tiled=True),)
    return rows, by_x(rows), by_y(rows)


def gather_second(*first):
    if len(first) == 1:
        return first
    rows, from_x, from_y = first
    half = rows.shape[1] // 2
    return rows, from_x, from_y, by_x(from_y[:, :half]), by_y(from_x[:, half:])


def scatter_first(*parts, size):
    if size != 4:
        (part,) = parts
        part = part.reshape(size, part.shape[0] // size, part.shape[1])
        return (lax.all_to_all(part, "fsdp", split_axis=0, concat_axis=0, tiled=True),)
    send_x, keep_x, send_y, keep_y = parts
    return keep_x, keep_y, by_x(send_x), by_y(send_y)


def pass_on_kernel(keep_x, from_x, keep_y, from_y, a_ref, b_ref):
    a_ref[...] = (keep_x[...].astype(F32) + from_x[...].astype(F32)).astype(BF16)
    b_ref[...] = (keep_y[...].astype(F32) + from_y[...].astype(F32)).astype(BF16)


def scatter_second(*first):
    if len(first) == 1:
        return [jnp.sum(first[0].astype(F32), axis=0)]
    keep_x, keep_y, from_x, from_y = first
    _, count, half = keep_x.shape
    second = pl.BlockSpec((None, count, half), lambda _: (1, 0, 0))
    a_pass, b_pass = pl.pallas_call(
        pass_on_kernel,
        grid=(1,),
        in_specs=[second] * 4,
        out_specs=[pl.BlockSpec((count, half), lambda _: (0, 0))] * 2,
        out_shape=[jax.ShapeDtypeStruct((count, half), BF16)] * 2,
        compiler_params=params(60),
        name="pass_on",
    )(keep_x, from_x, keep_y, from_y)
    return [keep_x, keep_y, from_x, by_y(a_pass), from_y, by_x(b_pass)]


def term_specs(terms, row_tile, width):
    full = pl.BlockSpec((row_tile, width), lambda r: (r, 0))
    if len(terms) == 1:
        return [full]
    half = width // 2
    row = pl.BlockSpec((row_tile, half), lambda r: (r, 0))
    first = pl.BlockSpec((1, row_tile, half), lambda r: (0, r, 0))
    return [first, first, first, row, first, row]


def pair_swap(part):
    return lax.ppermute(part, "dp", [(i, i ^ 1) for i in range(lax.axis_size("dp"))])


def columns_share(block, size, group):
    half = block.shape[0] // 2
    return block if size != 4 else lax.dynamic_slice_in_dim(block, group % 2 * half, half, 0)


def columns_first(mine, size):
    if size != 4:
        return (lax.all_gather(mine, "fsdp", axis=0, tiled=False),)
    return by_x(mine), by_y(mine)


def columns_second(*first):
    if len(first) == 1:
        return first
    from_x, from_y = first
    share = from_x.shape[0] // 2
    return (
        from_x, from_y, by_x(from_y[:share]), by_y(from_x[share:]),
        pair_swap(from_x), pair_swap(from_y),
    )


def columns_third(block, *second):
    if len(second) == 1:
        return [second[0][f] for f in range(second[0].shape[0])]
    from_x, from_y, diagonal_x, diagonal_y, other_x, other_y = second
    return [
        block, from_x, from_y, diagonal_x, diagonal_y,
        other_x, other_y, pair_swap(diagonal_x), pair_swap(diagonal_y),
    ]


def assembled(pieces, group, shard):
    if len(pieces) != 9:
        return jnp.stack(pieces)
    block = pieces[0]
    half = block.shape[0] // 2
    core = group % 2
    out = jnp.zeros((4,) + block.shape, block.dtype)

    def put(out, part, f, at):
        return lax.dynamic_update_slice(out, part[None], (f, at, 0, 0))

    out = put(out, block, shard, 0)
    masks = ((1, 0), (2, 0), (3, 0), (3, half // 2))
    for side, at in ((pieces[1:5], core * half), (pieces[5:], (1 - core) * half)):
        for part, (mask, offset) in zip(side, masks):
            out = put(out, part, shard ^ mask, at + offset)
    return out


def shifted(array, size, direction):
    moved = []
    for step in range(2, size):
        if direction > 0:
            perm = [(i, i + step) for i in range(size - step)]
        else:
            perm = [(i + step, i) for i in range(size - step)]
        moved.append(lax.ppermute(array, "fsdp", perm))
    return moved


def deal_out(rows):
    count, width = rows.shape
    groups = lax.axis_size("dp")
    pieces = rows.reshape(groups, count // groups, width)
    return lax.all_to_all(pieces, "dp", split_axis=0, concat_axis=0, tiled=True)


def reorder_kernel(at_ref, in_ref, out_ref):
    for j in range(out_ref.shape[0]):
        out_ref[j] = in_ref[at_ref[j]]


def reordered(spread, order):
    return pl.pallas_call(
        reorder_kernel,
        in_specs=[pl.BlockSpec(memory_space=pltpu.SMEM), pl.BlockSpec(memory_space=pltpu.VMEM)],
        out_specs=pl.BlockSpec(memory_space=pltpu.VMEM),
        out_shape=jax.ShapeDtypeStruct(spread.shape, spread.dtype),
        compiler_params=pltpu.CompilerParams(vmem_limit_bytes=60 * MIB),
        name="reorder",
    )(order, spread)


def deal_in(ordered):
    groups, share, width = ordered.shape
    settled = lax.all_to_all(ordered, "dp", split_axis=0, concat_axis=0, tiled=True)
    return settled.reshape(groups * share, width)


def shards(
    inputs, cotangent, lengths, dealing, wq, wk, wv, wo, wg, wu, wd,
    down_ad, up_qo, up_kv, fmap_q, fmap_k, gains,
):
    n_dp = lax.axis_size("dp")
    n_f = lax.axis_size("fsdp")
    group = lax.axis_index("dp")
    quarter = lax.axis_index("fsdp")
    micro, rows, width = inputs.shape[1:]
    total = micro * rows
    depth = wq.shape[0]
    q_cols, k_cols = wq.shape[1], wk.shape[1]
    kv_heads = k_cols // HEAD_SIZE
    heads = q_cols // HEAD_SIZE
    halves = wo.shape[0] // depth
    n_all = n_dp * n_f
    x = inputs[0].reshape(total, width)

    small_parts = [down_ad, up_qo, up_kv, fmap_q, fmap_k, gains]
    flat = jnp.concatenate([part.reshape(-1) for part in small_parts])
    small_rows = -(-flat.shape[0] // (16 * 128)) * 16
    flat = jnp.pad(flat, (0, small_rows * 128 - flat.shape[0])).reshape(1, small_rows, 128)
    small = lax.all_gather(flat.reshape(small_rows, 128), "dp", axis=0, tiled=False)
    small = lax.all_gather(small, "fsdp", axis=0, tiled=False)
    small = small.transpose(1, 0, 2, 3).reshape(n_all, small_rows * 128)
    at = 0
    fetched = []
    for part in small_parts:
        fetched.append(
            small[:, at : at + part.size].reshape((n_all * part.shape[0],) + part.shape[1:])
        )
        at += part.size
    down_ad, up_qo, up_kv, fmap_q, fmap_k, gains = fetched

    pack_cols = q_cols + 2 * k_cols
    w_qkv, w_out = pl.pallas_call(
        pack_attention_kernel,
        out_shape=[
            jax.ShapeDtypeStruct((depth, pack_cols), BF16),
            jax.ShapeDtypeStruct((depth, q_cols), BF16),
        ],
        compiler_params=pltpu.CompilerParams(vmem_limit_bytes=60 * MIB),
        name="pack_attention",
    )(wq, wk, wv, wo)
    w_qkv = lax.all_gather(w_qkv, "dp", axis=0, tiled=False)
    near, spread = together(
        (functools.partial(columns_first, size=n_f), columns_share(w_qkv, n_f, group)),
        (deal_out, after(cotangent[0].reshape(total, width), small)),
    )
    w_out = lax.all_gather(after(w_out, near[-1]), "dp", axis=0, tiled=False)
    share_micro = group * (total // n_dp) // rows
    order = lax.dynamic_index_in_dim(dealing, share_micro, 0, keepdims=False)

    gain_one = gains[:, 0].astype(F32)
    gain_two = gains[:, 1].astype(F32)

    hidden = wg.shape[1]
    tile = hidden // 4
    cuts = (0, 2 * tile, hidden)
    w_ffn = pl.pallas_call(
        functools.partial(pack_ffn_kernel, cuts),
        out_shape=[
            jax.ShapeDtypeStruct((depth, 3 * (stop - start)), BF16)
            for start, stop in zip(cuts, cuts[1:])
        ],
        compiler_params=pltpu.CompilerParams(vmem_limit_bytes=60 * MIB),
        name="pack_feed_forward",
    )(wg, wu, wd)
    positions = quarter * rows + jnp.arange(rows, dtype=jnp.int32)
    seq_len = lax.dynamic_index_in_dim(lengths, group, 0, keepdims=False)
    valid = (positions[None, :] < seq_len[:, None]).reshape(total, 1)

    xf = x.astype(F32)
    r1 = lax.rsqrt(jnp.mean(xf * xf, axis=-1, keepdims=True) + EPSILON)
    h1 = (xf * r1 * gain_one).astype(BF16)
    rank = ADAPTER_RANK
    lanes = RANK_LANES
    a_qkv = jnp.pad(down_ad[:, : 3 * rank], ((0, 0), (0, lanes - 3 * rank)))
    a_o = jnp.pad(down_ad[:, 3 * rank :], ((0, 0), (0, lanes - rank)))
    u = dot(h1, a_qkv).astype(BF16)
    b_q = up_qo[:, :rank].reshape(n_f, q_cols, rank)
    b_k = up_kv[:, :rank].reshape(n_f, k_cols, rank)
    b_v = up_kv[:, rank:].reshape(n_f, k_cols, rank)
    b_o = jnp.pad(up_qo[:, rank:], ((0, 0), (0, lanes - rank)))

    def placed(block, at):
        return jnp.pad(block.transpose(0, 2, 1), ((0, 0), (at, lanes - at - rank), (0, 0)))

    b_q_t = placed(b_q, 0)
    b_kv_t = jnp.concatenate([placed(b_k, rank), placed(b_v, 2 * rank)], axis=2)
    fq = fmap_q.reshape(H, HEAD_SIZE, HEAD_SIZE)
    fk = fmap_k.reshape(KEY_VALUE_HEADS, HEAD_SIZE, HEAD_SIZE)
    fq_t = jnp.concatenate([fq.transpose(0, 2, 1), -fq.transpose(0, 2, 1)], axis=1)
    fk_t = jnp.concatenate([fk.transpose(0, 2, 1), -fk.transpose(0, 2, 1)], axis=1)
    cos_t, sin_t = rope_tables_t(jnp.tile(positions, micro))
    pairs = rows // 128
    prepared = (h1, u, a_qkv, a_o, b_q_t, b_kv_t, b_o, fq, fk, fq_t, fk_t, cos_t, sin_t)
    inverse = jnp.argsort(dealing, axis=1).astype(jnp.int32)
    prepared += (inverse,)
    second, cot, prepared = together(
        (columns_second, *near),
        (lambda spread, order: deal_in(reordered(spread, order)), spread, order),
        (lambda *arrays: arrays, *prepared),
    )
    h1, u, a_qkv, a_o, b_q_t, b_kv_t, b_o, fq, fk, fq_t, fk_t, cos_t, sin_t, inverse = prepared
    fetched_ffn = [lax.all_gather(after(w_ffn[0], cot), "dp", axis=0, tiled=False)]
    (qkv_pieces,) = together((columns_third, w_qkv, *second))

    place = jnp.stack([quarter, group % 2]).astype(jnp.int32)
    smem = pl.BlockSpec(memory_space=pltpu.SMEM)
    vmem = pl.BlockSpec(memory_space=pltpu.VMEM)

    def columns(pieces, size, at):
        return [
            pl.BlockSpec(part.shape[:2] + (size,), lambda _: (0, 0, at), pipeline_mode=pl.Buffered(1))
            for part in pieces
        ]

    def key_values(h1, u, *pieces):
        return pl.pallas_call(
            functools.partial(kv_kernel, kv_heads, micro, depth, n_dp),
            grid=(1,),
            in_specs=[smem] + [vmem] * 6 + columns(pieces, 2 * k_cols, q_cols // (2 * k_cols)),
            out_specs=[vmem] * 3,
            out_shape=[
                jax.ShapeDtypeStruct((KEY_VALUE_HEADS, micro, rows, 256), BF16),
                jax.ShapeDtypeStruct((KEY_VALUE_HEADS, micro, AUG, 128), BF16),
                jax.ShapeDtypeStruct((KEY_VALUE_HEADS, micro, 112, 256), BF16),
            ],
            compiler_params=params(40),
            cost_estimate=cost(4 * total * width * k_cols * n_f, 2 * (total * width + 2 * width * k_cols * n_f), 128 * 8 * total),
            name="key_value",
        )(place, h1, u, b_kv_t, cos_t, sin_t, fk_t, *pieces)

    def queries(h1, u, *pieces):
        return pl.pallas_call(
            functools.partial(q_kernel, heads, depth, n_dp),
            grid=(1,),
            in_specs=[smem] + [vmem] * 6 + columns(pieces, q_cols, 0),
            out_specs=[vmem, vmem],
            out_shape=[
                jax.ShapeDtypeStruct((H * 64, total), BF16),
                jax.ShapeDtypeStruct((H * 128, total), BF16),
            ],
            compiler_params=params(40),
            cost_estimate=cost(2 * total * width * q_cols * n_f, 2 * (total * width + width * q_cols * n_f + 3 * total * 2048), 128 * 32 * total),
            name="query",
        )(place, h1, u, b_q_t, cos_t, sin_t, fq_t, *pieces)

    forward_one = [(i, i + 1) for i in range(n_f - 1)]
    backward_one = [(i + 1, i) for i in range(n_f - 1)]

    (kv_natural, totals, message), out_near = together(
        (key_values, h1, u, *qkv_pieces),
        (functools.partial(columns_first, size=n_f), columns_share(w_out, n_f, group)),
    )

    def send_on(message, totals):
        return lax.ppermute(message, "fsdp", forward_one), shifted(totals, n_f, 1)

    (q_rot, q_feat), (message, bases) = together(
        (queries, h1, u, *qkv_pieces), (send_on, message, totals)
    )
    part = after(w_ffn[1], q_rot)
    fetched_ffn.append(lax.all_gather(part, "dp", axis=0, tiled=False))
    w_ffn = fetched_ffn

    has_prev = (quarter > 0).astype(jnp.int32).reshape(1)
    g4 = REPEAT * 64
    prev_spec = smem
    n_spec = pl.BlockSpec((1, micro, rows, 256), lambda g: (g, 0, 0, 0))
    message_spec = pl.BlockSpec((1, micro, 112, 256), lambda g: (g, 0, 0, 0))
    back_spec = pl.BlockSpec((1, micro, 64 + AUG, 256), lambda g: (g, 0, 0, 0))
    state_spec = pl.BlockSpec((1, micro, pairs, 2 * AUG, 128), lambda g: (g, 0, 0, 0, 0))
    head_spec = pl.BlockSpec((g4, total), lambda g: (g, 0))
    feat_spec = pl.BlockSpec((2 * g4, total), lambda g: (g, 0))
    den_spec = pl.BlockSpec((1, 8, total), lambda g: (g, 0, 0))
    base_spec = pl.BlockSpec((1, micro, AUG, 128), lambda g: (g, 0, 0, 0))
    attend_flops = H * total * 2 * (192 * 64 + 128 * 128 + 160 * 128 + 192 * 64)
    gy_both = jnp.where(valid, cot, jnp.zeros_like(cot))
    gy = [gy_both[m * rows : (m + 1) * rows] for m in range(micro)]
    attend = pl.pallas_call(
        functools.partial(attend_kernel, micro),
        grid=(KEY_VALUE_HEADS,),
        in_specs=[
            prev_spec,
            n_spec,
            message_spec,
            head_spec,
            feat_spec,
        ]
        + [base_spec] * (n_f - 2),
        out_specs=[pl.BlockSpec((total, g4), lambda g: (0, g)), head_spec, den_spec, state_spec],
        out_shape=[
            jax.ShapeDtypeStruct((total, H * 64), BF16),
            jax.ShapeDtypeStruct((H * 64, total), BF16),
            jax.ShapeDtypeStruct((KEY_VALUE_HEADS, 8, total), F32),
            jax.ShapeDtypeStruct((KEY_VALUE_HEADS, micro, pairs, 2 * AUG, 128), BF16),
        ],
        compiler_params=params(60),
        cost_estimate=cost(attend_flops, 14 * MIB, 128 * H * total),
        name="attend",
    )
    (o, o_t, den, states), gy_first, out_second = together(
        (attend, has_prev, kv_natural, message, q_rot, q_feat, *bases),
        (functools.partial(gather_first, size=n_f), gy[0]),
        (columns_second, *out_near),
    )
    (out_pieces,) = together((columns_third, w_out, *out_second))

    project_out = pl.pallas_call(
        functools.partial(out_kernel, depth, n_dp),
        grid=(1,),
        in_specs=[smem] + [vmem] * 5 + columns(out_pieces, q_cols, 0),
        out_specs=[vmem] * 4,
        out_shape=[
            jax.ShapeDtypeStruct((total, width), F32),
            jax.ShapeDtypeStruct((total, width), BF16),
            jax.ShapeDtypeStruct((total, lanes), BF16),
            jax.ShapeDtypeStruct((total, 1), F32),
        ],
        scratch_shapes=[pltpu.VMEM((n_dp, total, depth), F32)],
        compiler_params=params(40),
        cost_estimate=cost(2 * total * width * H * 64, 20 * MIB),
        name="output_projection",
    )
    (x2, h2, uo, r2), gy_zero = together(
        (project_out, place, o, a_o, b_o, x, gain_two.reshape(1, width), *out_pieces),
        (gather_second, *gy_first),
    )
    gather = functools.partial(gather_first, size=n_f)

    def assemble(*pieces):
        return assembled(pieces, group, quarter)

    (h2_first,) = together((gather, h2[:rows]))
    (h2_zero,) = together((gather_second, *h2_first))

    def piece(array, m):
        return array[m * rows : (m + 1) * rows]

    row_tile = min(128, rows)

    def finish(m, terms):
        return pl.pallas_call(
            functools.partial(result_kernel, len(terms)),
            grid=(rows // row_tile,),
            in_specs=[
                pl.BlockSpec((row_tile, width), lambda r: (m * (rows // row_tile) + r, 0)),
                pl.BlockSpec((row_tile, 1), lambda r: (m * (rows // row_tile) + r, 0)),
            ]
            + term_specs(terms, row_tile, width),
            out_specs=pl.BlockSpec((row_tile, width), lambda r: (r, 0)),
            out_shape=jax.ShapeDtypeStruct((rows, width), BF16),
            compiler_params=params(40),
            cost_estimate=cost(4 * rows * width, 10 * rows * width),
            name="result",
        )(x2, valid_rows, *terms)

    def mid_back(m, terms, gy, *whole_arrays):
        here = pl.BlockSpec((row_tile, width), lambda r: (m * (rows // row_tile) + r, 0))
        thin = pl.BlockSpec((row_tile, lanes), lambda r: (m * (rows // row_tile) + r, 0))
        count = 6 + len(terms)
        return pl.pallas_call(
            functools.partial(mid_back_kernel, len(terms)),
            grid=(rows // row_tile,),
            in_specs=[
                here,
                pl.BlockSpec((row_tile, 1), lambda r: (m * (rows // row_tile) + r, 0)),
                whole((1, width)),
                pl.BlockSpec((row_tile, width), lambda r: (r, 0)),
                thin,
                whole((width, lanes)),
            ]
            + term_specs(terms, row_tile, width)
            + [pl.BlockSpec(memory_space=pl.ANY)] * len(whole_arrays),
            out_specs=[here, here, thin, whole((1, width)), whole((16, width))],
            out_shape=[
                jax.ShapeDtypeStruct((total, width), F32),
                jax.ShapeDtypeStruct((total, width), BF16),
                jax.ShapeDtypeStruct((total, lanes), BF16),
                jax.ShapeDtypeStruct((1, width), F32),
                jax.ShapeDtypeStruct((16, width), F32),
            ],
            input_output_aliases={count + i: i for i in range(len(whole_arrays))},
            compiler_params=params(40),
            cost_estimate=cost(20 * rows * width, 16 * rows * width),
            name="mid_back",
        )(x2, r2, gain_two.reshape(1, width), gy, uo, b_o, *terms, *whole_arrays)

    valid_rows = valid.astype(jnp.int32)
    def feed(split):
        def run(h2, gy, weights, *carried):
            return ffn(tile, split, h2, gy, weights, *carried)

        return run

    scatter = functools.partial(scatter_first, size=n_f)
    head_zero, h2_first, gy_first = together(
        (feed(False), h2_zero, gy_zero, w_ffn[0]), (gather, h2[rows:]), (gather, gy[1])
    )
    h2_one, gy_one, w_qkv = together(
        (gather_second, *h2_first), (gather_second, *gy_first), (assemble, *qkv_pieces)
    )
    (head_one,) = together((feed(False), h2_one, gy_one, w_ffn[0]))
    h2_zero = after(h2_zero[0], head_one[0]), *h2_zero[1:]
    ((down_zero, gh_zero),) = together((feed(True), h2_zero, gy_zero, w_ffn[1], *head_zero))
    gh_zero_terms, down_zero_terms, (down_one, gh_one) = together(
        (scatter, *gh_zero),
        (scatter, *down_zero),
        (feed(True), h2_one, gy_one, w_ffn[1], *head_one),
    )
    gh_one_first, gh_zero_terms, w_out = together(
        (scatter, *gh_one), (scatter_second, *gh_zero_terms), (assemble, *out_pieces)
    )

    go_back = pl.pallas_call(
        functools.partial(go_kernel, depth),
        grid=(n_f,),
        in_specs=[
            whole((total, width)),
            pl.BlockSpec((1, n_dp, depth, q_cols), lambda f: (f, 0, 0, 0)),
            pl.BlockSpec((q_cols, lanes), lambda f: (f, 0)),
            whole((total, lanes)),
            pl.BlockSpec((total, q_cols), lambda f: (0, f)),
        ],
        out_specs=[
            pl.BlockSpec((q_cols, total), lambda f: (f, 0)),
            pl.BlockSpec((16, q_cols), lambda f: (0, f)),
        ],
        out_shape=[
            jax.ShapeDtypeStruct((H * 64, total), BF16),
            jax.ShapeDtypeStruct((16, H * 64), F32),
        ],
        compiler_params=params(60),
        cost_estimate=cost(2 * total * width * H * 64, 12 * MIB),
        name="output_projection_back",
    )

    attend_back = pl.pallas_call(
        functools.partial(attend_back_kernel, micro),
        grid=(KEY_VALUE_HEADS,),
        in_specs=[
            prev_spec,
            n_spec,
            message_spec,
            state_spec,
            head_spec,
            feat_spec,
            head_spec,
            head_spec,
            den_spec,
            pl.BlockSpec((REPEAT, 64, 64), lambda g: (g, 0, 0)),
            whole((32, total)),
            whole((32, total)),
        ],
        out_specs=[
            pl.BlockSpec((1, total, g4), lambda g: (g * g4 // q_cols, 0, g % (q_cols // g4))),
            pl.BlockSpec((1, g4, 64), lambda g: (g, 0, 0)),
            n_spec,
            state_spec,
            back_spec,
            base_spec,
        ],
        out_shape=[
            jax.ShapeDtypeStruct((n_f, total, q_cols), BF16),
            jax.ShapeDtypeStruct((KEY_VALUE_HEADS, g4, 64), F32),
            jax.ShapeDtypeStruct((KEY_VALUE_HEADS, micro, rows, 256), F32),
            jax.ShapeDtypeStruct((KEY_VALUE_HEADS, micro, pairs, 2 * AUG, 128), F32),
            jax.ShapeDtypeStruct((KEY_VALUE_HEADS, micro, 64 + AUG, 256), BF16),
            jax.ShapeDtypeStruct((KEY_VALUE_HEADS, micro, AUG, 128), BF16),
        ],
        scratch_shapes=[pltpu.VMEM((g4, total), F32), pltpu.VMEM((g4, total), BF16)],
        compiler_params=params(60),
        cost_estimate=cost(3 * attend_flops, 24 * MIB, 128 * H * total),
        name="attend_back",
    )
    gh_one_terms, down_zero_terms, zero = together(
        (scatter_second, *gh_one_first),
        (scatter_second, *down_zero_terms),
        (functools.partial(mid_back, 0), gh_zero_terms, gy[0]),
    )

    def norm_to_heads(gh_one, gy_one, *zero):
        gx2, gb, guo, *one = mid_back(1, gh_one, gy_one, *zero[:3])
        go_t, d_ao_t = go_back(gb, w_out, a_o, guo, o)
        back = attend_back(
            has_prev, kv_natural, message, states, q_rot, q_feat, go_t, o_t, den, fq, cos_t, sin_t
        )
        return back, gx2, d_ao_t, zero[3] + one[0], zero[4] + one[1]

    def finish_and_deal(m, terms):
        return deal_out(finish(m, terms))

    (back, gx2, d_ao_t, dg2, d_bo_t), spread_zero, down_one_terms = together(
        (norm_to_heads, gh_one_terms, gy[1], *zero),
        (functools.partial(finish_and_deal, 0), down_zero_terms),
        (scatter, *down_one),
    )
    gq, d_fq, g_keys, g_states, g_message, g_total = back

    query_part = pl.pallas_call(
        functools.partial(gx_query_kernel, n_f),
        grid=(n_dp,),
        in_specs=[
            whole((n_f, total, q_cols)),
            pl.BlockSpec((n_f, 1, depth, q_cols), lambda j: (0, j, 0, 0)),
            whole((total, lanes)),
            whole((n_f, lanes, q_cols)),
        ],
        out_specs=[
            pl.BlockSpec((total, depth), lambda j: (0, j)),
            whole((total, lanes)),
            whole((32, H * 64)),
        ],
        out_shape=[
            jax.ShapeDtypeStruct((total, width), F32),
            jax.ShapeDtypeStruct((total, lanes), F32),
            jax.ShapeDtypeStruct((32, H * 64), F32),
        ],
        compiler_params=params(60),
        cost_estimate=cost(2 * total * width * 2048, 16 * MIB),
        name="query_input_gradient",
    )

    def exchange(g_message, g_total):
        return lax.ppermute(g_message, "fsdp", backward_one), shifted(g_total, n_f, -1)

    (gh_q, gu_q, d_bq_t), (g_message, g_next), down_one_terms, out_zero = together(
        (query_part, gq, w_qkv, u, b_q_t),
        (exchange, g_message, g_total),
        (scatter_second, *down_one_terms),
        (deal_in, reordered(spread_zero, inverse[0])),
    )

    next_spec = pl.BlockSpec((kv_heads, micro, AUG, 128), lambda f: (f, 0, 0, 0))
    kv_back = pl.pallas_call(
        functools.partial(kv_back_kernel, kv_heads, micro),
        grid=(n_f,),
        in_specs=[
            pl.BlockSpec((kv_heads, micro, rows, 256), lambda f: (f, 0, 0, 0)),
            pl.BlockSpec((kv_heads, micro, 64 + AUG, 256), lambda f: (f, 0, 0, 0)),
            pl.BlockSpec((kv_heads, micro, rows, 256), lambda f: (f, 0, 0, 0)),
            pl.BlockSpec((kv_heads, micro, pairs, 2 * AUG, 128), lambda f: (f, 0, 0, 0, 0)),
            pl.BlockSpec((kv_heads, 64, 64), lambda f: (f, 0, 0)),
            whole((32, total)),
            whole((32, total)),
            whole((total, lanes)),
            pl.BlockSpec((1, lanes, 2 * k_cols), lambda f: (f, 0, 0)),
            whole((total, lanes)),
            whole((total, width)),
        ]
        + [next_spec] * (n_f - 2),
        out_specs=[
            pl.BlockSpec((1, total, 2 * k_cols), lambda f: (f, 0, 0)),
            pl.BlockSpec((1, k_cols, 64), lambda f: (f, 0, 0)),
            whole((total, lanes)),
            pl.BlockSpec((None, 32, 2 * k_cols), lambda f: (f, 0, 0)),
            whole((32, width)),
        ],
        out_shape=[
            jax.ShapeDtypeStruct((n_f, total, 2 * k_cols), BF16),
            jax.ShapeDtypeStruct((n_f, k_cols, 64), F32),
            jax.ShapeDtypeStruct((total, lanes), BF16),
            jax.ShapeDtypeStruct((n_f, 32, 2 * k_cols), F32),
            jax.ShapeDtypeStruct((32, width), F32),
        ],
        scratch_shapes=[pltpu.VMEM((total, lanes), F32)],
        compiler_params=params(60),
        cost_estimate=cost(8 * total * 128 * 128, 8 * MIB),
        name="key_value_back",
    )
    input_back = pl.pallas_call(
        functools.partial(gx_kernel, n_f, depth),
        grid=(n_dp,),
        in_specs=[
            pl.BlockSpec((total, depth), lambda j: (0, j)),
            whole((n_f, total, 2 * k_cols)),
            pl.BlockSpec((n_f, 1, depth, 2 * k_cols), lambda j: (0, j, 0, q_cols // (2 * k_cols))),
            whole((total, lanes)),
            pl.BlockSpec((depth, lanes), lambda j: (j, 0)),
            pl.BlockSpec((total, depth), lambda j: (0, j)),
            whole((total, width)),
            whole((total, width)),
            whole((total, 1)),
            whole((n_dp, 1, depth)),
        ],
        out_specs=[whole((total, width)), pl.BlockSpec((1, depth), lambda j: (0, j))],
        out_shape=[
            jax.ShapeDtypeStruct((total, width), BF16),
            jax.ShapeDtypeStruct((1, width), F32),
        ],
        scratch_shapes=[pltpu.VMEM((n_dp, total, depth), F32), pltpu.VMEM((total, 1), F32)],
        compiler_params=params(60),
        cost_estimate=cost(2 * total * width * 1024, 30 * MIB),
        name="input_gradient",
    )
    def heads_to_input(g_keys, g_message, g_next, gu_q, gh_q):
        gkv, d_fk, gu, d_bkv_t, d_qkv_t = kv_back(
            g_keys, g_message, kv_natural, g_states, fk, cos_t, sin_t, u, b_kv_t, gu_q, h1,
            *g_next,
        )
        gx, dg1 = input_back(
            gh_q, gkv, w_qkv, gu, a_qkv, x, x, gx2, r1, gain_one.reshape(n_dp, 1, depth)
        )
        return gx, dg1, d_fk, d_bkv_t, d_qkv_t

    (gx, dg1, d_fk, d_bkv_t, d_qkv_t), spread_one = together(
        (heads_to_input, g_keys, g_message, g_next, gu_q, gh_q),
        (functools.partial(finish_and_deal, 1), down_one_terms),
    )
    output = [out_zero, deal_in(reordered(spread_one, inverse[1]))]

    wide = pl.pallas_call(
        table_kernel,
        out_shape=jax.ShapeDtypeStruct((width, lanes), F32),
        compiler_params=pltpu.CompilerParams(vmem_limit_bytes=60 * MIB),
        name="table",
    )(d_fq.reshape(H * 64, 64), d_qkv_t, d_ao_t, d_bq_t, d_bo_t, dg1, dg2)
    kv_rows = KEY_VALUE_HEADS * 64
    d_bk = d_bkv_t[:, rank : 2 * rank, :k_cols].transpose(0, 2, 1).reshape(kv_rows, rank)
    d_bv = d_bkv_t[:, 2 * rank : 3 * rank, k_cols:].transpose(0, 2, 1).reshape(kv_rows, rank)
    narrow = jnp.concatenate(
        [d_fk.reshape(kv_rows, 64), d_bk, d_bv, jnp.zeros((kv_rows, lanes - 80), F32)], axis=1
    )
    wide = wide.reshape(n_all, width // n_all, lanes)
    narrow = narrow.reshape(n_all, kv_rows // n_all, lanes)
    table = jnp.concatenate([wide, narrow], axis=1).astype(BF16)
    moved = lax.all_to_all(table, ("dp", "fsdp"), split_axis=0, concat_axis=0, tiled=True)
    table = jnp.sum(moved.astype(F32), axis=0)
    wide, narrow = table[: width // n_all], table[width // n_all :]
    shares = (
        wide[:, 64:96],
        wide[:, 96:112],
        narrow[:, 64:80],
        wide[:, :64],
        narrow[:, :64],
        wide[:, 112:114],
    )
    return (jnp.stack(output)[None], gx.reshape(1, micro, rows, width), *shares)


def solution(mesh):
    every = ("dp", "fsdp")
    blocks = P("dp", None, "fsdp", None)
    in_specs = (
        blocks,
        blocks,
        P(),
        P(),
        P("dp", "fsdp"),
        P("dp", "fsdp"),
        P("dp", "fsdp"),
        P("fsdp", "dp"),
        P("dp", "fsdp"),
        P("dp", "fsdp"),
        P("fsdp", "dp"),
    ) + (P(every, None),) * 6
    out_specs = (blocks, blocks) + (P(every, None),) * 6
    return jax.shard_map(shards, mesh=mesh, in_specs=in_specs, out_specs=out_specs, check_vma=False)
```

```python
import functools
import math

import jax
import jax.numpy as jnp
from jax import lax
from jax.experimental import pallas as pl
from jax.experimental.pallas import tpu as pltpu
from jax.sharding import PartitionSpec as P

H = 32
KEY_VALUE_HEADS = 8
REPEAT = H // KEY_VALUE_HEADS
HEAD_SIZE = 64
ADAPTER_RANK = 8
WIN = 64
AUG = 80
RANK_LANES = 128

EPSILON = 1e-05
ROPE_BASE = 500000.0
F32 = jnp.float32
BF16 = jnp.bfloat16
MIB = 1024 * 1024
X_PAIRS = [(i, i ^ 1) for i in range(4)]
Y_PAIRS = [(i, i ^ 2) for i in range(4)]


def dot(a, b):
    return lax.dot_general(a, b, (((1,), (0,)), ((), ())), preferred_element_type=F32)


def dot_nt(a, b):
    return lax.dot_general(a, b, (((1,), (1,)), ((), ())), preferred_element_type=F32)


def params(mib, semantics=("arbitrary",)):
    return pltpu.CompilerParams(vmem_limit_bytes=mib * MIB, dimension_semantics=semantics)


def cost(flops, bytes_accessed, transcendentals=0):
    return pl.CostEstimate(
        flops=int(flops), bytes_accessed=int(bytes_accessed), transcendentals=int(transcendentals)
    )


def whole(shape):
    return pl.BlockSpec(shape, lambda *_: (0,) * len(shape))


def after(value, *others):
    return lax.optimization_barrier((value, *others))[0]


def together(*jobs):
    arguments = lax.optimization_barrier([job[1:] for job in jobs])
    return lax.optimization_barrier([job[0](*args) for job, args in zip(jobs, arguments)])


def by_x(rows):
    return lax.ppermute(rows, "fsdp", X_PAIRS)


def by_y(rows):
    return lax.ppermute(rows, "fsdp", Y_PAIRS)


def rope_tables_t(positions):
    half_size = HEAD_SIZE // 2
    frequencies = jnp.exp(
        -(2.0 * jnp.arange(half_size, dtype=F32) / HEAD_SIZE) * math.log(ROPE_BASE)
    )
    angles = frequencies[:, None] * positions.astype(F32)[None, :]
    return jnp.cos(angles), jnp.sin(angles)


def rotate_t(head, cos_t, sin_t):
    a, b = head[:32], head[32:]
    return jnp.concatenate([a * cos_t - b * sin_t, b * cos_t + a * sin_t], axis=0)


def rotate_back_t(head, cos_t, sin_t):
    a, b = head[:32], head[32:]
    return jnp.concatenate([a * cos_t + b * sin_t, b * cos_t - a * sin_t], axis=0)


def half_softmax_t(scores):
    e = jnp.exp(scores - jnp.max(scores, axis=0, keepdims=True))
    return e * (1.0 / jnp.sum(e, axis=0, keepdims=True))


def features_t(mapped):
    return jnp.concatenate([half_softmax_t(mapped[:64]), half_softmax_t(mapped[64:])], axis=0)


def features_back_t(e, f):
    ef = e * f
    t1 = jnp.sum(ef[:64], axis=0, keepdims=True)
    t2 = jnp.sum(ef[64:], axis=0, keepdims=True)
    return (ef[:64] - e[:64] * t1) - (ef[64:] - e[64:] * t2)


def block_pieces(refs, place_ref, n_dp):
    if len(refs) == 9:
        own, x_mine, y_mine, dx_mine, dy_mine, x_other, y_other, dx_other, dy_other = refs
        shard, core = place_ref[0], place_ref[1]
        half = n_dp // 2
        mine, other = core * half, (1 - core) * half
        quarter = half // 2
        return [
            (shard, [(own, 0)]),
            (shard ^ 1, [(x_mine, mine), (x_other, other)]),
            (shard ^ 2, [(y_mine, mine), (y_other, other)]),
            (
                shard ^ 3,
                [
                    (dx_mine, mine),
                    (dy_mine, mine + quarter),
                    (dx_other, other),
                    (dy_other, other + quarter),
                ],
            ),
        ]
    return [(f, [(ref, 0)]) for f, ref in enumerate(refs)]


def project(h1_ref, u_ref, pieces, low_rank, depth):
    total = dot(u_ref[...], low_rank)
    for ref, start in pieces:
        count = ref.shape[0] * depth
        if isinstance(start, int):
            columns = h1_ref[:, start * depth : start * depth + count]
        else:
            columns = h1_ref[:, pl.ds(pl.multiple_of(start * depth, depth), count)]
        total += dot(columns, ref[...].reshape(count, ref.shape[2]))
    return total


def kv_kernel(kv_heads, micro, depth, n_dp, place_ref, h1_ref, u_ref, b_ref, cos_ref, sin_ref,
              f_ref, *refs):
    *w_refs, n_ref, tot_ref, msg_ref = refs
    rows = h1_ref.shape[0] // micro
    cos_t, sin_t = cos_ref[...], sin_ref[...]
    width = kv_heads * HEAD_SIZE
    for f, pieces in block_pieces(w_refs, place_ref, n_dp):
        kv_t = project(h1_ref, u_ref, pieces, b_ref[f], depth).T
        for g in range(kv_heads):
            head = f * kv_heads + g
            kr = rotate_t(kv_t[g * 64 : (g + 1) * 64], cos_t, sin_t).astype(BF16)
            v = kv_t[width + g * 64 : width + (g + 1) * 64].astype(BF16)
            pk = features_t(dot(f_ref[head], kr)).astype(BF16)
            natural = (
                jnp.concatenate([pk.astype(F32), kr.astype(F32), v.astype(F32)], axis=0).T
            ).astype(BF16)
            v_aug = jnp.concatenate([v, jnp.ones((AUG - 64, v.shape[1]), BF16)], axis=0)
            for m in range(micro):
                part = natural[m * rows : (m + 1) * rows]
                n_ref[head, m] = part
                sums = dot(v_aug[:, m * rows : (m + 1) * rows], part[:, :128])
                tot_ref[head, m] = sums.astype(BF16)
                msg_ref[head, m, :64] = part[rows - 64 :]
                tail = jnp.concatenate([sums[48:], jnp.zeros((16, 128), F32)], axis=0)
                msg_ref[head, m, 64:] = jnp.concatenate([sums[:48], tail], axis=1).astype(BF16)


def q_kernel(heads, depth, n_dp, place_ref, h1_ref, u_ref, b_ref, cos_ref, sin_ref, f_ref, *refs):
    *w_refs, qr_ref, pq_ref = refs
    cos_t, sin_t = cos_ref[...], sin_ref[...]
    for f, pieces in block_pieces(w_refs, place_ref, n_dp):
        q_t = project(h1_ref, u_ref, pieces, b_ref[f], depth).T
        for h in range(heads):
            head = f * heads + h
            qr = rotate_t(q_t[h * 64 : (h + 1) * 64], cos_t, sin_t).astype(BF16)
            pq = features_t(dot(f_ref[head], qr)).astype(BF16)
            if isinstance(head, int):
                qr_ref[head * 64 : (head + 1) * 64] = qr
                pq_ref[head * 128 : (head + 1) * 128] = pq
            else:
                qr_ref[pl.ds(pl.multiple_of(head * 64, 64), 64)] = qr
                pq_ref[pl.ds(pl.multiple_of(head * 128, 128), 128)] = pq


def pair_masks(has_prev):
    lane = lax.broadcasted_iota(jnp.int32, (64, REPEAT * 128), 1)
    row = lax.broadcasted_iota(jnp.int32, (64, REPEAT * 128), 0)
    low = (lane % 128) < 64
    ahead = row - lane % 64
    value = jnp.where(low, ahead - 1, -ahead)
    hidden = jnp.where(low, (1 - has_prev) * 1024, 0)
    return low, value >= 0, value - hidden >= 0


def heads_side(ref, size, start):
    return jnp.concatenate(
        [ref[h * size : (h + 1) * size, start : start + 128] for h in range(REPEAT)], axis=1
    )


def attend_kernel(micro, prev_ref, n_ref, msg_ref, qr_ref, pq_ref, *refs):
    *base_refs, o_ref, ot_ref, den_ref, s_ref = refs
    rows = n_ref.shape[2]
    low, mask_a, mask_first = pair_masks(prev_ref[0])
    low_row = (lax.broadcasted_iota(jnp.int32, (1, REPEAT * 128), 1) % 128) < 64
    key_lane = lax.broadcasted_iota(jnp.int32, (AUG, 128), 1) < 64
    for m in range(micro):
        ext = jnp.concatenate([msg_ref[0, m, :64], n_ref[0, m]], axis=0)
        ext_t = ext.astype(F32).T.astype(BF16)
        near = jnp.concatenate([msg_ref[0, m, 64:112, :128], msg_ref[0, m, 64:96, 128:]], axis=0)
        v_aug_all = jnp.concatenate([ext_t[192:256], jnp.ones((AUG - 64, rows + WIN), BF16)], axis=0)
        running = near.astype(F32)
        for base_ref in base_refs:
            running += base_ref[0, m].astype(F32)
        for p in range(rows // 128):
            start = m * rows + p * 128
            r0 = p * 128
            qr4 = heads_side(qr_ref, 64, start)
            pq4 = heads_side(pq_ref, 128, start)
            pk = ext[r0 : r0 + 128, :128]
            kr = ext[r0 : r0 + 192, 128:192]
            v_aug = v_aug_all[:, r0 : r0 + 128]
            zero = jnp.zeros_like(v_aug)
            spans = dot(
                jnp.concatenate(
                    [jnp.where(key_lane, v_aug, zero), jnp.where(key_lane, zero, v_aug)], axis=0
                ),
                pk,
            )
            if p == 0:
                running = running - spans[:AUG]
            state = jnp.concatenate([running, running + spans[:AUG]], axis=0).astype(BF16)
            running = running + spans[:AUG] + spans[AUG:]
            s_ref[0, m, p] = state
            from_state = dot(state, pq4)
            scores = dot(kr, qr4) * (1.0 / math.sqrt(HEAD_SIZE))
            linear = dot(pk, pq4)
            exp_a = jnp.exp(jnp.where(low, scores[:64], scores[128:]))
            exp_b = jnp.exp(scores[64:128])
            mask = mask_first if p == 0 else mask_a
            w_a = jnp.where(mask, exp_a, jnp.where(low, linear[:64], 0.0))
            w_b = jnp.where(mask_a, jnp.where(low, 0.0, linear[64:]), exp_b)
            den = (
                jnp.sum(w_a, axis=0, keepdims=True)
                + jnp.sum(w_b, axis=0, keepdims=True)
                + jnp.where(low_row, from_state[64:65], from_state[AUG + 64 : AUG + 65])
            )
            inv = 1.0 / den
            p_a = w_a * inv
            weights = jnp.concatenate(
                [jnp.where(low, p_a, 0.0), w_b * inv, jnp.where(low, 0.0, p_a)], axis=0
            ).astype(BF16)
            out = (
                dot(ext_t[192:256, r0 : r0 + 192], weights)
                + jnp.where(low, from_state[:64], from_state[AUG : AUG + 64]) * inv
            )
            for h in range(REPEAT):
                den_ref[0, h : h + 1, start : start + 128] = den[:, h * 128 : (h + 1) * 128]
            out_t = jnp.concatenate(
                [out[:, h * 128 : (h + 1) * 128] for h in range(REPEAT)], axis=0
            )
            ot_ref[:, start : start + 128] = out_t.astype(BF16)
            o_ref[start : start + 128, :] = out_t.T.astype(BF16)


def attend_back_kernel(micro, prev_ref, n_ref, msg_ref, s_ref, qr_ref, pq_ref, go_ref, ot_ref,
                       den_ref, f_ref, cos_ref, sin_ref,
                       gq_ref, df_ref, gn_ref, gs_ref, back_ref, total_ref,
                       gqr_ref, gmq_ref):
    rows = n_ref.shape[2]
    low, mask_a, mask_first = pair_masks(prev_ref[0])
    low_aug = (lax.broadcasted_iota(jnp.int32, (AUG, REPEAT * 128), 1) % 128) < 64
    low_feat = (lax.broadcasted_iota(jnp.int32, (128, REPEAT * 128), 1) % 128) < 64
    scale = 1.0 / math.sqrt(HEAD_SIZE)
    for m in range(micro):
        ext = jnp.concatenate([msg_ref[0, m, :64], n_ref[0, m]], axis=0)
        ext_t = ext.astype(F32).T.astype(BF16)
        tail = g_sum = None
        for p in range(rows // 128):
            start = m * rows + p * 128
            r0 = p * 128
            qr4 = heads_side(qr_ref, 64, start)
            pq4 = heads_side(pq_ref, 128, start)
            go4 = heads_side(go_ref, 64, start)
            o4 = heads_side(ot_ref, 64, start)
            den = jnp.concatenate(
                [den_ref[0, h : h + 1, start : start + 128] for h in range(REPEAT)], axis=1
            )
            inv = 1.0 / den
            pk = ext[r0 : r0 + 128, :128]
            kr = ext[r0 : r0 + 192, 128:192]
            v = ext[r0 : r0 + 192, 192:256]
            go_f = go4.astype(F32)
            delta = jnp.sum(go_f * o4.astype(F32), axis=0, keepdims=True)
            scores = dot(kr, qr4) * scale
            linear = dot(pk, pq4)
            g_p = dot(v, go4)
            mask = mask_first if p == 0 else mask_a
            exp_a = jnp.exp(jnp.where(low, scores[:64], scores[128:]))
            exp_b = jnp.exp(scores[64:128])
            p_a = jnp.where(mask, exp_a, jnp.where(low, linear[:64], 0.0)) * inv
            p_b = jnp.where(mask_a, jnp.where(low, 0.0, linear[64:]), exp_b) * inv
            weights = jnp.concatenate(
                [jnp.where(low, p_a, 0.0), p_b, jnp.where(low, 0.0, p_a)], axis=0
            ).astype(BF16)
            gw_a = (jnp.where(low, g_p[:64], g_p[128:]) - delta) * inv
            gw_b = (g_p[64:128] - delta) * inv
            gs_a = jnp.where(mask, gw_a * exp_a, 0.0)
            gs_b = jnp.where(mask_a, 0.0, gw_b * exp_b)
            g_scores = jnp.concatenate(
                [jnp.where(low, gs_a, 0.0), gs_b, jnp.where(low, 0.0, gs_a)], axis=0
            ).astype(BF16)
            g_linear = jnp.concatenate(
                [
                    jnp.where(mask_a, 0.0, jnp.where(low, gw_a, 0.0)),
                    jnp.where(mask_a, jnp.where(low, 0.0, gw_b), 0.0),
                ],
                axis=0,
            ).astype(BF16)
            go_aug = jnp.concatenate(
                [go_f * inv, -delta * inv, jnp.zeros((AUG - 65, REPEAT * 128), F32)], axis=0
            )
            go_aug_b = go_aug.astype(BF16)
            gqr = dot(ext_t[128:192, r0 : r0 + 192], g_scores) * scale
            state_t = s_ref[0, m, p].astype(F32).T.astype(BF16)
            gpq = dot(ext_t[:128, r0 : r0 + 128], g_linear) + jnp.where(
                low_feat, dot(state_t[:, :AUG], go_aug_b), dot(state_t[:, AUG:], go_aug_b)
            )
            zero = jnp.zeros_like(go_aug_b)
            g_spans = dot_nt(
                jnp.concatenate(
                    [jnp.where(low_aug, go_aug_b, zero), jnp.where(low_aug, zero, go_aug_b)], axis=0
                ),
                pq4,
            )
            gs_ref[0, m, p] = g_spans
            both = g_spans[:AUG] + g_spans[AUG:]
            g_sum = both if p == 0 else g_sum + both
            if p == 0:
                back_ref[0, m, 64:, :128] = g_spans[:AUG].astype(BF16)
            g_pk = dot_nt(g_linear, pq4)
            g_kr = dot_nt(g_scores, qr4) * scale
            g_v = dot_nt(weights, go4)
            g_keys = jnp.concatenate(
                [
                    jnp.concatenate([g_pk, jnp.zeros((64, 128), F32)], axis=0),
                    g_kr,
                    g_v,
                ],
                axis=1,
            )
            if p == 0:
                back_ref[0, m, :64] = g_keys[:64].astype(BF16)
            else:
                gn_ref[0, m, r0 - 64 : r0] = g_keys[:64] + tail
            gn_ref[0, m, r0 : r0 + 64] = g_keys[64:128]
            tail = g_keys[128:]
            if p == rows // 128 - 1:
                gn_ref[0, m, rows - 64 : rows] = tail
                total_ref[0, m] = g_sum.astype(BF16)
                back_ref[0, m, 64:, 128:] = g_sum.astype(BF16)
            pq_f = pq4.astype(F32)
            gmq = features_back_t(pq_f, gpq).astype(BF16)
            for h in range(REPEAT):
                gqr_ref[h * 64 : (h + 1) * 64, start : start + 128] = gqr[:, h * 128 : (h + 1) * 128]
                gmq_ref[h * 64 : (h + 1) * 64, start : start + 128] = gmq[:, h * 128 : (h + 1) * 128]
    cos_t, sin_t = cos_ref[...], sin_ref[...]
    grads = []
    for h in range(REPEAT):
        sl = slice(h * 64, (h + 1) * 64)
        gmq = gmq_ref[sl]
        df_ref[0, sl] = dot_nt(qr_ref[sl], gmq)
        grads.append(rotate_back_t(gqr_ref[sl] + dot(f_ref[h], gmq), cos_t, sin_t))
    gq_ref[0] = jnp.concatenate(grads, axis=0).T.astype(BF16)


def kv_back_kernel(kv_heads, micro, gn_ref, back_ref, n_ref, gs_ref, f_ref, cos_ref, sin_ref,
                   u_ref, b_ref, guq_ref, h1_ref, *refs):
    *next_refs, gkv_ref, df_ref, gu_ref, db_ref, dqkv_ref, acc_ref = refs
    rows = n_ref.shape[2]
    spans = rows // WIN
    cos_t, sin_t = cos_ref[...], sin_ref[...]
    keys, values = [], []
    unit = (lax.broadcasted_iota(jnp.int32, (64, AUG - 64), 1) == 0).astype(BF16)
    for g in range(kv_heads):
        parts = []
        for m in range(micro):
            natural = n_ref[g, m]
            later = [None] * spans
            after_here = back_ref[g, m, 64:, 128:].astype(F32)
            for ref in next_refs:
                after_here += ref[g, m].astype(F32)
            later[spans - 1] = after_here - back_ref[g, m, 64:, :128].astype(F32)
            later[spans - 2] = after_here
            for c in range(spans - 3, -1, -1):
                later[c] = later[c + 1] + gs_ref[g, m, (c + 2) // 2, ((c + 2) % 2) * AUG : ((c + 2) % 2 + 1) * AUG]
            for c in range(spans):
                part = natural[c * 64 : (c + 1) * 64]
                grad = gn_ref[g, m, c * 64 : (c + 1) * 64]
                if c == spans - 1:
                    grad = grad + back_ref[g, m, :64].astype(F32)
                big = later[c].astype(BF16)
                g_pk = dot(jnp.concatenate([part[:, 192:256], unit], axis=1), big)
                g_v = dot_nt(part[:, :128], big[:64])
                parts.append(
                    grad + jnp.concatenate([g_pk, jnp.zeros((64, 64), F32), g_v], axis=1)
                )
        grad_t = jnp.concatenate(parts, axis=0).T
        nat_t = jnp.concatenate([n_ref[g, m, :, :192] for m in range(micro)], axis=0).astype(F32).T
        gmk = features_back_t(nat_t[:128], grad_t[:128]).astype(BF16)
        df_ref[0, g * 64 : (g + 1) * 64] = dot_nt(nat_t[128:].astype(BF16), gmk)
        keys.append(rotate_back_t(grad_t[128:192] + dot(f_ref[g], gmk), cos_t, sin_t))
        values.append(grad_t[192:256])
    gkv = jnp.concatenate(keys + values, axis=0).T.astype(BF16)
    gkv_ref[0] = gkv
    db_ref[...] = dot(u_ref[...].astype(F32).T[:32].astype(BF16), gkv)
    rank_grad = dot_nt(gkv, b_ref[0])

    @pl.when(pl.program_id(0) == 0)
    def _():
        acc_ref[...] = guq_ref[...] + rank_grad

    @pl.when(pl.program_id(0) > 0)
    def _():
        acc_ref[...] += rank_grad

    @pl.when(pl.program_id(0) == pl.num_programs(0) - 1)
    def _():
        gu_ref[...] = acc_ref[...].astype(BF16)
        dqkv_ref[...] = dot(acc_ref[...].T[:32].astype(BF16), h1_ref[...])


def table_kernel(heads_ref, dqkv_ref, dao_ref, dbq_ref, dbo_ref, dg1_ref, dg2_ref, out_ref):
    width = dqkv_ref.shape[1]
    gains = jnp.concatenate([dg1_ref[...], dg2_ref[...], jnp.zeros((6, width), F32)], axis=0)
    rows = jnp.concatenate(
        [dqkv_ref[:24], dao_ref[:8], dbq_ref[:8], dbo_ref[:8], gains, jnp.zeros((8, width), F32)],
        axis=0,
    )
    out_ref[...] = jnp.concatenate([heads_ref[...], rows.T], axis=1)


def out_kernel(depth, n_dp, place_ref, o_ref, ao_ref, bo_ref, x_ref, gain_ref, *refs):
    *w_refs, x2_ref, h2_ref, uo_ref, r2_ref, acc_ref = refs
    uo = dot(o_ref[...], ao_ref[...]).astype(BF16)
    uo_ref[...] = uo
    for j in range(n_dp):
        cols = slice(j * depth, (j + 1) * depth)
        acc_ref[j] = x_ref[:, cols].astype(F32) + dot_nt(uo, bo_ref[cols])
    halves = w_refs[0].shape[2] // depth
    block = halves * depth
    for f, pieces in block_pieces(w_refs, place_ref, n_dp):
        for ref, start in pieces:
            for i in range(ref.shape[0]):
                total = None
                for a in range(halves):
                    e0 = f * block + a * depth
                    if not isinstance(f, int):
                        e0 = pl.multiple_of(e0, depth)
                    term = dot(o_ref[:, pl.ds(e0, depth)], ref[i, :, a * depth : (a + 1) * depth])
                    total = term if total is None else total + term
                acc_ref[start + i] += total
    squares = 0.0
    for j in range(n_dp):
        x2 = acc_ref[j]
        x2_ref[:, j * depth : (j + 1) * depth] = x2
        squares += jnp.sum(x2 * x2, axis=1, keepdims=True)
    r2 = lax.rsqrt(squares * (1.0 / (n_dp * depth)) + EPSILON)
    r2_ref[...] = r2
    for j in range(n_dp):
        cols = slice(j * depth, (j + 1) * depth)
        h2_ref[:, cols] = (acc_ref[j] * r2 * gain_ref[:, cols]).astype(BF16)


def go_kernel(depth, gb_ref, w_ref, ao_ref, guo_ref, o_ref, go_ref, dao_ref):
    groups = w_ref.shape[1]
    halves = w_ref.shape[3] // depth
    guo = guo_ref[...]
    low_rank = dot_nt(ao_ref[...], guo)
    for a in range(halves):
        total = low_rank[a * depth : (a + 1) * depth]
        for j in range(groups):
            total += dot_nt(
                w_ref[0, j, :, a * depth : (a + 1) * depth], gb_ref[:, j * depth : (j + 1) * depth]
            )
        go_ref[a * depth : (a + 1) * depth] = total.astype(BF16)
    dao_ref[...] = dot(guo.astype(F32).T[:16].astype(BF16), o_ref[...])


def gx_query_kernel(shards, gq_ref, wq_ref, u_ref, b_ref, out_ref, gu_ref, db_ref):
    total = dot_nt(gq_ref[0], wq_ref[0, 0])
    for f in range(1, shards):
        total += dot_nt(gq_ref[f], wq_ref[f, 0])
    out_ref[...] = total

    @pl.when(pl.program_id(0) == 0)
    def _():
        u_t = u_ref[...].astype(F32).T[:32].astype(BF16)
        cols = gq_ref.shape[2]
        rank_grad = 0.0
        for f in range(shards):
            rank_grad += dot_nt(gq_ref[f], b_ref[f])
            db_ref[:, f * cols : (f + 1) * cols] = dot(u_t, gq_ref[f])
        gu_ref[...] = rank_grad


def gx_kernel(shards, depth, part_ref, gkv_ref, wkv_ref, gu_ref, a_ref, x_ref, x_all_ref,
              gx2_ref, r1_ref, gain_ref, gx_ref, dg_ref, gh_all, dot_ref):
    j = pl.program_id(0)
    last = pl.num_programs(0) - 1

    @pl.when(j == 0)
    def _():
        dot_ref[...] = jnp.zeros_like(dot_ref)

    total = part_ref[...] + dot_nt(gu_ref[...], a_ref[...])
    for f in range(shards):
        total += dot_nt(gkv_ref[f], wkv_ref[f, 0])
    gh_all[j] = total
    hx = total * x_ref[...].astype(F32)
    dg_ref[...] = jnp.sum(hx * r1_ref[...], axis=0, keepdims=True)
    dot_ref[...] += jnp.sum(hx * gain_ref[0], axis=1, keepdims=True)

    @pl.when(j == last)
    def _():
        count = gh_all.shape[0]
        r1 = r1_ref[...]
        back = r1 * r1 * r1 * dot_ref[...] * (1.0 / (count * depth))
        for i in range(count):
            cols = slice(i * depth, (i + 1) * depth)
            gx_ref[:, cols] = (
                gx2_ref[:, cols]
                + r1 * gain_ref[i] * gh_all[i]
                - x_all_ref[:, cols].astype(F32) * back
            ).astype(BF16)


def pack_attention_kernel(wq_ref, wk_ref, wv_ref, wo_ref, qkv_ref, out_ref):
    depth, q_cols = wq_ref.shape
    qkv_ref[:, :q_cols] = wq_ref[...]
    qkv_ref[:, q_cols:] = jnp.concatenate([wk_ref[...], wv_ref[...]], axis=1)
    for a in range(wo_ref.shape[0] // depth):
        out_ref[:, a * depth : (a + 1) * depth] = wo_ref[a * depth : (a + 1) * depth]


def pack_ffn_kernel(cuts, wg_ref, wu_ref, wd_ref, *refs):
    for ref, start, stop in zip(refs, cuts, cuts[1:]):
        count = stop - start
        ref[:, :count] = wg_ref[:, start:stop]
        ref[:, count : 2 * count] = wu_ref[:, start:stop]
        step = min(256, count)
        for at in range(0, count, step):
            ref[:, 2 * count + at : 2 * count + at + step] = (
                wd_ref[start + at : start + at + step].astype(F32).T.astype(BF16)
            )


def joined(refs):
    own_a, own_b, x_a, y_a, y_b, x_b = refs
    left = own_a[0].astype(F32) + x_a[0].astype(F32) + y_a[...].astype(F32)
    right = own_b[0].astype(F32) + y_b[0].astype(F32) + x_b[...].astype(F32)
    return jnp.concatenate([left, right], axis=1)


def result_kernel(count, x2_ref, valid_ref, *refs):
    *parts, out_ref = refs
    total = joined(parts) if count == 6 else parts[0][...]
    out_ref[...] = jnp.where(valid_ref[...] > 0, x2_ref[...] + total, 0.0).astype(BF16)


def mid_back_kernel(count, x2_ref, r2_ref, gain_ref, gy_ref, uo_ref, bo_ref, *refs):
    gx2_ref, gb_ref, guo_ref, dg_ref, dbo_ref = refs[-5:]
    parts = refs[:count]
    gh = joined(parts) if count == 6 else parts[0][...]
    x2, r2 = x2_ref[...], r2_ref[...]
    gx = gh * x2
    scaled = gh * gain_ref[...]
    mean = jnp.mean(scaled * x2, axis=1, keepdims=True)
    gx2 = gy_ref[...].astype(F32) + r2 * scaled - x2 * (r2 * r2 * r2 * mean)
    gx2_ref[...] = gx2
    gb = gx2.astype(BF16)
    gb_ref[...] = gb
    guo_ref[...] = dot(gb, bo_ref[...]).astype(BF16)
    dg = jnp.sum(gx * r2, axis=0, keepdims=True)
    dbo = dot(uo_ref[...].astype(F32).T[:16].astype(BF16), gb)

    @pl.when(pl.program_id(0) == 0)
    def _():
        dg_ref[...] = dg
        dbo_ref[...] = dbo

    @pl.when(pl.program_id(0) > 0)
    def _():
        dg_ref[...] += dg
        dbo_ref[...] += dbo


def row_copies(refs, rows_ref, sems, r):
    tile, width = rows_ref.shape[1:]
    half_tile, half = tile // 2, width // 2
    if len(refs) == 1:
        parts = [(refs[0].at[r * tile : (r + 1) * tile], rows_ref.at[r])]
    elif r == 0:
        parts = [(refs[i], rows_ref.at[0, i * half_tile : (i + 1) * half_tile]) for i in range(2)]
    else:
        parts = [(refs[2], rows_ref.at[1, :half_tile])]
        parts += [
            (refs[3 + i], rows_ref.at[1, half_tile:, i * half : (i + 1) * half]) for i in range(2)
        ]
    return [
        pltpu.make_async_copy(source, target, sems.at[r, i])
        for i, (source, target) in enumerate(parts)
    ]


def store_rows(value_ref, refs):
    if len(refs) == 1:
        refs[0][...] = value_ref[...].astype(BF16)
        return
    send_x, keep_x, send_y, keep_y = refs
    count, half = value_ref.shape[0] // 2, value_ref.shape[1] // 2
    keep_x[0] = value_ref[:count, :half].astype(BF16)
    send_x[0] = value_ref[count:, :half].astype(BF16)
    for here, ref in enumerate((keep_y, send_y)):

        @pl.when(pl.program_id(0) == here)
        def _(ref=ref):
            ref[0] = value_ref[:count, half:].astype(BF16)
            ref[1] = value_ref[count:, half:].astype(BF16)


def ffn_kernel(pieces, carries, wg_ref, wu_ref, wd_ref, *refs):
    h2_refs, gy_refs = refs[:pieces], refs[pieces : 2 * pieces]
    carried = refs[2 * pieces : 2 * pieces + carries]
    *out_refs, h2_ref, gy_ref, out_acc, gh_acc, h2_sems, gy_sems = refs[2 * pieces + carries :]
    r, j = pl.program_id(0), pl.program_id(1)
    copies = [
        row_copies(h2_refs, h2_ref, h2_sems, tile) + row_copies(gy_refs, gy_ref, gy_sems, tile)
        for tile in range(2)
    ]

    @pl.when((r == 0) & (j == 0))
    def _():
        for copy in copies[0] + copies[1]:
            copy.start()
        for copy in copies[0]:
            copy.wait()

    @pl.when((r == 1) & (j == 0))
    def _():
        for copy in copies[1]:
            copy.wait()

    h2, gy = h2_ref[r], gy_ref[r]
    shape = (wg_ref.shape[0] * wg_ref.shape[1], wg_ref.shape[2])
    wg, wu, wd = wg_ref[...].reshape(shape), wu_ref[...].reshape(shape), wd_ref[...].reshape(shape)
    gate = dot(h2, wg)
    up = dot(h2, wu)
    g_hid = dot(gy, wd)
    sig = 1.0 / (1.0 + jnp.exp(-gate))
    silu = gate * sig
    hid = (silu * up).astype(BF16)
    g_gate = (g_hid * up * sig * (1.0 + gate * (1.0 - sig))).astype(BF16)
    g_up = (g_hid * silu).astype(BF16)

    @pl.when(j == 0)
    def _():
        out, gh = dot_nt(hid, wd), dot_nt(g_gate, wg) + dot_nt(g_up, wu)
        if carries:
            out += carried[0][...].astype(F32)
            gh += carried[1][...].astype(F32)
        out_acc[...] = out
        gh_acc[...] = gh

    @pl.when(j > 0)
    def _():
        out_acc[...] += dot_nt(hid, wd)
        gh_acc[...] += dot_nt(g_gate, wg) + dot_nt(g_up, wu)

    @pl.when(j == pl.num_programs(1) - 1)
    def _():
        half = len(out_refs) // 2
        store_rows(out_acc, out_refs[:half])
        store_rows(gh_acc, out_refs[half:])


def ffn(tile, split, h2, gy, weights, *carried):
    total = sum(part.size for part in h2) // h2[0].shape[1]
    width = h2[0].shape[1]
    groups, depth, cols = weights.shape
    tiles = cols // (3 * tile)
    pieces = len(h2)
    row_tile = total // 2
    row_spec = pl.BlockSpec((row_tile, width), lambda r, j: (r, 0))

    def weight_spec(kind):
        return pl.BlockSpec((groups, depth, tile), lambda r, j: (0, 0, kind * tiles + j))

    piece_specs = [pl.BlockSpec(memory_space=pl.ANY)] * pieces
    if split and pieces > 1:
        count, half = row_tile // 2, width // 2
        moving = pl.BlockSpec((1, count, half), lambda r, j: (r, 0, 0))
        fixed = pl.BlockSpec((2, count, half), lambda r, j: (0, 0, 0))
        out_specs = [moving, moving, fixed, fixed] * 2
        out_shape = [jax.ShapeDtypeStruct((2, count, half), BF16)] * 8
    else:
        out_specs = [row_spec, row_spec]
        out_shape = [jax.ShapeDtypeStruct((total, width), BF16)] * 2
    outs = pl.pallas_call(
        functools.partial(ffn_kernel, pieces, len(carried)),
        grid=(total // row_tile, tiles),
        in_specs=[weight_spec(0), weight_spec(1), weight_spec(2)]
        + piece_specs * 2
        + [row_spec] * len(carried),
        out_specs=out_specs,
        out_shape=out_shape,
        scratch_shapes=[pltpu.VMEM((2, row_tile, width), BF16)] * 2
        + [pltpu.VMEM((row_tile, width), F32)] * 2
        + [pltpu.SemaphoreType.DMA((2, 3))] * 2,
        compiler_params=params(60, ("arbitrary", "arbitrary")),
        cost_estimate=cost(4 * total * width * cols, 2 * width * cols * (total // row_tile) + 12 * total * width),
        name="feed_forward",
    )(weights, weights, weights, *h2, *gy, *carried)
    return (outs[: len(outs) // 2], outs[len(outs) // 2 :]) if split else outs


def gather_first(rows, size):
    if size != 4:
        return (lax.all_gather(rows, "fsdp", axis=0, tiled=True),)
    return rows, by_x(rows), by_y(rows)


def gather_second(*first):
    if len(first) == 1:
        return first
    rows, from_x, from_y = first
    half = rows.shape[1] // 2
    return rows, from_x, from_y, by_x(from_y[:, :half]), by_y(from_x[:, half:])


def scatter_first(*parts, size):
    if size != 4:
        (part,) = parts
        part = part.reshape(size, part.shape[0] // size, part.shape[1])
        return (lax.all_to_all(part, "fsdp", split_axis=0, concat_axis=0, tiled=True),)
    send_x, keep_x, send_y, keep_y = parts
    return keep_x, keep_y, by_x(send_x), by_y(send_y)


def pass_on_kernel(keep_x, from_x, keep_y, from_y, a_ref, b_ref):
    a_ref[...] = (keep_x[...].astype(F32) + from_x[...].astype(F32)).astype(BF16)
    b_ref[...] = (keep_y[...].astype(F32) + from_y[...].astype(F32)).astype(BF16)


def scatter_second(*first):
    if len(first) == 1:
        return [jnp.sum(first[0].astype(F32), axis=0)]
    keep_x, keep_y, from_x, from_y = first
    _, count, half = keep_x.shape
    second = pl.BlockSpec((None, count, half), lambda _: (1, 0, 0))
    a_pass, b_pass = pl.pallas_call(
        pass_on_kernel,
        grid=(1,),
        in_specs=[second] * 4,
        out_specs=[pl.BlockSpec((count, half), lambda _: (0, 0))] * 2,
        out_shape=[jax.ShapeDtypeStruct((count, half), BF16)] * 2,
        compiler_params=params(60),
        name="pass_on",
    )(keep_x, from_x, keep_y, from_y)
    return [keep_x, keep_y, from_x, by_y(a_pass), from_y, by_x(b_pass)]


def term_specs(terms, row_tile, width):
    full = pl.BlockSpec((row_tile, width), lambda r: (r, 0))
    if len(terms) == 1:
        return [full]
    half = width // 2
    row = pl.BlockSpec((row_tile, half), lambda r: (r, 0))
    first = pl.BlockSpec((1, row_tile, half), lambda r: (0, r, 0))
    return [first, first, first, row, first, row]


def pair_swap(part):
    return lax.ppermute(part, "dp", [(i, i ^ 1) for i in range(lax.axis_size("dp"))])


def columns_share(block, size, group):
    half = block.shape[0] // 2
    return block if size != 4 else lax.dynamic_slice_in_dim(block, group % 2 * half, half, 0)


def columns_first(mine, size):
    if size != 4:
        return (lax.all_gather(mine, "fsdp", axis=0, tiled=False),)
    return by_x(mine), by_y(mine)


def columns_second(*first):
    if len(first) == 1:
        return first
    from_x, from_y = first
    share = from_x.shape[0] // 2
    return (
        from_x, from_y, by_x(from_y[:share]), by_y(from_x[share:]),
        pair_swap(from_x), pair_swap(from_y),
    )


def columns_third(block, *second):
    if len(second) == 1:
        return [second[0][f] for f in range(second[0].shape[0])]
    from_x, from_y, diagonal_x, diagonal_y, other_x, other_y = second
    return [
        block, from_x, from_y, diagonal_x, diagonal_y,
        other_x, other_y, pair_swap(diagonal_x), pair_swap(diagonal_y),
    ]


def assembled(pieces, group, shard):
    if len(pieces) != 9:
        return jnp.stack(pieces)
    block = pieces[0]
    half = block.shape[0] // 2
    core = group % 2
    out = jnp.zeros((4,) + block.shape, block.dtype)

    def put(out, part, f, at):
        return lax.dynamic_update_slice(out, part[None], (f, at, 0, 0))

    out = put(out, block, shard, 0)
    masks = ((1, 0), (2, 0), (3, 0), (3, half // 2))
    for side, at in ((pieces[1:5], core * half), (pieces[5:], (1 - core) * half)):
        for part, (mask, offset) in zip(side, masks):
            out = put(out, part, shard ^ mask, at + offset)
    return out


def shifted(array, size, direction):
    moved = []
    for step in range(2, size):
        if direction > 0:
            perm = [(i, i + step) for i in range(size - step)]
        else:
            perm = [(i + step, i) for i in range(size - step)]
        moved.append(lax.ppermute(array, "fsdp", perm))
    return moved


def deal_out(rows):
    count, width = rows.shape
    groups = lax.axis_size("dp")
    pieces = rows.reshape(groups, count // groups, width)
    return lax.all_to_all(pieces, "dp", split_axis=0, concat_axis=0, tiled=True)


def reorder_kernel(at_ref, in_ref, out_ref):
    for j in range(out_ref.shape[0]):
        out_ref[j] = in_ref[at_ref[j]]


def reordered(spread, order):
    return pl.pallas_call(
        reorder_kernel,
        in_specs=[pl.BlockSpec(memory_space=pltpu.SMEM), pl.BlockSpec(memory_space=pltpu.VMEM)],
        out_specs=pl.BlockSpec(memory_space=pltpu.VMEM),
        out_shape=jax.ShapeDtypeStruct(spread.shape, spread.dtype),
        compiler_params=pltpu.CompilerParams(vmem_limit_bytes=60 * MIB),
        name="reorder",
    )(order, spread)


def deal_in(ordered):
    groups, share, width = ordered.shape
    settled = lax.all_to_all(ordered, "dp", split_axis=0, concat_axis=0, tiled=True)
    return settled.reshape(groups * share, width)


def halved(table):
    n_dp, n_f = lax.axis_size("dp"), lax.axis_size("fsdp")
    dp_bits, f_bits = n_dp.bit_length() - 1, n_f.bit_length() - 1
    bits = [("dp", b) for b in range(dp_bits)][::-1] + [("fsdp", b) for b in range(f_bits)][::-1]
    left = table.reshape((2,) * len(bits) + table.shape[1:])
    order = [("dp", 0)] + [("fsdp", b) for b in range(f_bits)] + [("dp", b) for b in range(1, dp_bits)]
    for axis, bit in order:
        at = bits.index((axis, bit))
        bits.pop(at)
        mine = (lax.axis_index(axis) >> bit) & 1
        keep = lax.dynamic_index_in_dim(left, mine, at, keepdims=False)
        send = lax.dynamic_index_in_dim(left, 1 - mine, at, keepdims=False).astype(BF16)
        perm = [(i, i ^ (1 << bit)) for i in range(lax.axis_size(axis))]
        left = keep + lax.ppermute(send, axis, perm).astype(F32)
    return left


def shards(
    inputs, cotangent, lengths, dealing, wq, wk, wv, wo, wg, wu, wd,
    down_ad, up_qo, up_kv, fmap_q, fmap_k, gains,
):
    n_dp = lax.axis_size("dp")
    n_f = lax.axis_size("fsdp")
    group = lax.axis_index("dp")
    quarter = lax.axis_index("fsdp")
    micro, rows, width = inputs.shape[1:]
    total = micro * rows
    depth = wq.shape[0]
    q_cols, k_cols = wq.shape[1], wk.shape[1]
    kv_heads = k_cols // HEAD_SIZE
    heads = q_cols // HEAD_SIZE
    halves = wo.shape[0] // depth
    n_all = n_dp * n_f
    x = inputs[0].reshape(total, width)

    small_parts = [down_ad, up_qo, up_kv, fmap_q, fmap_k, gains]
    flat = jnp.concatenate([part.reshape(-1) for part in small_parts])
    small_rows = -(-flat.shape[0] // (16 * 128)) * 16
    flat = jnp.pad(flat, (0, small_rows * 128 - flat.shape[0])).reshape(1, small_rows, 128)
    small = lax.all_gather(flat.reshape(small_rows, 128), "dp", axis=0, tiled=False)
    small = lax.all_gather(small, "fsdp", axis=0, tiled=False)
    small = small.transpose(1, 0, 2, 3).reshape(n_all, small_rows * 128)
    at = 0
    fetched = []
    for part in small_parts:
        fetched.append(
            small[:, at : at + part.size].reshape((n_all * part.shape[0],) + part.shape[1:])
        )
        at += part.size
    down_ad, up_qo, up_kv, fmap_q, fmap_k, gains = fetched

    pack_cols = q_cols + 2 * k_cols
    w_qkv, w_out = pl.pallas_call(
        pack_attention_kernel,
        out_shape=[
            jax.ShapeDtypeStruct((depth, pack_cols), BF16),
            jax.ShapeDtypeStruct((depth, q_cols), BF16),
        ],
        compiler_params=pltpu.CompilerParams(vmem_limit_bytes=60 * MIB),
        name="pack_attention",
    )(wq, wk, wv, wo)
    w_qkv = lax.all_gather(w_qkv, "dp", axis=0, tiled=False)
    w_out = lax.all_gather(w_out, "dp", axis=0, tiled=False)
    near, spread = together(
        (functools.partial(columns_first, size=n_f), columns_share(w_qkv, n_f, group)),
        (deal_out, after(cotangent[0].reshape(total, width), small)),
    )
    share_micro = group * (total // n_dp) // rows
    order = lax.dynamic_index_in_dim(dealing, share_micro, 0, keepdims=False)

    gain_one = gains[:, 0].astype(F32)
    gain_two = gains[:, 1].astype(F32)

    hidden = wg.shape[1]
    tile = hidden // 4
    cuts = (0, 3 * tile, hidden)
    w_ffn = pl.pallas_call(
        functools.partial(pack_ffn_kernel, cuts),
        out_shape=[
            jax.ShapeDtypeStruct((depth, 3 * (stop - start)), BF16)
            for start, stop in zip(cuts, cuts[1:])
        ],
        compiler_params=pltpu.CompilerParams(vmem_limit_bytes=60 * MIB),
        name="pack_feed_forward",
    )(wg, wu, wd)
    positions = quarter * rows + jnp.arange(rows, dtype=jnp.int32)
    seq_len = lax.dynamic_index_in_dim(lengths, group, 0, keepdims=False)
    valid = (positions[None, :] < seq_len[:, None]).reshape(total, 1)

    xf = x.astype(F32)
    r1 = lax.rsqrt(jnp.mean(xf * xf, axis=-1, keepdims=True) + EPSILON)
    h1 = (xf * r1 * gain_one).astype(BF16)
    rank = ADAPTER_RANK
    lanes = RANK_LANES
    a_qkv = jnp.pad(down_ad[:, : 3 * rank], ((0, 0), (0, lanes - 3 * rank)))
    a_o = jnp.pad(down_ad[:, 3 * rank :], ((0, 0), (0, lanes - rank)))
    u = dot(h1, a_qkv).astype(BF16)
    b_q = up_qo[:, :rank].reshape(n_f, q_cols, rank)
    b_k = up_kv[:, :rank].reshape(n_f, k_cols, rank)
    b_v = up_kv[:, rank:].reshape(n_f, k_cols, rank)
    b_o = jnp.pad(up_qo[:, rank:], ((0, 0), (0, lanes - rank)))

    def placed(block, at):
        return jnp.pad(block.transpose(0, 2, 1), ((0, 0), (at, lanes - at - rank), (0, 0)))

    b_q_t = placed(b_q, 0)
    b_kv_t = jnp.concatenate([placed(b_k, rank), placed(b_v, 2 * rank)], axis=2)
    fq = fmap_q.reshape(H, HEAD_SIZE, HEAD_SIZE)
    fk = fmap_k.reshape(KEY_VALUE_HEADS, HEAD_SIZE, HEAD_SIZE)
    fq_t = jnp.concatenate([fq.transpose(0, 2, 1), -fq.transpose(0, 2, 1)], axis=1)
    fk_t = jnp.concatenate([fk.transpose(0, 2, 1), -fk.transpose(0, 2, 1)], axis=1)
    cos_t, sin_t = rope_tables_t(jnp.tile(positions, micro))
    pairs = rows // 128
    prepared = (h1, u, a_qkv, a_o, b_q_t, b_kv_t, b_o, fq, fk, fq_t, fk_t, cos_t, sin_t)
    inverse = jnp.argsort(dealing, axis=1).astype(jnp.int32)
    prepared += (inverse,)
    second, out_near, cot, prepared = together(
        (columns_second, *near),
        (functools.partial(columns_first, size=n_f), columns_share(w_out, n_f, group)),
        (lambda spread, order: deal_in(reordered(spread, order)), spread, order),
        (lambda *arrays: arrays, *prepared),
    )
    h1, u, a_qkv, a_o, b_q_t, b_kv_t, b_o, fq, fk, fq_t, fk_t, cos_t, sin_t, inverse = prepared
    fetched_ffn = [lax.all_gather(after(w_ffn[0], cot), "dp", axis=0, tiled=False)]
    (qkv_pieces,) = together((columns_third, w_qkv, *second))

    place = jnp.stack([quarter, group % 2]).astype(jnp.int32)
    smem = pl.BlockSpec(memory_space=pltpu.SMEM)
    vmem = pl.BlockSpec(memory_space=pltpu.VMEM)

    def columns(pieces, size, at):
        return [
            pl.BlockSpec(part.shape[:2] + (size,), lambda _: (0, 0, at), pipeline_mode=pl.Buffered(1))
            for part in pieces
        ]

    def key_values(h1, u, *pieces):
        return pl.pallas_call(
            functools.partial(kv_kernel, kv_heads, micro, depth, n_dp),
            grid=(1,),
            in_specs=[smem] + [vmem] * 6 + columns(pieces, 2 * k_cols, q_cols // (2 * k_cols)),
            out_specs=[vmem] * 3,
            out_shape=[
                jax.ShapeDtypeStruct((KEY_VALUE_HEADS, micro, rows, 256), BF16),
                jax.ShapeDtypeStruct((KEY_VALUE_HEADS, micro, AUG, 128), BF16),
                jax.ShapeDtypeStruct((KEY_VALUE_HEADS, micro, 112, 256), BF16),
            ],
            compiler_params=params(40),
            cost_estimate=cost(4 * total * width * k_cols * n_f, 2 * (total * width + 2 * width * k_cols * n_f), 128 * 8 * total),
            name="key_value",
        )(place, h1, u, b_kv_t, cos_t, sin_t, fk_t, *pieces)

    def queries(h1, u, *pieces):
        return pl.pallas_call(
            functools.partial(q_kernel, heads, depth, n_dp),
            grid=(1,),
            in_specs=[smem] + [vmem] * 6 + columns(pieces, q_cols, 0),
            out_specs=[vmem, vmem],
            out_shape=[
                jax.ShapeDtypeStruct((H * 64, total), BF16),
                jax.ShapeDtypeStruct((H * 128, total), BF16),
            ],
            compiler_params=params(40),
            cost_estimate=cost(2 * total * width * q_cols * n_f, 2 * (total * width + width * q_cols * n_f + 3 * total * 2048), 128 * 32 * total),
            name="query",
        )(place, h1, u, b_q_t, cos_t, sin_t, fq_t, *pieces)

    forward_one = [(i, i + 1) for i in range(n_f - 1)]
    backward_one = [(i + 1, i) for i in range(n_f - 1)]

    gy_both = jnp.where(valid, cot, jnp.zeros_like(cot))
    gy = [gy_both[m * rows : (m + 1) * rows] for m in range(micro)]
    gather = functools.partial(gather_first, size=n_f)
    (kv_natural, totals, message), out_second = together(
        (key_values, h1, u, *qkv_pieces), (columns_second, *out_near)
    )

    def send_on(message, totals):
        return lax.ppermute(message, "fsdp", forward_one), shifted(totals, n_f, 1)

    (q_rot, q_feat), (message, bases) = together(
        (queries, h1, u, *qkv_pieces), (send_on, message, totals)
    )
    part = after(w_ffn[1], q_rot)
    fetched_ffn.append(lax.all_gather(part, "dp", axis=0, tiled=False))
    w_ffn = fetched_ffn

    has_prev = (quarter > 0).astype(jnp.int32).reshape(1)
    g4 = REPEAT * 64
    prev_spec = smem
    n_spec = pl.BlockSpec((1, micro, rows, 256), lambda g: (g, 0, 0, 0))
    message_spec = pl.BlockSpec((1, micro, 112, 256), lambda g: (g, 0, 0, 0))
    back_spec = pl.BlockSpec((1, micro, 64 + AUG, 256), lambda g: (g, 0, 0, 0))
    state_spec = pl.BlockSpec((1, micro, pairs, 2 * AUG, 128), lambda g: (g, 0, 0, 0, 0))
    head_spec = pl.BlockSpec((g4, total), lambda g: (g, 0))
    feat_spec = pl.BlockSpec((2 * g4, total), lambda g: (g, 0))
    den_spec = pl.BlockSpec((1, 8, total), lambda g: (g, 0, 0))
    base_spec = pl.BlockSpec((1, micro, AUG, 128), lambda g: (g, 0, 0, 0))
    attend_flops = H * total * 2 * (192 * 64 + 128 * 128 + 160 * 128 + 192 * 64)
    attend = pl.pallas_call(
        functools.partial(attend_kernel, micro),
        grid=(KEY_VALUE_HEADS,),
        in_specs=[
            prev_spec,
            n_spec,
            message_spec,
            head_spec,
            feat_spec,
        ]
        + [base_spec] * (n_f - 2),
        out_specs=[pl.BlockSpec((total, g4), lambda g: (0, g)), head_spec, den_spec, state_spec],
        out_shape=[
            jax.ShapeDtypeStruct((total, H * 64), BF16),
            jax.ShapeDtypeStruct((H * 64, total), BF16),
            jax.ShapeDtypeStruct((KEY_VALUE_HEADS, 8, total), F32),
            jax.ShapeDtypeStruct((KEY_VALUE_HEADS, micro, pairs, 2 * AUG, 128), BF16),
        ],
        compiler_params=params(40),
        cost_estimate=cost(attend_flops, 14 * MIB, 128 * H * total),
        name="attend",
    )
    (o, o_t, den, states), gy_first, out_pieces = together(
        (attend, has_prev, kv_natural, message, q_rot, q_feat, *bases),
        (gather, gy[0]),
        (columns_third, w_out, *out_second),
    )
    project_out = pl.pallas_call(
        functools.partial(out_kernel, depth, n_dp),
        grid=(1,),
        in_specs=[smem] + [vmem] * 5 + columns(out_pieces, q_cols, 0),
        out_specs=[vmem] * 4,
        out_shape=[
            jax.ShapeDtypeStruct((total, width), F32),
            jax.ShapeDtypeStruct((total, width), BF16),
            jax.ShapeDtypeStruct((total, lanes), BF16),
            jax.ShapeDtypeStruct((total, 1), F32),
        ],
        scratch_shapes=[pltpu.VMEM((n_dp, total, depth), F32)],
        compiler_params=params(40),
        cost_estimate=cost(2 * total * width * H * 64, 20 * MIB),
        name="output_projection",
    )
    (x2, h2, uo, r2), gy_zero = together(
        (project_out, place, o, a_o, b_o, x, gain_two.reshape(1, width), *out_pieces),
        (gather_second, *gy_first),
    )
    gather = functools.partial(gather_first, size=n_f)

    def assemble(*pieces):
        return assembled(pieces, group, quarter)

    h2_first, w_qkv = together((gather, h2[:rows]), (assemble, *qkv_pieces))
    (h2_zero,) = together((gather_second, *h2_first))

    def piece(array, m):
        return array[m * rows : (m + 1) * rows]

    row_tile = min(128, rows)

    def finish(m, terms):
        return pl.pallas_call(
            functools.partial(result_kernel, len(terms)),
            grid=(rows // row_tile,),
            in_specs=[
                pl.BlockSpec((row_tile, width), lambda r: (m * (rows // row_tile) + r, 0)),
                pl.BlockSpec((row_tile, 1), lambda r: (m * (rows // row_tile) + r, 0)),
            ]
            + term_specs(terms, row_tile, width),
            out_specs=pl.BlockSpec((row_tile, width), lambda r: (r, 0)),
            out_shape=jax.ShapeDtypeStruct((rows, width), BF16),
            compiler_params=params(40),
            cost_estimate=cost(4 * rows * width, 10 * rows * width),
            name="result",
        )(x2, valid_rows, *terms)

    def mid_back(m, terms, gy, *whole_arrays):
        here = pl.BlockSpec((row_tile, width), lambda r: (m * (rows // row_tile) + r, 0))
        thin = pl.BlockSpec((row_tile, lanes), lambda r: (m * (rows // row_tile) + r, 0))
        count = 6 + len(terms)
        return pl.pallas_call(
            functools.partial(mid_back_kernel, len(terms)),
            grid=(rows // row_tile,),
            in_specs=[
                here,
                pl.BlockSpec((row_tile, 1), lambda r: (m * (rows // row_tile) + r, 0)),
                whole((1, width)),
                pl.BlockSpec((row_tile, width), lambda r: (r, 0)),
                thin,
                whole((width, lanes)),
            ]
            + term_specs(terms, row_tile, width)
            + [pl.BlockSpec(memory_space=pl.ANY)] * len(whole_arrays),
            out_specs=[here, here, thin, whole((1, width)), whole((16, width))],
            out_shape=[
                jax.ShapeDtypeStruct((total, width), F32),
                jax.ShapeDtypeStruct((total, width), BF16),
                jax.ShapeDtypeStruct((total, lanes), BF16),
                jax.ShapeDtypeStruct((1, width), F32),
                jax.ShapeDtypeStruct((16, width), F32),
            ],
            input_output_aliases={count + i: i for i in range(len(whole_arrays))},
            compiler_params=params(40),
            cost_estimate=cost(20 * rows * width, 16 * rows * width),
            name="mid_back",
        )(x2, r2, gain_two.reshape(1, width), gy, uo, b_o, *terms, *whole_arrays)

    valid_rows = valid.astype(jnp.int32)
    def feed(split):
        def run(h2, gy, *carried):
            return ffn(tile, split, h2, gy, w_ffn[1 if split else 0], *carried)

        return run

    scatter = functools.partial(scatter_first, size=n_f)
    head_zero, h2_first, gy_first = together(
        (feed(False), h2_zero, gy_zero), (gather, h2[rows:]), (gather, gy[1])
    )
    (down_zero, gh_zero), h2_one, gy_one = together(
        (feed(True), h2_zero, gy_zero, *head_zero),
        (gather_second, *h2_first),
        (gather_second, *gy_first),
    )
    head_one, gh_zero_terms, down_zero_terms = together(
        (feed(False), h2_one, gy_one), (scatter, *gh_zero), (scatter, *down_zero)
    )
    (down_one, gh_one), gh_zero_terms, down_zero_terms = together(
        (feed(True), h2_one, gy_one, *head_one),
        (scatter_second, *gh_zero_terms),
        (scatter_second, *down_zero_terms),
    )

    go_back = pl.pallas_call(
        functools.partial(go_kernel, depth),
        grid=(n_f,),
        in_specs=[
            whole((total, width)),
            pl.BlockSpec((1, n_dp, depth, q_cols), lambda f: (f, 0, 0, 0)),
            pl.BlockSpec((q_cols, lanes), lambda f: (f, 0)),
            whole((total, lanes)),
            pl.BlockSpec((total, q_cols), lambda f: (0, f)),
        ],
        out_specs=[
            pl.BlockSpec((q_cols, total), lambda f: (f, 0)),
            pl.BlockSpec((16, q_cols), lambda f: (0, f)),
        ],
        out_shape=[
            jax.ShapeDtypeStruct((H * 64, total), BF16),
            jax.ShapeDtypeStruct((16, H * 64), F32),
        ],
        compiler_params=params(60),
        cost_estimate=cost(2 * total * width * H * 64, 12 * MIB),
        name="output_projection_back",
    )

    attend_back = pl.pallas_call(
        functools.partial(attend_back_kernel, micro),
        grid=(KEY_VALUE_HEADS,),
        in_specs=[
            prev_spec,
            n_spec,
            message_spec,
            state_spec,
            head_spec,
            feat_spec,
            head_spec,
            head_spec,
            den_spec,
            pl.BlockSpec((REPEAT, 64, 64), lambda g: (g, 0, 0)),
            whole((32, total)),
            whole((32, total)),
        ],
        out_specs=[
            pl.BlockSpec((1, total, g4), lambda g: (g * g4 // q_cols, 0, g % (q_cols // g4))),
            pl.BlockSpec((1, g4, 64), lambda g: (g, 0, 0)),
            n_spec,
            state_spec,
            back_spec,
            base_spec,
        ],
        out_shape=[
            jax.ShapeDtypeStruct((n_f, total, q_cols), BF16),
            jax.ShapeDtypeStruct((KEY_VALUE_HEADS, g4, 64), F32),
            jax.ShapeDtypeStruct((KEY_VALUE_HEADS, micro, rows, 256), F32),
            jax.ShapeDtypeStruct((KEY_VALUE_HEADS, micro, pairs, 2 * AUG, 128), F32),
            jax.ShapeDtypeStruct((KEY_VALUE_HEADS, micro, 64 + AUG, 256), BF16),
            jax.ShapeDtypeStruct((KEY_VALUE_HEADS, micro, AUG, 128), BF16),
        ],
        scratch_shapes=[pltpu.VMEM((g4, total), F32), pltpu.VMEM((g4, total), BF16)],
        compiler_params=params(60),
        cost_estimate=cost(3 * attend_flops, 24 * MIB, 128 * H * total),
        name="attend_back",
    )
    gh_one_terms, zero, result_zero, w_out = together(
        (scatter, *gh_one),
        (functools.partial(mid_back, 0), gh_zero_terms, gy[0]),
        (functools.partial(finish, 0), down_zero_terms),
        (assemble, *out_pieces),
    )
    (gh_one_terms,) = together((scatter_second, *gh_one_terms))

    def norm_to_output(gh_one, gy_one, *zero):
        gx2, gb, guo, *one = mid_back(1, gh_one, gy_one, *zero[:3])
        go_t, d_ao_t = go_back(gb, w_out, a_o, guo, o)
        return gx2, go_t, d_ao_t, zero[3] + one[0], zero[4] + one[1]

    (gx2, go_t, d_ao_t, dg2, d_bo_t), down_one_terms = together(
        (norm_to_output, gh_one_terms, gy[1], *zero), (scatter, *down_one)
    )
    back, down_one_terms, spread_zero = together(
        (attend_back, has_prev, kv_natural, message, states, q_rot, q_feat, go_t, o_t, den, fq, cos_t, sin_t),
        (scatter_second, *down_one_terms),
        (deal_out, result_zero),
    )
    gq, d_fq, g_keys, g_states, g_message, g_total = back

    query_part = pl.pallas_call(
        functools.partial(gx_query_kernel, n_f),
        grid=(n_dp,),
        in_specs=[
            whole((n_f, total, q_cols)),
            pl.BlockSpec((n_f, 1, depth, q_cols), lambda j: (0, j, 0, 0)),
            whole((total, lanes)),
            whole((n_f, lanes, q_cols)),
        ],
        out_specs=[
            pl.BlockSpec((total, depth), lambda j: (0, j)),
            whole((total, lanes)),
            whole((32, H * 64)),
        ],
        out_shape=[
            jax.ShapeDtypeStruct((total, width), F32),
            jax.ShapeDtypeStruct((total, lanes), F32),
            jax.ShapeDtypeStruct((32, H * 64), F32),
        ],
        compiler_params=params(60),
        cost_estimate=cost(2 * total * width * 2048, 16 * MIB),
        name="query_input_gradient",
    )

    def exchange(g_message, g_total):
        return lax.ppermute(g_message, "fsdp", backward_one), shifted(g_total, n_f, -1)

    (gh_q, gu_q, d_bq_t), (g_message, g_next), out_zero, result_one = together(
        (query_part, gq, w_qkv, u, b_q_t),
        (exchange, g_message, g_total),
        (lambda spread, order: deal_in(reordered(spread, order)), spread_zero, inverse[0]),
        (functools.partial(finish, 1), down_one_terms),
    )

    next_spec = pl.BlockSpec((kv_heads, micro, AUG, 128), lambda f: (f, 0, 0, 0))
    kv_back = pl.pallas_call(
        functools.partial(kv_back_kernel, kv_heads, micro),
        grid=(n_f,),
        in_specs=[
            pl.BlockSpec((kv_heads, micro, rows, 256), lambda f: (f, 0, 0, 0)),
            pl.BlockSpec((kv_heads, micro, 64 + AUG, 256), lambda f: (f, 0, 0, 0)),
            pl.BlockSpec((kv_heads, micro, rows, 256), lambda f: (f, 0, 0, 0)),
            pl.BlockSpec((kv_heads, micro, pairs, 2 * AUG, 128), lambda f: (f, 0, 0, 0, 0)),
            pl.BlockSpec((kv_heads, 64, 64), lambda f: (f, 0, 0)),
            whole((32, total)),
            whole((32, total)),
            whole((total, lanes)),
            pl.BlockSpec((1, lanes, 2 * k_cols), lambda f: (f, 0, 0)),
            whole((total, lanes)),
            whole((total, width)),
        ]
        + [next_spec] * (n_f - 2),
        out_specs=[
            pl.BlockSpec((1, total, 2 * k_cols), lambda f: (f, 0, 0)),
            pl.BlockSpec((1, k_cols, 64), lambda f: (f, 0, 0)),
            whole((total, lanes)),
            pl.BlockSpec((None, 32, 2 * k_cols), lambda f: (f, 0, 0)),
            whole((32, width)),
        ],
        out_shape=[
            jax.ShapeDtypeStruct((n_f, total, 2 * k_cols), BF16),
            jax.ShapeDtypeStruct((n_f, k_cols, 64), F32),
            jax.ShapeDtypeStruct((total, lanes), BF16),
            jax.ShapeDtypeStruct((n_f, 32, 2 * k_cols), F32),
            jax.ShapeDtypeStruct((32, width), F32),
        ],
        scratch_shapes=[pltpu.VMEM((total, lanes), F32)],
        compiler_params=params(60),
        cost_estimate=cost(8 * total * 128 * 128, 8 * MIB),
        name="key_value_back",
    )
    input_back = pl.pallas_call(
        functools.partial(gx_kernel, n_f, depth),
        grid=(n_dp,),
        in_specs=[
            pl.BlockSpec((total, depth), lambda j: (0, j)),
            whole((n_f, total, 2 * k_cols)),
            pl.BlockSpec((n_f, 1, depth, 2 * k_cols), lambda j: (0, j, 0, q_cols // (2 * k_cols))),
            whole((total, lanes)),
            pl.BlockSpec((depth, lanes), lambda j: (j, 0)),
            pl.BlockSpec((total, depth), lambda j: (0, j)),
            whole((total, width)),
            whole((total, width)),
            whole((total, 1)),
            whole((n_dp, 1, depth)),
        ],
        out_specs=[whole((total, width)), pl.BlockSpec((1, depth), lambda j: (0, j))],
        out_shape=[
            jax.ShapeDtypeStruct((total, width), BF16),
            jax.ShapeDtypeStruct((1, width), F32),
        ],
        scratch_shapes=[pltpu.VMEM((n_dp, total, depth), F32), pltpu.VMEM((total, 1), F32)],
        compiler_params=params(60),
        cost_estimate=cost(2 * total * width * 1024, 30 * MIB),
        name="input_gradient",
    )
    def heads_to_input(g_keys, g_message, g_next, gu_q, gh_q):
        gkv, d_fk, gu, d_bkv_t, d_qkv_t = kv_back(
            g_keys, g_message, kv_natural, g_states, fk, cos_t, sin_t, u, b_kv_t, gu_q, h1,
            *g_next,
        )
        gx, dg1 = input_back(
            gh_q, gkv, w_qkv, gu, a_qkv, x, x, gx2, r1, gain_one.reshape(n_dp, 1, depth)
        )
        return gx, dg1, d_fk, d_bkv_t, d_qkv_t

    (gx, dg1, d_fk, d_bkv_t, d_qkv_t), spread_one = together(
        (heads_to_input, g_keys, g_message, g_next, gu_q, gh_q),
        (deal_out, result_one),
    )

    wide = pl.pallas_call(
        table_kernel,
        out_shape=jax.ShapeDtypeStruct((width, lanes), F32),
        compiler_params=pltpu.CompilerParams(vmem_limit_bytes=60 * MIB),
        name="table",
    )(d_fq.reshape(H * 64, 64), d_qkv_t, d_ao_t, d_bq_t, d_bo_t, dg1, dg2)
    kv_rows = KEY_VALUE_HEADS * 64
    d_bk = d_bkv_t[:, rank : 2 * rank, :k_cols].transpose(0, 2, 1).reshape(kv_rows, rank)
    d_bv = d_bkv_t[:, 2 * rank : 3 * rank, k_cols:].transpose(0, 2, 1).reshape(kv_rows, rank)
    narrow = jnp.concatenate(
        [d_fk.reshape(kv_rows, 64), d_bk, d_bv, jnp.zeros((kv_rows, lanes - 80), F32)], axis=1
    )
    wide = wide.reshape(n_all, width // n_all, lanes)
    narrow = narrow.reshape(n_all, kv_rows // n_all, lanes)
    table = jnp.concatenate([wide, narrow], axis=1)
    table, out_one = together(
        (halved, table), (lambda spread, order: deal_in(reordered(spread, order)), spread_one, inverse[1])
    )
    output = [out_zero, out_one]
    wide, narrow = table[: width // n_all], table[width // n_all :]
    shares = (
        wide[:, 64:96],
        wide[:, 96:112],
        narrow[:, 64:80],
        wide[:, :64],
        narrow[:, :64],
        wide[:, 112:114],
    )
    return (jnp.stack(output)[None], gx.reshape(1, micro, rows, width), *shares)


def solution(mesh):
    every = ("dp", "fsdp")
    blocks = P("dp", None, "fsdp", None)
    in_specs = (
        blocks,
        blocks,
        P(),
        P(),
        P("dp", "fsdp"),
        P("dp", "fsdp"),
        P("dp", "fsdp"),
        P("fsdp", "dp"),
        P("dp", "fsdp"),
        P("dp", "fsdp"),
        P("fsdp", "dp"),
    ) + (P(every, None),) * 6
    out_specs = (blocks, blocks) + (P(every, None),) * 6
    return jax.shard_map(shards, mesh=mesh, in_specs=in_specs, out_specs=out_specs, check_vma=False)
```

```python
import functools
import math

import jax
import jax.numpy as jnp
from jax import lax
from jax.experimental import pallas as pl
from jax.experimental.pallas import tpu as pltpu
from jax.sharding import PartitionSpec as P

H = 32
KEY_VALUE_HEADS = 8
REPEAT = H // KEY_VALUE_HEADS
HEAD_SIZE = 64
ADAPTER_RANK = 8
WIN = 64
AUG = 80
RANK_LANES = 128

EPSILON = 1e-05
ROPE_BASE = 500000.0
F32 = jnp.float32
BF16 = jnp.bfloat16
MIB = 1024 * 1024
X_PAIRS = [(i, i ^ 1) for i in range(4)]
Y_PAIRS = [(i, i ^ 2) for i in range(4)]


def dot(a, b):
    return lax.dot_general(a, b, (((1,), (0,)), ((), ())), preferred_element_type=F32)


def dot_nt(a, b):
    return lax.dot_general(a, b, (((1,), (1,)), ((), ())), preferred_element_type=F32)


def params(mib, semantics=("arbitrary",)):
    return pltpu.CompilerParams(vmem_limit_bytes=mib * MIB, dimension_semantics=semantics)


def cost(flops, bytes_accessed, transcendentals=0):
    return pl.CostEstimate(
        flops=int(flops), bytes_accessed=int(bytes_accessed), transcendentals=int(transcendentals)
    )


def whole(shape):
    return pl.BlockSpec(shape, lambda *_: (0,) * len(shape))


def after(value, *others):
    return lax.optimization_barrier((value, *others))[0]


def together(*jobs):
    arguments = lax.optimization_barrier([job[1:] for job in jobs])
    return lax.optimization_barrier([job[0](*args) for job, args in zip(jobs, arguments)])


def by_x(rows):
    return lax.ppermute(rows, "fsdp", X_PAIRS)


def by_y(rows):
    return lax.ppermute(rows, "fsdp", Y_PAIRS)


def rope_tables_t(positions):
    half_size = HEAD_SIZE // 2
    frequencies = jnp.exp(
        -(2.0 * jnp.arange(half_size, dtype=F32) / HEAD_SIZE) * math.log(ROPE_BASE)
    )
    angles = frequencies[:, None] * positions.astype(F32)[None, :]
    return jnp.cos(angles), jnp.sin(angles)


def rotate_t(head, cos_t, sin_t):
    a, b = head[:32], head[32:]
    return jnp.concatenate([a * cos_t - b * sin_t, b * cos_t + a * sin_t], axis=0)


def rotate_back_t(head, cos_t, sin_t):
    a, b = head[:32], head[32:]
    return jnp.concatenate([a * cos_t + b * sin_t, b * cos_t - a * sin_t], axis=0)


def half_softmax_t(scores):
    e = jnp.exp(scores - jnp.max(scores, axis=0, keepdims=True))
    return e * (1.0 / jnp.sum(e, axis=0, keepdims=True))


def features_t(mapped):
    return jnp.concatenate([half_softmax_t(mapped[:64]), half_softmax_t(mapped[64:])], axis=0)


def features_back_t(e, f):
    ef = e * f
    t1 = jnp.sum(ef[:64], axis=0, keepdims=True)
    t2 = jnp.sum(ef[64:], axis=0, keepdims=True)
    return (ef[:64] - e[:64] * t1) - (ef[64:] - e[64:] * t2)


def block_pieces(refs, place_ref, n_dp):
    if len(refs) == 9:
        own, x_mine, y_mine, dx_mine, dy_mine, x_other, y_other, dx_other, dy_other = refs
        shard, core = place_ref[0], place_ref[1]
        half = n_dp // 2
        mine, other = core * half, (1 - core) * half
        quarter = half // 2
        return [
            (shard, [(own, 0)]),
            (shard ^ 1, [(x_mine, mine), (x_other, other)]),
            (shard ^ 2, [(y_mine, mine), (y_other, other)]),
            (
                shard ^ 3,
                [
                    (dx_mine, mine),
                    (dy_mine, mine + quarter),
                    (dx_other, other),
                    (dy_other, other + quarter),
                ],
            ),
        ]
    return [(f, [(ref, 0)]) for f, ref in enumerate(refs)]


def project(h1_ref, u_ref, pieces, low_rank, depth):
    total = dot(u_ref[...], low_rank)
    for ref, start in pieces:
        count = ref.shape[0] * depth
        if isinstance(start, int):
            columns = h1_ref[:, start * depth : start * depth + count]
        else:
            columns = h1_ref[:, pl.ds(pl.multiple_of(start * depth, depth), count)]
        total += dot(columns, ref[...].reshape(count, ref.shape[2]))
    return total


def kv_kernel(kv_heads, micro, depth, n_dp, place_ref, h1_ref, u_ref, b_ref, cos_ref, sin_ref,
              f_ref, *refs):
    *w_refs, n_ref, tot_ref, msg_ref = refs
    rows = h1_ref.shape[0] // micro
    cos_t, sin_t = cos_ref[...], sin_ref[...]
    width = kv_heads * HEAD_SIZE
    for f, pieces in block_pieces(w_refs, place_ref, n_dp):
        kv_t = project(h1_ref, u_ref, pieces, b_ref[f], depth).T
        for g in range(kv_heads):
            head = f * kv_heads + g
            kr = rotate_t(kv_t[g * 64 : (g + 1) * 64], cos_t, sin_t).astype(BF16)
            v = kv_t[width + g * 64 : width + (g + 1) * 64].astype(BF16)
            pk = features_t(dot(f_ref[head], kr)).astype(BF16)
            natural = (
                jnp.concatenate([pk.astype(F32), kr.astype(F32), v.astype(F32)], axis=0).T
            ).astype(BF16)
            v_aug = jnp.concatenate([v, jnp.ones((AUG - 64, v.shape[1]), BF16)], axis=0)
            for m in range(micro):
                part = natural[m * rows : (m + 1) * rows]
                n_ref[head, m] = part
                sums = dot(v_aug[:, m * rows : (m + 1) * rows], part[:, :128])
                tot_ref[head, m] = sums.astype(BF16)
                msg_ref[head, m, :64] = part[rows - 64 :]
                tail = jnp.concatenate([sums[48:], jnp.zeros((16, 128), F32)], axis=0)
                msg_ref[head, m, 64:] = jnp.concatenate([sums[:48], tail], axis=1).astype(BF16)


def q_kernel(heads, depth, n_dp, place_ref, h1_ref, u_ref, b_ref, cos_ref, sin_ref, f_ref, *refs):
    *w_refs, qr_ref, pq_ref = refs
    cos_t, sin_t = cos_ref[...], sin_ref[...]
    for f, pieces in block_pieces(w_refs, place_ref, n_dp):
        q_t = project(h1_ref, u_ref, pieces, b_ref[f], depth).T
        for h in range(heads):
            head = f * heads + h
            qr = rotate_t(q_t[h * 64 : (h + 1) * 64], cos_t, sin_t).astype(BF16)
            pq = features_t(dot(f_ref[head], qr)).astype(BF16)
            if isinstance(head, int):
                qr_ref[head * 64 : (head + 1) * 64] = qr
                pq_ref[head * 128 : (head + 1) * 128] = pq
            else:
                qr_ref[pl.ds(pl.multiple_of(head * 64, 64), 64)] = qr
                pq_ref[pl.ds(pl.multiple_of(head * 128, 128), 128)] = pq


def pair_masks(has_prev):
    lane = lax.broadcasted_iota(jnp.int32, (64, REPEAT * 128), 1)
    row = lax.broadcasted_iota(jnp.int32, (64, REPEAT * 128), 0)
    low = (lane % 128) < 64
    ahead = row - lane % 64
    value = jnp.where(low, ahead - 1, -ahead)
    hidden = jnp.where(low, (1 - has_prev) * 1024, 0)
    return low, value >= 0, value - hidden >= 0


def heads_side(ref, size, start):
    return jnp.concatenate(
        [ref[h * size : (h + 1) * size, start : start + 128] for h in range(REPEAT)], axis=1
    )


def attend_kernel(micro, prev_ref, n_ref, msg_ref, qr_ref, pq_ref, *refs):
    *base_refs, o_ref, ot_ref, den_ref, s_ref = refs
    rows = n_ref.shape[2]
    low, mask_a, mask_first = pair_masks(prev_ref[0])
    low_row = (lax.broadcasted_iota(jnp.int32, (1, REPEAT * 128), 1) % 128) < 64
    key_lane = lax.broadcasted_iota(jnp.int32, (AUG, 128), 1) < 64
    for m in range(micro):
        ext = jnp.concatenate([msg_ref[0, m, :64], n_ref[0, m]], axis=0)
        ext_t = ext.astype(F32).T.astype(BF16)
        near = jnp.concatenate([msg_ref[0, m, 64:112, :128], msg_ref[0, m, 64:96, 128:]], axis=0)
        v_aug_all = jnp.concatenate([ext_t[192:256], jnp.ones((AUG - 64, rows + WIN), BF16)], axis=0)
        running = near.astype(F32)
        for base_ref in base_refs:
            running += base_ref[0, m].astype(F32)
        for p in range(rows // 128):
            start = m * rows + p * 128
            r0 = p * 128
            qr4 = heads_side(qr_ref, 64, start)
            pq4 = heads_side(pq_ref, 128, start)
            pk = ext[r0 : r0 + 128, :128]
            kr = ext[r0 : r0 + 192, 128:192]
            v_aug = v_aug_all[:, r0 : r0 + 128]
            zero = jnp.zeros_like(v_aug)
            spans = dot(
                jnp.concatenate(
                    [jnp.where(key_lane, v_aug, zero), jnp.where(key_lane, zero, v_aug)], axis=0
                ),
                pk,
            )
            if p == 0:
                running = running - spans[:AUG]
            state = jnp.concatenate([running, running + spans[:AUG]], axis=0).astype(BF16)
            running = running + spans[:AUG] + spans[AUG:]
            s_ref[0, m, p] = state
            from_state = dot(state, pq4)
            scores = dot(kr, qr4) * (1.0 / math.sqrt(HEAD_SIZE))
            linear = dot(pk, pq4)
            exp_a = jnp.exp(jnp.where(low, scores[:64], scores[128:]))
            exp_b = jnp.exp(scores[64:128])
            mask = mask_first if p == 0 else mask_a
            w_a = jnp.where(mask, exp_a, jnp.where(low, linear[:64], 0.0))
            w_b = jnp.where(mask_a, jnp.where(low, 0.0, linear[64:]), exp_b)
            den = (
                jnp.sum(w_a, axis=0, keepdims=True)
                + jnp.sum(w_b, axis=0, keepdims=True)
                + jnp.where(low_row, from_state[64:65], from_state[AUG + 64 : AUG + 65])
            )
            inv = 1.0 / den
            p_a = w_a * inv
            weights = jnp.concatenate(
                [jnp.where(low, p_a, 0.0), w_b * inv, jnp.where(low, 0.0, p_a)], axis=0
            ).astype(BF16)
            out = (
                dot(ext_t[192:256, r0 : r0 + 192], weights)
                + jnp.where(low, from_state[:64], from_state[AUG : AUG + 64]) * inv
            )
            for h in range(REPEAT):
                den_ref[0, h : h + 1, start : start + 128] = den[:, h * 128 : (h + 1) * 128]
            out_t = jnp.concatenate(
                [out[:, h * 128 : (h + 1) * 128] for h in range(REPEAT)], axis=0
            )
            ot_ref[:, start : start + 128] = out_t.astype(BF16)
            o_ref[start : start + 128, :] = out_t.T.astype(BF16)


def attend_back_kernel(micro, prev_ref, n_ref, msg_ref, s_ref, qr_ref, pq_ref, go_ref, ot_ref,
                       den_ref, f_ref, cos_ref, sin_ref,
                       gq_ref, df_ref, gn_ref, gs_ref, back_ref, total_ref,
                       gqr_ref, gmq_ref):
    rows = n_ref.shape[2]
    low, mask_a, mask_first = pair_masks(prev_ref[0])
    low_aug = (lax.broadcasted_iota(jnp.int32, (AUG, REPEAT * 128), 1) % 128) < 64
    low_feat = (lax.broadcasted_iota(jnp.int32, (128, REPEAT * 128), 1) % 128) < 64
    scale = 1.0 / math.sqrt(HEAD_SIZE)
    for m in range(micro):
        ext = jnp.concatenate([msg_ref[0, m, :64], n_ref[0, m]], axis=0)
        ext_t = ext.astype(F32).T.astype(BF16)
        tail = g_sum = None
        for p in range(rows // 128):
            start = m * rows + p * 128
            r0 = p * 128
            qr4 = heads_side(qr_ref, 64, start)
            pq4 = heads_side(pq_ref, 128, start)
            go4 = heads_side(go_ref, 64, start)
            o4 = heads_side(ot_ref, 64, start)
            den = jnp.concatenate(
                [den_ref[0, h : h + 1, start : start + 128] for h in range(REPEAT)], axis=1
            )
            inv = 1.0 / den
            pk = ext[r0 : r0 + 128, :128]
            kr = ext[r0 : r0 + 192, 128:192]
            v = ext[r0 : r0 + 192, 192:256]
            go_f = go4.astype(F32)
            delta = jnp.sum(go_f * o4.astype(F32), axis=0, keepdims=True)
            scores = dot(kr, qr4) * scale
            linear = dot(pk, pq4)
            g_p = dot(v, go4)
            mask = mask_first if p == 0 else mask_a
            exp_a = jnp.exp(jnp.where(low, scores[:64], scores[128:]))
            exp_b = jnp.exp(scores[64:128])
            p_a = jnp.where(mask, exp_a, jnp.where(low, linear[:64], 0.0)) * inv
            p_b = jnp.where(mask_a, jnp.where(low, 0.0, linear[64:]), exp_b) * inv
            weights = jnp.concatenate(
                [jnp.where(low, p_a, 0.0), p_b, jnp.where(low, 0.0, p_a)], axis=0
            ).astype(BF16)
            gw_a = (jnp.where(low, g_p[:64], g_p[128:]) - delta) * inv
            gw_b = (g_p[64:128] - delta) * inv
            gs_a = jnp.where(mask, gw_a * exp_a, 0.0)
            gs_b = jnp.where(mask_a, 0.0, gw_b * exp_b)
            g_scores = jnp.concatenate(
                [jnp.where(low, gs_a, 0.0), gs_b, jnp.where(low, 0.0, gs_a)], axis=0
            ).astype(BF16)
            g_linear = jnp.concatenate(
                [
                    jnp.where(mask_a, 0.0, jnp.where(low, gw_a, 0.0)),
                    jnp.where(mask_a, jnp.where(low, 0.0, gw_b), 0.0),
                ],
                axis=0,
            ).astype(BF16)
            go_aug = jnp.concatenate(
                [go_f * inv, -delta * inv, jnp.zeros((AUG - 65, REPEAT * 128), F32)], axis=0
            )
            go_aug_b = go_aug.astype(BF16)
            gqr = dot(ext_t[128:192, r0 : r0 + 192], g_scores) * scale
            state_t = s_ref[0, m, p].astype(F32).T.astype(BF16)
            gpq = dot(ext_t[:128, r0 : r0 + 128], g_linear) + jnp.where(
                low_feat, dot(state_t[:, :AUG], go_aug_b), dot(state_t[:, AUG:], go_aug_b)
            )
            zero = jnp.zeros_like(go_aug_b)
            g_spans = dot_nt(
                jnp.concatenate(
                    [jnp.where(low_aug, go_aug_b, zero), jnp.where(low_aug, zero, go_aug_b)], axis=0
                ),
                pq4,
            )
            gs_ref[0, m, p] = g_spans
            both = g_spans[:AUG] + g_spans[AUG:]
            g_sum = both if p == 0 else g_sum + both
            if p == 0:
                back_ref[0, m, 64:, :128] = g_spans[:AUG].astype(BF16)
            g_pk = dot_nt(g_linear, pq4)
            g_kr = dot_nt(g_scores, qr4) * scale
            g_v = dot_nt(weights, go4)
            g_keys = jnp.concatenate(
                [
                    jnp.concatenate([g_pk, jnp.zeros((64, 128), F32)], axis=0),
                    g_kr,
                    g_v,
                ],
                axis=1,
            )
            if p == 0:
                back_ref[0, m, :64] = g_keys[:64].astype(BF16)
            else:
                gn_ref[0, m, r0 - 64 : r0] = g_keys[:64] + tail
            gn_ref[0, m, r0 : r0 + 64] = g_keys[64:128]
            tail = g_keys[128:]
            if p == rows // 128 - 1:
                gn_ref[0, m, rows - 64 : rows] = tail
                total_ref[0, m] = g_sum.astype(BF16)
                back_ref[0, m, 64:, 128:] = g_sum.astype(BF16)
            pq_f = pq4.astype(F32)
            gmq = features_back_t(pq_f, gpq).astype(BF16)
            for h in range(REPEAT):
                gqr_ref[h * 64 : (h + 1) * 64, start : start + 128] = gqr[:, h * 128 : (h + 1) * 128]
                gmq_ref[h * 64 : (h + 1) * 64, start : start + 128] = gmq[:, h * 128 : (h + 1) * 128]
    cos_t, sin_t = cos_ref[...], sin_ref[...]
    grads = []
    for h in range(REPEAT):
        sl = slice(h * 64, (h + 1) * 64)
        gmq = gmq_ref[sl]
        df_ref[0, sl] = dot_nt(qr_ref[sl], gmq)
        grads.append(rotate_back_t(gqr_ref[sl] + dot(f_ref[h], gmq), cos_t, sin_t))
    gq_ref[0] = jnp.concatenate(grads, axis=0).T.astype(BF16)


def kv_back_kernel(kv_heads, micro, gn_ref, back_ref, n_ref, gs_ref, f_ref, cos_ref, sin_ref,
                   u_ref, b_ref, guq_ref, h1_ref, *refs):
    *next_refs, gkv_ref, df_ref, gu_ref, db_ref, dqkv_ref, acc_ref = refs
    rows = n_ref.shape[2]
    spans = rows // WIN
    cos_t, sin_t = cos_ref[...], sin_ref[...]
    keys, values = [], []
    unit = (lax.broadcasted_iota(jnp.int32, (64, AUG - 64), 1) == 0).astype(BF16)
    for g in range(kv_heads):
        parts = []
        for m in range(micro):
            natural = n_ref[g, m]
            later = [None] * spans
            after_here = back_ref[g, m, 64:, 128:].astype(F32)
            for ref in next_refs:
                after_here += ref[g, m].astype(F32)
            later[spans - 1] = after_here - back_ref[g, m, 64:, :128].astype(F32)
            later[spans - 2] = after_here
            for c in range(spans - 3, -1, -1):
                later[c] = later[c + 1] + gs_ref[g, m, (c + 2) // 2, ((c + 2) % 2) * AUG : ((c + 2) % 2 + 1) * AUG]
            for c in range(spans):
                part = natural[c * 64 : (c + 1) * 64]
                grad = gn_ref[g, m, c * 64 : (c + 1) * 64]
                if c == spans - 1:
                    grad = grad + back_ref[g, m, :64].astype(F32)
                big = later[c].astype(BF16)
                g_pk = dot(jnp.concatenate([part[:, 192:256], unit], axis=1), big)
                g_v = dot_nt(part[:, :128], big[:64])
                parts.append(
                    grad + jnp.concatenate([g_pk, jnp.zeros((64, 64), F32), g_v], axis=1)
                )
        grad_t = jnp.concatenate(parts, axis=0).T
        nat_t = jnp.concatenate([n_ref[g, m, :, :192] for m in range(micro)], axis=0).astype(F32).T
        gmk = features_back_t(nat_t[:128], grad_t[:128]).astype(BF16)
        df_ref[0, g * 64 : (g + 1) * 64] = dot_nt(nat_t[128:].astype(BF16), gmk)
        keys.append(rotate_back_t(grad_t[128:192] + dot(f_ref[g], gmk), cos_t, sin_t))
        values.append(grad_t[192:256])
    gkv = jnp.concatenate(keys + values, axis=0).T.astype(BF16)
    gkv_ref[0] = gkv
    db_ref[...] = dot(u_ref[...].astype(F32).T[:32].astype(BF16), gkv)
    rank_grad = dot_nt(gkv, b_ref[0])

    @pl.when(pl.program_id(0) == 0)
    def _():
        acc_ref[...] = guq_ref[...] + rank_grad

    @pl.when(pl.program_id(0) > 0)
    def _():
        acc_ref[...] += rank_grad

    @pl.when(pl.program_id(0) == pl.num_programs(0) - 1)
    def _():
        gu_ref[...] = acc_ref[...].astype(BF16)
        dqkv_ref[...] = dot(acc_ref[...].T[:32].astype(BF16), h1_ref[...])


def table_kernel(heads_ref, dqkv_ref, dao_ref, dbq_ref, dbo_ref, dg1_ref, dg2_ref, out_ref):
    width = dqkv_ref.shape[1]
    gains = jnp.concatenate([dg1_ref[...], dg2_ref[...], jnp.zeros((6, width), F32)], axis=0)
    rows = jnp.concatenate(
        [dqkv_ref[:24], dao_ref[:8], dbq_ref[:8], dbo_ref[:8], gains, jnp.zeros((8, width), F32)],
        axis=0,
    )
    out_ref[...] = jnp.concatenate([heads_ref[...], rows.T], axis=1)


def out_kernel(depth, n_dp, place_ref, o_ref, ao_ref, bo_ref, x_ref, gain_ref, *refs):
    *w_refs, x2_ref, h2_ref, uo_ref, r2_ref, acc_ref = refs
    uo = dot(o_ref[...], ao_ref[...]).astype(BF16)
    uo_ref[...] = uo
    for j in range(n_dp):
        cols = slice(j * depth, (j + 1) * depth)
        acc_ref[j] = x_ref[:, cols].astype(F32) + dot_nt(uo, bo_ref[cols])
    halves = w_refs[0].shape[2] // depth
    block = halves * depth
    for f, pieces in block_pieces(w_refs, place_ref, n_dp):
        for ref, start in pieces:
            for i in range(ref.shape[0]):
                total = None
                for a in range(halves):
                    e0 = f * block + a * depth
                    if not isinstance(f, int):
                        e0 = pl.multiple_of(e0, depth)
                    term = dot(o_ref[:, pl.ds(e0, depth)], ref[i, :, a * depth : (a + 1) * depth])
                    total = term if total is None else total + term
                acc_ref[start + i] += total
    squares = 0.0
    for j in range(n_dp):
        x2 = acc_ref[j]
        x2_ref[:, j * depth : (j + 1) * depth] = x2
        squares += jnp.sum(x2 * x2, axis=1, keepdims=True)
    r2 = lax.rsqrt(squares * (1.0 / (n_dp * depth)) + EPSILON)
    r2_ref[...] = r2
    for j in range(n_dp):
        cols = slice(j * depth, (j + 1) * depth)
        h2_ref[:, cols] = (acc_ref[j] * r2 * gain_ref[:, cols]).astype(BF16)


def go_kernel(depth, gb_ref, w_ref, ao_ref, guo_ref, o_ref, go_ref, dao_ref):
    groups = w_ref.shape[1]
    halves = w_ref.shape[3] // depth
    guo = guo_ref[...]
    low_rank = dot_nt(ao_ref[...], guo)
    for a in range(halves):
        total = low_rank[a * depth : (a + 1) * depth]
        for j in range(groups):
            total += dot_nt(
                w_ref[0, j, :, a * depth : (a + 1) * depth], gb_ref[:, j * depth : (j + 1) * depth]
            )
        go_ref[a * depth : (a + 1) * depth] = total.astype(BF16)
    dao_ref[...] = dot(guo.astype(F32).T[:16].astype(BF16), o_ref[...])


def gx_query_kernel(shards, gq_ref, wq_ref, u_ref, b_ref, out_ref, gu_ref, db_ref):
    total = dot_nt(gq_ref[0], wq_ref[0, 0])
    for f in range(1, shards):
        total += dot_nt(gq_ref[f], wq_ref[f, 0])
    out_ref[...] = total

    @pl.when(pl.program_id(0) == 0)
    def _():
        u_t = u_ref[...].astype(F32).T[:32].astype(BF16)
        cols = gq_ref.shape[2]
        rank_grad = 0.0
        for f in range(shards):
            rank_grad += dot_nt(gq_ref[f], b_ref[f])
            db_ref[:, f * cols : (f + 1) * cols] = dot(u_t, gq_ref[f])
        gu_ref[...] = rank_grad


def gx_kernel(shards, depth, part_ref, gkv_ref, wkv_ref, gu_ref, a_ref, x_ref, x_all_ref,
              gx2_ref, r1_ref, gain_ref, gx_ref, dg_ref, gh_all, dot_ref):
    j = pl.program_id(0)
    last = pl.num_programs(0) - 1

    @pl.when(j == 0)
    def _():
        dot_ref[...] = jnp.zeros_like(dot_ref)

    total = part_ref[...] + dot_nt(gu_ref[...], a_ref[...])
    for f in range(shards):
        total += dot_nt(gkv_ref[f], wkv_ref[f, 0])
    gh_all[j] = total
    hx = total * x_ref[...].astype(F32)
    dg_ref[...] = jnp.sum(hx * r1_ref[...], axis=0, keepdims=True)
    dot_ref[...] += jnp.sum(hx * gain_ref[0], axis=1, keepdims=True)

    @pl.when(j == last)
    def _():
        count = gh_all.shape[0]
        r1 = r1_ref[...]
        back = r1 * r1 * r1 * dot_ref[...] * (1.0 / (count * depth))
        for i in range(count):
            cols = slice(i * depth, (i + 1) * depth)
            gx_ref[:, cols] = (
                gx2_ref[:, cols]
                + r1 * gain_ref[i] * gh_all[i]
                - x_all_ref[:, cols].astype(F32) * back
            ).astype(BF16)


def pack_attention_kernel(wq_ref, wk_ref, wv_ref, wo_ref, qkv_ref, out_ref):
    depth, q_cols = wq_ref.shape
    qkv_ref[:, :q_cols] = wq_ref[...]
    qkv_ref[:, q_cols:] = jnp.concatenate([wk_ref[...], wv_ref[...]], axis=1)
    for a in range(wo_ref.shape[0] // depth):
        out_ref[:, a * depth : (a + 1) * depth] = wo_ref[a * depth : (a + 1) * depth]


def pack_ffn_kernel(cuts, wg_ref, wu_ref, wd_ref, *refs):
    for ref, start, stop in zip(refs, cuts, cuts[1:]):
        count = stop - start
        ref[:, :count] = wg_ref[:, start:stop]
        ref[:, count : 2 * count] = wu_ref[:, start:stop]
        step = min(256, count)
        for at in range(0, count, step):
            ref[:, 2 * count + at : 2 * count + at + step] = (
                wd_ref[start + at : start + at + step].astype(F32).T.astype(BF16)
            )


def joined(refs):
    own_a, own_b, x_a, y_a, y_b, x_b = refs
    left = own_a[0].astype(F32) + x_a[0].astype(F32) + y_a[...].astype(F32)
    right = own_b[0].astype(F32) + y_b[0].astype(F32) + x_b[...].astype(F32)
    return jnp.concatenate([left, right], axis=1)


def result_kernel(count, x2_ref, valid_ref, *refs):
    *parts, out_ref = refs
    total = joined(parts) if count == 6 else parts[0][...]
    out_ref[...] = jnp.where(valid_ref[...] > 0, x2_ref[...] + total, 0.0).astype(BF16)


def mid_back_kernel(count, x2_ref, r2_ref, gain_ref, gy_ref, uo_ref, bo_ref, *refs):
    gx2_ref, gb_ref, guo_ref, dg_ref, dbo_ref = refs[-5:]
    parts = refs[:count]
    gh = joined(parts) if count == 6 else parts[0][...]
    x2, r2 = x2_ref[...], r2_ref[...]
    gx = gh * x2
    scaled = gh * gain_ref[...]
    mean = jnp.mean(scaled * x2, axis=1, keepdims=True)
    gx2 = gy_ref[...].astype(F32) + r2 * scaled - x2 * (r2 * r2 * r2 * mean)
    gx2_ref[...] = gx2
    gb = gx2.astype(BF16)
    gb_ref[...] = gb
    guo_ref[...] = dot(gb, bo_ref[...]).astype(BF16)
    dg = jnp.sum(gx * r2, axis=0, keepdims=True)
    dbo = dot(uo_ref[...].astype(F32).T[:16].astype(BF16), gb)

    @pl.when(pl.program_id(0) == 0)
    def _():
        dg_ref[...] = dg
        dbo_ref[...] = dbo

    @pl.when(pl.program_id(0) > 0)
    def _():
        dg_ref[...] += dg
        dbo_ref[...] += dbo


def row_copies(refs, rows_ref, sems, r):
    tile, width = rows_ref.shape[1:]
    half_tile, half = tile // 2, width // 2
    if len(refs) == 1:
        parts = [(refs[0].at[r * tile : (r + 1) * tile], rows_ref.at[r])]
    elif r == 0:
        parts = [(refs[i], rows_ref.at[0, i * half_tile : (i + 1) * half_tile]) for i in range(2)]
    else:
        parts = [(refs[2], rows_ref.at[1, :half_tile])]
        parts += [
            (refs[3 + i], rows_ref.at[1, half_tile:, i * half : (i + 1) * half]) for i in range(2)
        ]
    return [
        pltpu.make_async_copy(source, target, sems.at[r, i])
        for i, (source, target) in enumerate(parts)
    ]


def store_rows(value_ref, refs):
    if len(refs) == 1:
        refs[0][...] = value_ref[...].astype(BF16)
        return
    send_x, keep_x, send_y, keep_y = refs
    count, half = value_ref.shape[0] // 2, value_ref.shape[1] // 2
    keep_x[0] = value_ref[:count, :half].astype(BF16)
    send_x[0] = value_ref[count:, :half].astype(BF16)
    for here, ref in enumerate((keep_y, send_y)):

        @pl.when(pl.program_id(0) == here)
        def _(ref=ref):
            ref[0] = value_ref[:count, half:].astype(BF16)
            ref[1] = value_ref[count:, half:].astype(BF16)


def ffn_kernel(pieces, carries, wg_ref, wu_ref, wd_ref, *refs):
    h2_refs, gy_refs = refs[:pieces], refs[pieces : 2 * pieces]
    carried = refs[2 * pieces : 2 * pieces + carries]
    *out_refs, h2_ref, gy_ref, out_acc, gh_acc, h2_sems, gy_sems = refs[2 * pieces + carries :]
    r, j = pl.program_id(0), pl.program_id(1)
    copies = [
        row_copies(h2_refs, h2_ref, h2_sems, tile) + row_copies(gy_refs, gy_ref, gy_sems, tile)
        for tile in range(2)
    ]

    @pl.when((r == 0) & (j == 0))
    def _():
        for copy in copies[0] + copies[1]:
            copy.start()
        for copy in copies[0]:
            copy.wait()

    @pl.when((r == 1) & (j == 0))
    def _():
        for copy in copies[1]:
            copy.wait()

    h2, gy = h2_ref[r], gy_ref[r]
    shape = (wg_ref.shape[0] * wg_ref.shape[1], wg_ref.shape[2])
    wg, wu, wd = wg_ref[...].reshape(shape), wu_ref[...].reshape(shape), wd_ref[...].reshape(shape)
    gate = dot(h2, wg)
    up = dot(h2, wu)
    g_hid = dot(gy, wd)
    sig = 1.0 / (1.0 + jnp.exp(-gate))
    silu = gate * sig
    hid = (silu * up).astype(BF16)
    g_gate = (g_hid * up * sig * (1.0 + gate * (1.0 - sig))).astype(BF16)
    g_up = (g_hid * silu).astype(BF16)

    @pl.when(j == 0)
    def _():
        out, gh = dot_nt(hid, wd), dot_nt(g_gate, wg) + dot_nt(g_up, wu)
        if carries:
            out += carried[0][...].astype(F32)
            gh += carried[1][...].astype(F32)
        out_acc[...] = out
        gh_acc[...] = gh

    @pl.when(j > 0)
    def _():
        out_acc[...] += dot_nt(hid, wd)
        gh_acc[...] += dot_nt(g_gate, wg) + dot_nt(g_up, wu)

    @pl.when(j == pl.num_programs(1) - 1)
    def _():
        half = len(out_refs) // 2
        store_rows(out_acc, out_refs[:half])
        store_rows(gh_acc, out_refs[half:])


def ffn(tile, split, h2, gy, weights, *carried):
    total = sum(part.size for part in h2) // h2[0].shape[1]
    width = h2[0].shape[1]
    groups, depth, cols = weights.shape
    tiles = cols // (3 * tile)
    pieces = len(h2)
    row_tile = total // 2
    row_spec = pl.BlockSpec((row_tile, width), lambda r, j: (r, 0))

    def weight_spec(kind):
        return pl.BlockSpec((groups, depth, tile), lambda r, j: (0, 0, kind * tiles + j))

    piece_specs = [pl.BlockSpec(memory_space=pl.ANY)] * pieces
    if split and pieces > 1:
        count, half = row_tile // 2, width // 2
        moving = pl.BlockSpec((1, count, half), lambda r, j: (r, 0, 0))
        fixed = pl.BlockSpec((2, count, half), lambda r, j: (0, 0, 0))
        out_specs = [moving, moving, fixed, fixed] * 2
        out_shape = [jax.ShapeDtypeStruct((2, count, half), BF16)] * 8
    else:
        out_specs = [row_spec, row_spec]
        out_shape = [jax.ShapeDtypeStruct((total, width), BF16)] * 2
    outs = pl.pallas_call(
        functools.partial(ffn_kernel, pieces, len(carried)),
        grid=(total // row_tile, tiles),
        in_specs=[weight_spec(0), weight_spec(1), weight_spec(2)]
        + piece_specs * 2
        + [row_spec] * len(carried),
        out_specs=out_specs,
        out_shape=out_shape,
        scratch_shapes=[pltpu.VMEM((2, row_tile, width), BF16)] * 2
        + [pltpu.VMEM((row_tile, width), F32)] * 2
        + [pltpu.SemaphoreType.DMA((2, 3))] * 2,
        compiler_params=params(60, ("arbitrary", "arbitrary")),
        cost_estimate=cost(4 * total * width * cols, 2 * width * cols * (total // row_tile) + 12 * total * width),
        name="feed_forward",
    )(weights, weights, weights, *h2, *gy, *carried)
    return (outs[: len(outs) // 2], outs[len(outs) // 2 :]) if split else outs


def gather_first(rows, size):
    if size != 4:
        return (lax.all_gather(rows, "fsdp", axis=0, tiled=True),)
    return rows, by_x(rows), by_y(rows)


def gather_second(*first):
    if len(first) == 1:
        return first
    rows, from_x, from_y = first
    half = rows.shape[1] // 2
    return rows, from_x, from_y, by_x(from_y[:, :half]), by_y(from_x[:, half:])


def scatter_first(*parts, size):
    if size != 4:
        (part,) = parts
        part = part.reshape(size, part.shape[0] // size, part.shape[1])
        return (lax.all_to_all(part, "fsdp", split_axis=0, concat_axis=0, tiled=True),)
    send_x, keep_x, send_y, keep_y = parts
    return keep_x, keep_y, by_x(send_x), by_y(send_y)


def pass_on_kernel(keep_x, from_x, keep_y, from_y, a_ref, b_ref):
    a_ref[...] = (keep_x[...].astype(F32) + from_x[...].astype(F32)).astype(BF16)
    b_ref[...] = (keep_y[...].astype(F32) + from_y[...].astype(F32)).astype(BF16)


def scatter_second(*first):
    if len(first) == 1:
        return [jnp.sum(first[0].astype(F32), axis=0)]
    keep_x, keep_y, from_x, from_y = first
    _, count, half = keep_x.shape
    second = pl.BlockSpec((None, count, half), lambda _: (1, 0, 0))
    a_pass, b_pass = pl.pallas_call(
        pass_on_kernel,
        grid=(1,),
        in_specs=[second] * 4,
        out_specs=[pl.BlockSpec((count, half), lambda _: (0, 0))] * 2,
        out_shape=[jax.ShapeDtypeStruct((count, half), BF16)] * 2,
        compiler_params=params(60),
        name="pass_on",
    )(keep_x, from_x, keep_y, from_y)
    return [keep_x, keep_y, from_x, by_y(a_pass), from_y, by_x(b_pass)]


def term_specs(terms, row_tile, width):
    full = pl.BlockSpec((row_tile, width), lambda r: (r, 0))
    if len(terms) == 1:
        return [full]
    half = width // 2
    row = pl.BlockSpec((row_tile, half), lambda r: (r, 0))
    first = pl.BlockSpec((1, row_tile, half), lambda r: (0, r, 0))
    return [first, first, first, row, first, row]


def pair_swap(part):
    return lax.ppermute(part, "dp", [(i, i ^ 1) for i in range(lax.axis_size("dp"))])


def columns_share(block, size, group):
    half = block.shape[0] // 2
    return block if size != 4 else lax.dynamic_slice_in_dim(block, group % 2 * half, half, 0)


def columns_first(mine, size):
    if size != 4:
        return (lax.all_gather(mine, "fsdp", axis=0, tiled=False),)
    return by_x(mine), by_y(mine)


def columns_second(*first):
    if len(first) == 1:
        return first
    from_x, from_y = first
    share = from_x.shape[0] // 2
    return (
        from_x, from_y, by_x(from_y[:share]), by_y(from_x[share:]),
        pair_swap(from_x), pair_swap(from_y),
    )


def columns_third(block, *second):
    if len(second) == 1:
        return [second[0][f] for f in range(second[0].shape[0])]
    from_x, from_y, diagonal_x, diagonal_y, other_x, other_y = second
    return [
        block, from_x, from_y, diagonal_x, diagonal_y,
        other_x, other_y, pair_swap(diagonal_x), pair_swap(diagonal_y),
    ]


def assembled(pieces, group, shard):
    if len(pieces) != 9:
        return jnp.stack(pieces)
    block = pieces[0]
    half = block.shape[0] // 2
    core = group % 2
    out = jnp.broadcast_to(block[None], (4,) + block.shape)

    def put(out, part, f, at):
        return lax.dynamic_update_slice(out, part[None], (f, at, 0, 0))

    masks = ((1, 0), (2, 0), (3, 0), (3, half // 2))
    for side, at in ((pieces[1:5], core * half), (pieces[5:], (1 - core) * half)):
        for part, (mask, offset) in zip(side, masks):
            out = put(out, part, shard ^ mask, at + offset)
    return out


def shifted(array, size, direction):
    moved = []
    for step in range(2, size):
        if direction > 0:
            perm = [(i, i + step) for i in range(size - step)]
        else:
            perm = [(i + step, i) for i in range(size - step)]
        moved.append(lax.ppermute(array, "fsdp", perm))
    return moved


def deal_out(rows):
    count, width = rows.shape
    groups = lax.axis_size("dp")
    pieces = rows.reshape(groups, count // groups, width)
    return lax.all_to_all(pieces, "dp", split_axis=0, concat_axis=0, tiled=True)


def reorder_kernel(at_ref, in_ref, out_ref):
    for j in range(out_ref.shape[0]):
        out_ref[j] = in_ref[at_ref[j]]


def reordered(spread, order):
    return pl.pallas_call(
        reorder_kernel,
        in_specs=[pl.BlockSpec(memory_space=pltpu.SMEM), pl.BlockSpec(memory_space=pltpu.VMEM)],
        out_specs=pl.BlockSpec(memory_space=pltpu.VMEM),
        out_shape=jax.ShapeDtypeStruct(spread.shape, spread.dtype),
        compiler_params=pltpu.CompilerParams(vmem_limit_bytes=60 * MIB),
        name="reorder",
    )(order, spread)


def deal_in(ordered):
    groups, share, width = ordered.shape
    settled = lax.all_to_all(ordered, "dp", split_axis=0, concat_axis=0, tiled=True)
    return settled.reshape(groups * share, width)


def halved(table):
    n_dp, n_f = lax.axis_size("dp"), lax.axis_size("fsdp")
    dp_bits, f_bits = n_dp.bit_length() - 1, n_f.bit_length() - 1
    bits = [("dp", b) for b in range(dp_bits)][::-1] + [("fsdp", b) for b in range(f_bits)][::-1]
    left = table.reshape((2,) * len(bits) + table.shape[1:])
    order = [("dp", 0)] + [("fsdp", b) for b in range(f_bits)] + [("dp", b) for b in range(1, dp_bits)]
    for axis, bit in order:
        at = bits.index((axis, bit))
        bits.pop(at)
        mine = (lax.axis_index(axis) >> bit) & 1
        keep = lax.dynamic_index_in_dim(left, mine, at, keepdims=False)
        send = lax.dynamic_index_in_dim(left, 1 - mine, at, keepdims=False).astype(BF16)
        perm = [(i, i ^ (1 << bit)) for i in range(lax.axis_size(axis))]
        left = keep + lax.ppermute(send, axis, perm).astype(F32)
    return left


def shards(
    inputs, cotangent, lengths, dealing, wq, wk, wv, wo, wg, wu, wd,
    down_ad, up_qo, up_kv, fmap_q, fmap_k, gains,
):
    n_dp = lax.axis_size("dp")
    n_f = lax.axis_size("fsdp")
    group = lax.axis_index("dp")
    quarter = lax.axis_index("fsdp")
    micro, rows, width = inputs.shape[1:]
    total = micro * rows
    depth = wq.shape[0]
    q_cols, k_cols = wq.shape[1], wk.shape[1]
    kv_heads = k_cols // HEAD_SIZE
    heads = q_cols // HEAD_SIZE
    halves = wo.shape[0] // depth
    n_all = n_dp * n_f
    x = inputs[0].reshape(total, width)

    small_parts = [down_ad, up_qo, up_kv, fmap_q, fmap_k, gains]
    flat = jnp.concatenate([part.reshape(-1) for part in small_parts])
    small_rows = -(-flat.shape[0] // (16 * 128)) * 16
    flat = jnp.pad(flat, (0, small_rows * 128 - flat.shape[0])).reshape(1, small_rows, 128)
    small = lax.all_gather(flat.reshape(small_rows, 128), "dp", axis=0, tiled=False)
    small = lax.all_gather(small, "fsdp", axis=0, tiled=False)
    small = small.transpose(1, 0, 2, 3).reshape(n_all, small_rows * 128)
    at = 0
    fetched = []
    for part in small_parts:
        fetched.append(
            small[:, at : at + part.size].reshape((n_all * part.shape[0],) + part.shape[1:])
        )
        at += part.size
    down_ad, up_qo, up_kv, fmap_q, fmap_k, gains = fetched

    pack_cols = q_cols + 2 * k_cols
    w_qkv, w_out = pl.pallas_call(
        pack_attention_kernel,
        out_shape=[
            jax.ShapeDtypeStruct((depth, pack_cols), BF16),
            jax.ShapeDtypeStruct((depth, q_cols), BF16),
        ],
        compiler_params=pltpu.CompilerParams(vmem_limit_bytes=60 * MIB),
        name="pack_attention",
    )(wq, wk, wv, wo)
    w_qkv = lax.all_gather(w_qkv, "dp", axis=0, tiled=False)
    w_out = lax.all_gather(w_out, "dp", axis=0, tiled=False)
    near, spread = together(
        (functools.partial(columns_first, size=n_f), columns_share(w_qkv, n_f, group)),
        (deal_out, after(cotangent[0].reshape(total, width), small)),
    )
    share_micro = group * (total // n_dp) // rows
    order = lax.dynamic_index_in_dim(dealing, share_micro, 0, keepdims=False)

    gain_one = gains[:, 0].astype(F32)
    gain_two = gains[:, 1].astype(F32)

    hidden = wg.shape[1]
    tile = hidden // 4
    cuts = (0, 3 * tile, hidden)
    w_ffn = pl.pallas_call(
        functools.partial(pack_ffn_kernel, cuts),
        out_shape=[
            jax.ShapeDtypeStruct((depth, 3 * (stop - start)), BF16)
            for start, stop in zip(cuts, cuts[1:])
        ],
        compiler_params=pltpu.CompilerParams(vmem_limit_bytes=60 * MIB),
        name="pack_feed_forward",
    )(wg, wu, wd)
    positions = quarter * rows + jnp.arange(rows, dtype=jnp.int32)
    seq_len = lax.dynamic_index_in_dim(lengths, group, 0, keepdims=False)
    valid = (positions[None, :] < seq_len[:, None]).reshape(total, 1)

    xf = x.astype(F32)
    r1 = lax.rsqrt(jnp.mean(xf * xf, axis=-1, keepdims=True) + EPSILON)
    h1 = (xf * r1 * gain_one).astype(BF16)
    rank = ADAPTER_RANK
    lanes = RANK_LANES
    a_qkv = jnp.pad(down_ad[:, : 3 * rank], ((0, 0), (0, lanes - 3 * rank)))
    a_o = jnp.pad(down_ad[:, 3 * rank :], ((0, 0), (0, lanes - rank)))
    u = dot(h1, a_qkv).astype(BF16)
    b_q = up_qo[:, :rank].reshape(n_f, q_cols, rank)
    b_k = up_kv[:, :rank].reshape(n_f, k_cols, rank)
    b_v = up_kv[:, rank:].reshape(n_f, k_cols, rank)
    b_o = jnp.pad(up_qo[:, rank:], ((0, 0), (0, lanes - rank)))

    def placed(block, at):
        return jnp.pad(block.transpose(0, 2, 1), ((0, 0), (at, lanes - at - rank), (0, 0)))

    b_q_t = placed(b_q, 0)
    b_kv_t = jnp.concatenate([placed(b_k, rank), placed(b_v, 2 * rank)], axis=2)
    fq = fmap_q.reshape(H, HEAD_SIZE, HEAD_SIZE)
    fk = fmap_k.reshape(KEY_VALUE_HEADS, HEAD_SIZE, HEAD_SIZE)
    fq_t = jnp.concatenate([fq.transpose(0, 2, 1), -fq.transpose(0, 2, 1)], axis=1)
    fk_t = jnp.concatenate([fk.transpose(0, 2, 1), -fk.transpose(0, 2, 1)], axis=1)
    cos_t, sin_t = rope_tables_t(jnp.tile(positions, micro))
    pairs = rows // 128
    prepared = (h1, u, a_qkv, a_o, b_q_t, b_kv_t, b_o, fq, fk, fq_t, fk_t, cos_t, sin_t)
    inverse = jnp.argsort(dealing, axis=1).astype(jnp.int32)
    prepared += (inverse,)
    second, out_near, cot, prepared = together(
        (columns_second, *near),
        (functools.partial(columns_first, size=n_f), columns_share(w_out, n_f, group)),
        (lambda spread, order: deal_in(reordered(spread, order)), spread, order),
        (lambda *arrays: arrays, *prepared),
    )
    h1, u, a_qkv, a_o, b_q_t, b_kv_t, b_o, fq, fk, fq_t, fk_t, cos_t, sin_t, inverse = prepared
    fetched_ffn = [lax.all_gather(after(w_ffn[0], cot), "dp", axis=0, tiled=False)]
    (qkv_pieces,) = together((columns_third, w_qkv, *second))

    place = jnp.stack([quarter, group % 2]).astype(jnp.int32)
    smem = pl.BlockSpec(memory_space=pltpu.SMEM)
    vmem = pl.BlockSpec(memory_space=pltpu.VMEM)

    def columns(pieces, size, at):
        return [
            pl.BlockSpec(part.shape[:2] + (size,), lambda _: (0, 0, at), pipeline_mode=pl.Buffered(1))
            for part in pieces
        ]

    def key_values(h1, u, *pieces):
        return pl.pallas_call(
            functools.partial(kv_kernel, kv_heads, micro, depth, n_dp),
            grid=(1,),
            in_specs=[smem] + [vmem] * 6 + columns(pieces, 2 * k_cols, q_cols // (2 * k_cols)),
            out_specs=[vmem] * 3,
            out_shape=[
                jax.ShapeDtypeStruct((KEY_VALUE_HEADS, micro, rows, 256), BF16),
                jax.ShapeDtypeStruct((KEY_VALUE_HEADS, micro, AUG, 128), BF16),
                jax.ShapeDtypeStruct((KEY_VALUE_HEADS, micro, 112, 256), BF16),
            ],
            compiler_params=params(40),
            cost_estimate=cost(4 * total * width * k_cols * n_f, 2 * (total * width + 2 * width * k_cols * n_f), 128 * 8 * total),
            name="key_value",
        )(place, h1, u, b_kv_t, cos_t, sin_t, fk_t, *pieces)

    def queries(h1, u, *pieces):
        return pl.pallas_call(
            functools.partial(q_kernel, heads, depth, n_dp),
            grid=(1,),
            in_specs=[smem] + [vmem] * 6 + columns(pieces, q_cols, 0),
            out_specs=[vmem, vmem],
            out_shape=[
                jax.ShapeDtypeStruct((H * 64, total), BF16),
                jax.ShapeDtypeStruct((H * 128, total), BF16),
            ],
            compiler_params=params(40),
            cost_estimate=cost(2 * total * width * q_cols * n_f, 2 * (total * width + width * q_cols * n_f + 3 * total * 2048), 128 * 32 * total),
            name="query",
        )(place, h1, u, b_q_t, cos_t, sin_t, fq_t, *pieces)

    forward_one = [(i, i + 1) for i in range(n_f - 1)]
    backward_one = [(i + 1, i) for i in range(n_f - 1)]

    gy_both = jnp.where(valid, cot, jnp.zeros_like(cot))
    gy = [gy_both[m * rows : (m + 1) * rows] for m in range(micro)]
    gather = functools.partial(gather_first, size=n_f)
    (kv_natural, totals, message), out_second = together(
        (key_values, h1, u, *qkv_pieces), (columns_second, *out_near)
    )

    def send_on(message, totals):
        return lax.ppermute(message, "fsdp", forward_one), shifted(totals, n_f, 1)

    (q_rot, q_feat), (message, bases) = together(
        (queries, h1, u, *qkv_pieces), (send_on, message, totals)
    )
    part = after(w_ffn[1], q_rot)
    fetched_ffn.append(lax.all_gather(part, "dp", axis=0, tiled=False))
    w_ffn = fetched_ffn

    has_prev = (quarter > 0).astype(jnp.int32).reshape(1)
    g4 = REPEAT * 64
    prev_spec = smem
    n_spec = pl.BlockSpec((1, micro, rows, 256), lambda g: (g, 0, 0, 0))
    message_spec = pl.BlockSpec((1, micro, 112, 256), lambda g: (g, 0, 0, 0))
    back_spec = pl.BlockSpec((1, micro, 64 + AUG, 256), lambda g: (g, 0, 0, 0))
    state_spec = pl.BlockSpec((1, micro, pairs, 2 * AUG, 128), lambda g: (g, 0, 0, 0, 0))
    head_spec = pl.BlockSpec((g4, total), lambda g: (g, 0))
    feat_spec = pl.BlockSpec((2 * g4, total), lambda g: (g, 0))
    den_spec = pl.BlockSpec((1, 8, total), lambda g: (g, 0, 0))
    base_spec = pl.BlockSpec((1, micro, AUG, 128), lambda g: (g, 0, 0, 0))
    attend_flops = H * total * 2 * (192 * 64 + 128 * 128 + 160 * 128 + 192 * 64)
    attend = pl.pallas_call(
        functools.partial(attend_kernel, micro),
        grid=(KEY_VALUE_HEADS,),
        in_specs=[
            prev_spec,
            n_spec,
            message_spec,
            head_spec,
            feat_spec,
        ]
        + [base_spec] * (n_f - 2),
        out_specs=[pl.BlockSpec((total, g4), lambda g: (0, g)), head_spec, den_spec, state_spec],
        out_shape=[
            jax.ShapeDtypeStruct((total, H * 64), BF16),
            jax.ShapeDtypeStruct((H * 64, total), BF16),
            jax.ShapeDtypeStruct((KEY_VALUE_HEADS, 8, total), F32),
            jax.ShapeDtypeStruct((KEY_VALUE_HEADS, micro, pairs, 2 * AUG, 128), BF16),
        ],
        compiler_params=params(60),
        cost_estimate=cost(attend_flops, 14 * MIB, 128 * H * total),
        name="attend",
    )
    (o, o_t, den, states), gy_first, out_pieces = together(
        (attend, has_prev, kv_natural, message, q_rot, q_feat, *bases),
        (gather, gy[0]),
        (columns_third, w_out, *out_second),
    )
    project_out = pl.pallas_call(
        functools.partial(out_kernel, depth, n_dp),
        grid=(1,),
        in_specs=[smem] + [vmem] * 5 + columns(out_pieces, q_cols, 0),
        out_specs=[vmem] * 4,
        out_shape=[
            jax.ShapeDtypeStruct((total, width), F32),
            jax.ShapeDtypeStruct((total, width), BF16),
            jax.ShapeDtypeStruct((total, lanes), BF16),
            jax.ShapeDtypeStruct((total, 1), F32),
        ],
        scratch_shapes=[pltpu.VMEM((n_dp, total, depth), F32)],
        compiler_params=params(60),
        cost_estimate=cost(2 * total * width * H * 64, 20 * MIB),
        name="output_projection",
    )
    (x2, h2, uo, r2), gy_zero = together(
        (project_out, place, o, a_o, b_o, x, gain_two.reshape(1, width), *out_pieces),
        (gather_second, *gy_first),
    )
    gather = functools.partial(gather_first, size=n_f)

    def assemble(*pieces):
        return assembled(pieces, group, quarter)

    h2_first, w_qkv = together((gather, h2[:rows]), (assemble, *qkv_pieces))
    h2_zero, w_out = together((gather_second, *h2_first), (assemble, *out_pieces))

    def piece(array, m):
        return array[m * rows : (m + 1) * rows]

    row_tile = min(128, rows)

    def finish(m, terms):
        return pl.pallas_call(
            functools.partial(result_kernel, len(terms)),
            grid=(rows // row_tile,),
            in_specs=[
                pl.BlockSpec((row_tile, width), lambda r: (m * (rows // row_tile) + r, 0)),
                pl.BlockSpec((row_tile, 1), lambda r: (m * (rows // row_tile) + r, 0)),
            ]
            + term_specs(terms, row_tile, width),
            out_specs=pl.BlockSpec((row_tile, width), lambda r: (r, 0)),
            out_shape=jax.ShapeDtypeStruct((rows, width), BF16),
            compiler_params=params(60),
            cost_estimate=cost(4 * rows * width, 10 * rows * width),
            name="result",
        )(x2, valid_rows, *terms)

    def mid_back(m, terms, gy, *whole_arrays):
        here = pl.BlockSpec((row_tile, width), lambda r: (m * (rows // row_tile) + r, 0))
        thin = pl.BlockSpec((row_tile, lanes), lambda r: (m * (rows // row_tile) + r, 0))
        count = 6 + len(terms)
        return pl.pallas_call(
            functools.partial(mid_back_kernel, len(terms)),
            grid=(rows // row_tile,),
            in_specs=[
                here,
                pl.BlockSpec((row_tile, 1), lambda r: (m * (rows // row_tile) + r, 0)),
                whole((1, width)),
                pl.BlockSpec((row_tile, width), lambda r: (r, 0)),
                thin,
                whole((width, lanes)),
            ]
            + term_specs(terms, row_tile, width)
            + [pl.BlockSpec(memory_space=pl.ANY)] * len(whole_arrays),
            out_specs=[here, here, thin, whole((1, width)), whole((16, width))],
            out_shape=[
                jax.ShapeDtypeStruct((total, width), F32),
                jax.ShapeDtypeStruct((total, width), BF16),
                jax.ShapeDtypeStruct((total, lanes), BF16),
                jax.ShapeDtypeStruct((1, width), F32),
                jax.ShapeDtypeStruct((16, width), F32),
            ],
            input_output_aliases={count + i: i for i in range(len(whole_arrays))},
            compiler_params=params(60),
            cost_estimate=cost(20 * rows * width, 16 * rows * width),
            name="mid_back",
        )(x2, r2, gain_two.reshape(1, width), gy, uo, b_o, *terms, *whole_arrays)

    valid_rows = valid.astype(jnp.int32)
    def feed(split):
        def run(h2, gy, *carried):
            return ffn(tile, split, h2, gy, w_ffn[1 if split else 0], *carried)

        return run

    scatter = functools.partial(scatter_first, size=n_f)
    head_zero, h2_first, gy_first = together(
        (feed(False), h2_zero, gy_zero), (gather, h2[rows:]), (gather, gy[1])
    )
    (down_zero, gh_zero), h2_one, gy_one = together(
        (feed(True), h2_zero, gy_zero, *head_zero),
        (gather_second, *h2_first),
        (gather_second, *gy_first),
    )
    head_one, gh_zero_terms, down_zero_terms = together(
        (feed(False), h2_one, gy_one), (scatter, *gh_zero), (scatter, *down_zero)
    )
    (down_one, gh_one), gh_zero_terms, down_zero_terms = together(
        (feed(True), h2_one, gy_one, *head_one),
        (scatter_second, *gh_zero_terms),
        (scatter_second, *down_zero_terms),
    )

    go_back = pl.pallas_call(
        functools.partial(go_kernel, depth),
        grid=(n_f,),
        in_specs=[
            whole((total, width)),
            pl.BlockSpec((1, n_dp, depth, q_cols), lambda f: (f, 0, 0, 0)),
            pl.BlockSpec((q_cols, lanes), lambda f: (f, 0)),
            whole((total, lanes)),
            pl.BlockSpec((total, q_cols), lambda f: (0, f)),
        ],
        out_specs=[
            pl.BlockSpec((q_cols, total), lambda f: (f, 0)),
            pl.BlockSpec((16, q_cols), lambda f: (0, f)),
        ],
        out_shape=[
            jax.ShapeDtypeStruct((H * 64, total), BF16),
            jax.ShapeDtypeStruct((16, H * 64), F32),
        ],
        compiler_params=params(60),
        cost_estimate=cost(2 * total * width * H * 64, 12 * MIB),
        name="output_projection_back",
    )

    attend_back = pl.pallas_call(
        functools.partial(attend_back_kernel, micro),
        grid=(KEY_VALUE_HEADS,),
        in_specs=[
            prev_spec,
            n_spec,
            message_spec,
            state_spec,
            head_spec,
            feat_spec,
            head_spec,
            head_spec,
            den_spec,
            pl.BlockSpec((REPEAT, 64, 64), lambda g: (g, 0, 0)),
            whole((32, total)),
            whole((32, total)),
        ],
        out_specs=[
            pl.BlockSpec((1, total, g4), lambda g: (g * g4 // q_cols, 0, g % (q_cols // g4))),
            pl.BlockSpec((1, g4, 64), lambda g: (g, 0, 0)),
            n_spec,
            state_spec,
            back_spec,
            base_spec,
        ],
        out_shape=[
            jax.ShapeDtypeStruct((n_f, total, q_cols), BF16),
            jax.ShapeDtypeStruct((KEY_VALUE_HEADS, g4, 64), F32),
            jax.ShapeDtypeStruct((KEY_VALUE_HEADS, micro, rows, 256), F32),
            jax.ShapeDtypeStruct((KEY_VALUE_HEADS, micro, pairs, 2 * AUG, 128), F32),
            jax.ShapeDtypeStruct((KEY_VALUE_HEADS, micro, 64 + AUG, 256), BF16),
            jax.ShapeDtypeStruct((KEY_VALUE_HEADS, micro, AUG, 128), BF16),
        ],
        scratch_shapes=[pltpu.VMEM((g4, total), F32), pltpu.VMEM((g4, total), BF16)],
        compiler_params=params(60),
        cost_estimate=cost(3 * attend_flops, 24 * MIB, 128 * H * total),
        name="attend_back",
    )
    gh_one_terms, zero, result_zero = together(
        (scatter, *gh_one),
        (functools.partial(mid_back, 0), gh_zero_terms, gy[0]),
        (functools.partial(finish, 0), down_zero_terms),
    )
    (gh_one_terms,) = together((scatter_second, *gh_one_terms))

    def norm_to_output(gh_one, gy_one, *zero):
        gx2, gb, guo, *one = mid_back(1, gh_one, gy_one, *zero[:3])
        go_t, d_ao_t = go_back(gb, w_out, a_o, guo, o)
        return gx2, go_t, d_ao_t, zero[3] + one[0], zero[4] + one[1]

    (gx2, go_t, d_ao_t, dg2, d_bo_t), down_one_terms = together(
        (norm_to_output, gh_one_terms, gy[1], *zero), (scatter, *down_one)
    )
    back, down_one_terms, spread_zero = together(
        (attend_back, has_prev, kv_natural, message, states, q_rot, q_feat, go_t, o_t, den, fq, cos_t, sin_t),
        (scatter_second, *down_one_terms),
        (deal_out, result_zero),
    )
    gq, d_fq, g_keys, g_states, g_message, g_total = back

    query_part = pl.pallas_call(
        functools.partial(gx_query_kernel, n_f),
        grid=(n_dp,),
        in_specs=[
            whole((n_f, total, q_cols)),
            pl.BlockSpec((n_f, 1, depth, q_cols), lambda j: (0, j, 0, 0)),
            whole((total, lanes)),
            whole((n_f, lanes, q_cols)),
        ],
        out_specs=[
            pl.BlockSpec((total, depth), lambda j: (0, j)),
            whole((total, lanes)),
            whole((32, H * 64)),
        ],
        out_shape=[
            jax.ShapeDtypeStruct((total, width), F32),
            jax.ShapeDtypeStruct((total, lanes), F32),
            jax.ShapeDtypeStruct((32, H * 64), F32),
        ],
        compiler_params=params(60),
        cost_estimate=cost(2 * total * width * 2048, 16 * MIB),
        name="query_input_gradient",
    )

    def exchange(g_message, g_total):
        return lax.ppermute(g_message, "fsdp", backward_one), shifted(g_total, n_f, -1)

    (gh_q, gu_q, d_bq_t), (g_message, g_next), out_zero, result_one = together(
        (query_part, gq, w_qkv, u, b_q_t),
        (exchange, g_message, g_total),
        (lambda spread, order: deal_in(reordered(spread, order)), spread_zero, inverse[0]),
        (functools.partial(finish, 1), down_one_terms),
    )

    next_spec = pl.BlockSpec((kv_heads, micro, AUG, 128), lambda f: (f, 0, 0, 0))
    kv_back = pl.pallas_call(
        functools.partial(kv_back_kernel, kv_heads, micro),
        grid=(n_f,),
        in_specs=[
            pl.BlockSpec((kv_heads, micro, rows, 256), lambda f: (f, 0, 0, 0)),
            pl.BlockSpec((kv_heads, micro, 64 + AUG, 256), lambda f: (f, 0, 0, 0)),
            pl.BlockSpec((kv_heads, micro, rows, 256), lambda f: (f, 0, 0, 0)),
            pl.BlockSpec((kv_heads, micro, pairs, 2 * AUG, 128), lambda f: (f, 0, 0, 0, 0)),
            pl.BlockSpec((kv_heads, 64, 64), lambda f: (f, 0, 0)),
            whole((32, total)),
            whole((32, total)),
            whole((total, lanes)),
            pl.BlockSpec((1, lanes, 2 * k_cols), lambda f: (f, 0, 0)),
            whole((total, lanes)),
            whole((total, width)),
        ]
        + [next_spec] * (n_f - 2),
        out_specs=[
            pl.BlockSpec((1, total, 2 * k_cols), lambda f: (f, 0, 0)),
            pl.BlockSpec((1, k_cols, 64), lambda f: (f, 0, 0)),
            whole((total, lanes)),
            pl.BlockSpec((None, 32, 2 * k_cols), lambda f: (f, 0, 0)),
            whole((32, width)),
        ],
        out_shape=[
            jax.ShapeDtypeStruct((n_f, total, 2 * k_cols), BF16),
            jax.ShapeDtypeStruct((n_f, k_cols, 64), F32),
            jax.ShapeDtypeStruct((total, lanes), BF16),
            jax.ShapeDtypeStruct((n_f, 32, 2 * k_cols), F32),
            jax.ShapeDtypeStruct((32, width), F32),
        ],
        scratch_shapes=[pltpu.VMEM((total, lanes), F32)],
        compiler_params=params(60),
        cost_estimate=cost(8 * total * 128 * 128, 8 * MIB),
        name="key_value_back",
    )
    input_back = pl.pallas_call(
        functools.partial(gx_kernel, n_f, depth),
        grid=(n_dp,),
        in_specs=[
            pl.BlockSpec((total, depth), lambda j: (0, j)),
            whole((n_f, total, 2 * k_cols)),
            pl.BlockSpec((n_f, 1, depth, 2 * k_cols), lambda j: (0, j, 0, q_cols // (2 * k_cols))),
            whole((total, lanes)),
            pl.BlockSpec((depth, lanes), lambda j: (j, 0)),
            pl.BlockSpec((total, depth), lambda j: (0, j)),
            whole((total, width)),
            whole((total, width)),
            whole((total, 1)),
            whole((n_dp, 1, depth)),
        ],
        out_specs=[whole((total, width)), pl.BlockSpec((1, depth), lambda j: (0, j))],
        out_shape=[
            jax.ShapeDtypeStruct((total, width), BF16),
            jax.ShapeDtypeStruct((1, width), F32),
        ],
        scratch_shapes=[pltpu.VMEM((n_dp, total, depth), F32), pltpu.VMEM((total, 1), F32)],
        compiler_params=params(60),
        cost_estimate=cost(2 * total * width * 1024, 30 * MIB),
        name="input_gradient",
    )
    def heads_to_input(g_keys, g_message, g_next, gu_q, gh_q):
        gkv, d_fk, gu, d_bkv_t, d_qkv_t = kv_back(
            g_keys, g_message, kv_natural, g_states, fk, cos_t, sin_t, u, b_kv_t, gu_q, h1,
            *g_next,
        )
        gx, dg1 = input_back(
            gh_q, gkv, w_qkv, gu, a_qkv, x, x, gx2, r1, gain_one.reshape(n_dp, 1, depth)
        )
        return gx, dg1, d_fk, d_bkv_t, d_qkv_t

    (gx, dg1, d_fk, d_bkv_t, d_qkv_t), spread_one = together(
        (heads_to_input, g_keys, g_message, g_next, gu_q, gh_q),
        (deal_out, result_one),
    )

    wide = pl.pallas_call(
        table_kernel,
        out_shape=jax.ShapeDtypeStruct((width, lanes), F32),
        compiler_params=pltpu.CompilerParams(vmem_limit_bytes=60 * MIB),
        name="table",
    )(d_fq.reshape(H * 64, 64), d_qkv_t, d_ao_t, d_bq_t, d_bo_t, dg1, dg2)
    kv_rows = KEY_VALUE_HEADS * 64
    d_bk = d_bkv_t[:, rank : 2 * rank, :k_cols].transpose(0, 2, 1).reshape(kv_rows, rank)
    d_bv = d_bkv_t[:, 2 * rank : 3 * rank, k_cols:].transpose(0, 2, 1).reshape(kv_rows, rank)
    narrow = jnp.concatenate(
        [d_fk.reshape(kv_rows, 64), d_bk, d_bv, jnp.zeros((kv_rows, lanes - 80), F32)], axis=1
    )
    wide = wide.reshape(n_all, width // n_all, lanes)
    narrow = narrow.reshape(n_all, kv_rows // n_all, lanes)
    table = jnp.concatenate([wide, narrow], axis=1)
    table, out_one = together(
        (halved, table), (lambda spread, order: deal_in(reordered(spread, order)), spread_one, inverse[1])
    )
    output = [out_zero, out_one]
    wide, narrow = table[: width // n_all], table[width // n_all :]
    shares = (
        wide[:, 64:96],
        wide[:, 96:112],
        narrow[:, 64:80],
        wide[:, :64],
        narrow[:, :64],
        wide[:, 112:114],
    )
    return (jnp.stack(output)[None], gx.reshape(1, micro, rows, width), *shares)


def solution(mesh):
    every = ("dp", "fsdp")
    blocks = P("dp", None, "fsdp", None)
    in_specs = (
        blocks,
        blocks,
        P(),
        P(),
        P("dp", "fsdp"),
        P("dp", "fsdp"),
        P("dp", "fsdp"),
        P("fsdp", "dp"),
        P("dp", "fsdp"),
        P("dp", "fsdp"),
        P("fsdp", "dp"),
    ) + (P(every, None),) * 6
    out_specs = (blocks, blocks) + (P(every, None),) * 6
    return jax.shard_map(shards, mesh=mesh, in_specs=in_specs, out_specs=out_specs, check_vma=False)
```

```python
import functools
import math

import jax
import jax.numpy as jnp
from jax import lax
from jax.experimental import pallas as pl
from jax.experimental.pallas import tpu as pltpu
from jax.sharding import PartitionSpec as P

H = 32
KEY_VALUE_HEADS = 8
REPEAT = H // KEY_VALUE_HEADS
HEAD_SIZE = 64
ADAPTER_RANK = 8
WIN = 64
AUG = 80
RANK_LANES = 128

EPSILON = 1e-05
ROPE_BASE = 500000.0
F32 = jnp.float32
BF16 = jnp.bfloat16
MIB = 1024 * 1024
X_PAIRS = [(i, i ^ 1) for i in range(4)]
Y_PAIRS = [(i, i ^ 2) for i in range(4)]


def dot(a, b):
    return lax.dot_general(a, b, (((1,), (0,)), ((), ())), preferred_element_type=F32)


def dot_nt(a, b):
    return lax.dot_general(a, b, (((1,), (1,)), ((), ())), preferred_element_type=F32)


def params(mib, semantics=("arbitrary",)):
    return pltpu.CompilerParams(vmem_limit_bytes=mib * MIB, dimension_semantics=semantics)


def cost(flops, bytes_accessed, transcendentals=0):
    return pl.CostEstimate(
        flops=int(flops), bytes_accessed=int(bytes_accessed), transcendentals=int(transcendentals)
    )


def whole(shape):
    return pl.BlockSpec(shape, lambda *_: (0,) * len(shape))


def after(value, *others):
    return lax.optimization_barrier((value, *others))[0]


def together(*jobs):
    arguments = lax.optimization_barrier([job[1:] for job in jobs])
    return lax.optimization_barrier([job[0](*args) for job, args in zip(jobs, arguments)])


def by_x(rows):
    return lax.ppermute(rows, "fsdp", X_PAIRS)


def by_y(rows):
    return lax.ppermute(rows, "fsdp", Y_PAIRS)


def rope_tables_t(positions):
    half_size = HEAD_SIZE // 2
    frequencies = jnp.exp(
        -(2.0 * jnp.arange(half_size, dtype=F32) / HEAD_SIZE) * math.log(ROPE_BASE)
    )
    angles = frequencies[:, None] * positions.astype(F32)[None, :]
    return jnp.cos(angles), jnp.sin(angles)


def rotate_t(head, cos_t, sin_t):
    a, b = head[:32], head[32:]
    return jnp.concatenate([a * cos_t - b * sin_t, b * cos_t + a * sin_t], axis=0)


def rotate_back_t(head, cos_t, sin_t):
    a, b = head[:32], head[32:]
    return jnp.concatenate([a * cos_t + b * sin_t, b * cos_t - a * sin_t], axis=0)


def half_softmax_t(scores):
    e = jnp.exp(scores - jnp.max(scores, axis=0, keepdims=True))
    return e * (1.0 / jnp.sum(e, axis=0, keepdims=True))


def features_t(mapped):
    return jnp.concatenate([half_softmax_t(mapped[:64]), half_softmax_t(mapped[64:])], axis=0)


def features_back_t(e, f):
    ef = e * f
    t1 = jnp.sum(ef[:64], axis=0, keepdims=True)
    t2 = jnp.sum(ef[64:], axis=0, keepdims=True)
    return (ef[:64] - e[:64] * t1) - (ef[64:] - e[64:] * t2)


def block_pieces(refs, place_ref, n_dp):
    if len(refs) == 9:
        own, x_mine, y_mine, dx_mine, dy_mine, x_other, y_other, dx_other, dy_other = refs
        shard, core = place_ref[0], place_ref[1]
        half = n_dp // 2
        mine, other = core * half, (1 - core) * half
        quarter = half // 2
        return [
            (shard, [(own, 0)]),
            (shard ^ 1, [(x_mine, mine), (x_other, other)]),
            (shard ^ 2, [(y_mine, mine), (y_other, other)]),
            (
                shard ^ 3,
                [
                    (dx_mine, mine),
                    (dy_mine, mine + quarter),
                    (dx_other, other),
                    (dy_other, other + quarter),
                ],
            ),
        ]
    return [(f, [(ref, 0)]) for f, ref in enumerate(refs)]


def project(h1_ref, u_ref, pieces, low_rank, depth):
    total = dot(u_ref[...], low_rank)
    for ref, start in pieces:
        count = ref.shape[0] * depth
        if isinstance(start, int):
            columns = h1_ref[:, start * depth : start * depth + count]
        else:
            columns = h1_ref[:, pl.ds(pl.multiple_of(start * depth, depth), count)]
        total += dot(columns, ref[...].reshape(count, ref.shape[2]))
    return total


def kv_kernel(kv_heads, micro, depth, n_dp, place_ref, h1_ref, u_ref, b_ref, cos_ref, sin_ref,
              f_ref, *refs):
    *w_refs, n_ref, tot_ref, msg_ref = refs
    rows = h1_ref.shape[0] // micro
    cos_t, sin_t = cos_ref[...], sin_ref[...]
    width = kv_heads * HEAD_SIZE
    for f, pieces in block_pieces(w_refs, place_ref, n_dp):
        kv_t = project(h1_ref, u_ref, pieces, b_ref[f], depth).T
        for g in range(kv_heads):
            head = f * kv_heads + g
            kr = rotate_t(kv_t[g * 64 : (g + 1) * 64], cos_t, sin_t).astype(BF16)
            v = kv_t[width + g * 64 : width + (g + 1) * 64].astype(BF16)
            pk = features_t(dot(f_ref[head], kr)).astype(BF16)
            natural = (
                jnp.concatenate([pk.astype(F32), kr.astype(F32), v.astype(F32)], axis=0).T
            ).astype(BF16)
            v_aug = jnp.concatenate([v, jnp.ones((AUG - 64, v.shape[1]), BF16)], axis=0)
            for m in range(micro):
                part = natural[m * rows : (m + 1) * rows]
                n_ref[head, m] = part
                sums = dot(v_aug[:, m * rows : (m + 1) * rows], part[:, :128])
                tot_ref[head, m] = sums.astype(BF16)
                msg_ref[head, m, :64] = part[rows - 64 :]
                tail = jnp.concatenate([sums[48:], jnp.zeros((16, 128), F32)], axis=0)
                msg_ref[head, m, 64:] = jnp.concatenate([sums[:48], tail], axis=1).astype(BF16)


def q_kernel(heads, depth, n_dp, place_ref, h1_ref, u_ref, b_ref, cos_ref, sin_ref, f_ref, *refs):
    *w_refs, qr_ref, pq_ref = refs
    cos_t, sin_t = cos_ref[...], sin_ref[...]
    for f, pieces in block_pieces(w_refs, place_ref, n_dp):
        q_t = project(h1_ref, u_ref, pieces, b_ref[f], depth).T
        for h in range(heads):
            head = f * heads + h
            qr = rotate_t(q_t[h * 64 : (h + 1) * 64], cos_t, sin_t).astype(BF16)
            pq = features_t(dot(f_ref[head], qr)).astype(BF16)
            if isinstance(head, int):
                qr_ref[head * 64 : (head + 1) * 64] = qr
                pq_ref[head * 128 : (head + 1) * 128] = pq
            else:
                qr_ref[pl.ds(pl.multiple_of(head * 64, 64), 64)] = qr
                pq_ref[pl.ds(pl.multiple_of(head * 128, 128), 128)] = pq


def pair_masks(has_prev):
    lane = lax.broadcasted_iota(jnp.int32, (64, REPEAT * 128), 1)
    row = lax.broadcasted_iota(jnp.int32, (64, REPEAT * 128), 0)
    low = (lane % 128) < 64
    ahead = row - lane % 64
    value = jnp.where(low, ahead - 1, -ahead)
    hidden = jnp.where(low, (1 - has_prev) * 1024, 0)
    return low, value >= 0, value - hidden >= 0


def heads_side(ref, size, start):
    return jnp.concatenate(
        [ref[h * size : (h + 1) * size, start : start + 128] for h in range(REPEAT)], axis=1
    )


def attend_kernel(micro, prev_ref, n_ref, msg_ref, qr_ref, pq_ref, *refs):
    *base_refs, o_ref, ot_ref, den_ref, s_ref = refs
    rows = n_ref.shape[2]
    low, mask_a, mask_first = pair_masks(prev_ref[0])
    low_row = (lax.broadcasted_iota(jnp.int32, (1, REPEAT * 128), 1) % 128) < 64
    key_lane = lax.broadcasted_iota(jnp.int32, (AUG, 128), 1) < 64
    for m in range(micro):
        ext = jnp.concatenate([msg_ref[0, m, :64], n_ref[0, m]], axis=0)
        ext_t = ext.astype(F32).T.astype(BF16)
        near = jnp.concatenate([msg_ref[0, m, 64:112, :128], msg_ref[0, m, 64:96, 128:]], axis=0)
        v_aug_all = jnp.concatenate([ext_t[192:256], jnp.ones((AUG - 64, rows + WIN), BF16)], axis=0)
        running = near.astype(F32)
        for base_ref in base_refs:
            running += base_ref[0, m].astype(F32)
        for p in range(rows // 128):
            start = m * rows + p * 128
            r0 = p * 128
            qr4 = heads_side(qr_ref, 64, start)
            pq4 = heads_side(pq_ref, 128, start)
            pk = ext[r0 : r0 + 128, :128]
            kr = ext[r0 : r0 + 192, 128:192]
            v_aug = v_aug_all[:, r0 : r0 + 128]
            zero = jnp.zeros_like(v_aug)
            spans = dot(
                jnp.concatenate(
                    [jnp.where(key_lane, v_aug, zero), jnp.where(key_lane, zero, v_aug)], axis=0
                ),
                pk,
            )
            if p == 0:
                running = running - spans[:AUG]
            state = jnp.concatenate([running, running + spans[:AUG]], axis=0).astype(BF16)
            running = running + spans[:AUG] + spans[AUG:]
            s_ref[0, m, p] = state
            from_state = dot(state, pq4)
            scores = dot(kr, qr4) * (1.0 / math.sqrt(HEAD_SIZE))
            linear = dot(pk, pq4)
            exp_a = jnp.exp(jnp.where(low, scores[:64], scores[128:]))
            exp_b = jnp.exp(scores[64:128])
            mask = mask_first if p == 0 else mask_a
            w_a = jnp.where(mask, exp_a, jnp.where(low, linear[:64], 0.0))
            w_b = jnp.where(mask_a, jnp.where(low, 0.0, linear[64:]), exp_b)
            den = (
                jnp.sum(w_a, axis=0, keepdims=True)
                + jnp.sum(w_b, axis=0, keepdims=True)
                + jnp.where(low_row, from_state[64:65], from_state[AUG + 64 : AUG + 65])
            )
            inv = 1.0 / den
            p_a = w_a * inv
            weights = jnp.concatenate(
                [jnp.where(low, p_a, 0.0), w_b * inv, jnp.where(low, 0.0, p_a)], axis=0
            ).astype(BF16)
            out = (
                dot(ext_t[192:256, r0 : r0 + 192], weights)
                + jnp.where(low, from_state[:64], from_state[AUG : AUG + 64]) * inv
            )
            for h in range(REPEAT):
                den_ref[0, h : h + 1, start : start + 128] = den[:, h * 128 : (h + 1) * 128]
            out_t = jnp.concatenate(
                [out[:, h * 128 : (h + 1) * 128] for h in range(REPEAT)], axis=0
            )
            ot_ref[:, start : start + 128] = out_t.astype(BF16)
            o_ref[start : start + 128, :] = out_t.T.astype(BF16)


def attend_back_kernel(micro, prev_ref, n_ref, msg_ref, s_ref, qr_ref, pq_ref, go_ref, ot_ref,
                       den_ref, f_ref, cos_ref, sin_ref,
                       gq_ref, df_ref, gn_ref, gs_ref, back_ref, total_ref,
                       gqr_ref, gmq_ref):
    rows = n_ref.shape[2]
    low, mask_a, mask_first = pair_masks(prev_ref[0])
    low_aug = (lax.broadcasted_iota(jnp.int32, (AUG, REPEAT * 128), 1) % 128) < 64
    low_feat = (lax.broadcasted_iota(jnp.int32, (128, REPEAT * 128), 1) % 128) < 64
    scale = 1.0 / math.sqrt(HEAD_SIZE)
    for m in range(micro):
        ext = jnp.concatenate([msg_ref[0, m, :64], n_ref[0, m]], axis=0)
        ext_t = ext.astype(F32).T.astype(BF16)
        tail = g_sum = None
        for p in range(rows // 128):
            start = m * rows + p * 128
            r0 = p * 128
            qr4 = heads_side(qr_ref, 64, start)
            pq4 = heads_side(pq_ref, 128, start)
            go4 = heads_side(go_ref, 64, start)
            o4 = heads_side(ot_ref, 64, start)
            den = jnp.concatenate(
                [den_ref[0, h : h + 1, start : start + 128] for h in range(REPEAT)], axis=1
            )
            inv = 1.0 / den
            pk = ext[r0 : r0 + 128, :128]
            kr = ext[r0 : r0 + 192, 128:192]
            v = ext[r0 : r0 + 192, 192:256]
            go_f = go4.astype(F32)
            delta = jnp.sum(go_f * o4.astype(F32), axis=0, keepdims=True)
            scores = dot(kr, qr4) * scale
            linear = dot(pk, pq4)
            g_p = dot(v, go4)
            mask = mask_first if p == 0 else mask_a
            exp_a = jnp.exp(jnp.where(low, scores[:64], scores[128:]))
            exp_b = jnp.exp(scores[64:128])
            p_a = jnp.where(mask, exp_a, jnp.where(low, linear[:64], 0.0)) * inv
            p_b = jnp.where(mask_a, jnp.where(low, 0.0, linear[64:]), exp_b) * inv
            weights = jnp.concatenate(
                [jnp.where(low, p_a, 0.0), p_b, jnp.where(low, 0.0, p_a)], axis=0
            ).astype(BF16)
            gw_a = (jnp.where(low, g_p[:64], g_p[128:]) - delta) * inv
            gw_b = (g_p[64:128] - delta) * inv
            gs_a = jnp.where(mask, gw_a * exp_a, 0.0)
            gs_b = jnp.where(mask_a, 0.0, gw_b * exp_b)
            g_scores = jnp.concatenate(
                [jnp.where(low, gs_a, 0.0), gs_b, jnp.where(low, 0.0, gs_a)], axis=0
            ).astype(BF16)
            g_linear = jnp.concatenate(
                [
                    jnp.where(mask_a, 0.0, jnp.where(low, gw_a, 0.0)),
                    jnp.where(mask_a, jnp.where(low, 0.0, gw_b), 0.0),
                ],
                axis=0,
            ).astype(BF16)
            go_aug = jnp.concatenate(
                [go_f * inv, -delta * inv, jnp.zeros((AUG - 65, REPEAT * 128), F32)], axis=0
            )
            go_aug_b = go_aug.astype(BF16)
            gqr = dot(ext_t[128:192, r0 : r0 + 192], g_scores) * scale
            state_t = s_ref[0, m, p].astype(F32).T.astype(BF16)
            gpq = dot(ext_t[:128, r0 : r0 + 128], g_linear) + jnp.where(
                low_feat, dot(state_t[:, :AUG], go_aug_b), dot(state_t[:, AUG:], go_aug_b)
            )
            zero = jnp.zeros_like(go_aug_b)
            g_spans = dot_nt(
                jnp.concatenate(
                    [jnp.where(low_aug, go_aug_b, zero), jnp.where(low_aug, zero, go_aug_b)], axis=0
                ),
                pq4,
            )
            gs_ref[0, m, p] = g_spans
            both = g_spans[:AUG] + g_spans[AUG:]
            g_sum = both if p == 0 else g_sum + both
            if p == 0:
                back_ref[0, m, 64:, :128] = g_spans[:AUG].astype(BF16)
            g_pk = dot_nt(g_linear, pq4)
            g_kr = dot_nt(g_scores, qr4) * scale
            g_v = dot_nt(weights, go4)
            g_keys = jnp.concatenate(
                [
                    jnp.concatenate([g_pk, jnp.zeros((64, 128), F32)], axis=0),
                    g_kr,
                    g_v,
                ],
                axis=1,
            )
            if p == 0:
                back_ref[0, m, :64] = g_keys[:64].astype(BF16)
            else:
                gn_ref[0, m, r0 - 64 : r0] = g_keys[:64] + tail
            gn_ref[0, m, r0 : r0 + 64] = g_keys[64:128]
            tail = g_keys[128:]
            if p == rows // 128 - 1:
                gn_ref[0, m, rows - 64 : rows] = tail
                total_ref[0, m] = g_sum.astype(BF16)
                back_ref[0, m, 64:, 128:] = g_sum.astype(BF16)
            pq_f = pq4.astype(F32)
            gmq = features_back_t(pq_f, gpq).astype(BF16)
            for h in range(REPEAT):
                gqr_ref[h * 64 : (h + 1) * 64, start : start + 128] = gqr[:, h * 128 : (h + 1) * 128]
                gmq_ref[h * 64 : (h + 1) * 64, start : start + 128] = gmq[:, h * 128 : (h + 1) * 128]
    cos_t, sin_t = cos_ref[...], sin_ref[...]
    grads = []
    for h in range(REPEAT):
        sl = slice(h * 64, (h + 1) * 64)
        gmq = gmq_ref[sl]
        df_ref[0, sl] = dot_nt(qr_ref[sl], gmq)
        grads.append(rotate_back_t(gqr_ref[sl] + dot(f_ref[h], gmq), cos_t, sin_t))
    gq_ref[0] = jnp.concatenate(grads, axis=0).T.astype(BF16)


def kv_back_kernel(kv_heads, micro, gn_ref, back_ref, n_ref, gs_ref, f_ref, cos_ref, sin_ref,
                   u_ref, b_ref, guq_ref, h1_ref, *refs):
    *next_refs, gkv_ref, df_ref, gu_ref, db_ref, dqkv_ref, acc_ref = refs
    rows = n_ref.shape[2]
    spans = rows // WIN
    cos_t, sin_t = cos_ref[...], sin_ref[...]
    keys, values = [], []
    unit = (lax.broadcasted_iota(jnp.int32, (64, AUG - 64), 1) == 0).astype(BF16)
    for g in range(kv_heads):
        parts = []
        for m in range(micro):
            natural = n_ref[g, m]
            later = [None] * spans
            after_here = back_ref[g, m, 64:, 128:].astype(F32)
            for ref in next_refs:
                after_here += ref[g, m].astype(F32)
            later[spans - 1] = after_here - back_ref[g, m, 64:, :128].astype(F32)
            later[spans - 2] = after_here
            for c in range(spans - 3, -1, -1):
                later[c] = later[c + 1] + gs_ref[g, m, (c + 2) // 2, ((c + 2) % 2) * AUG : ((c + 2) % 2 + 1) * AUG]
            for c in range(spans):
                part = natural[c * 64 : (c + 1) * 64]
                grad = gn_ref[g, m, c * 64 : (c + 1) * 64]
                if c == spans - 1:
                    grad = grad + back_ref[g, m, :64].astype(F32)
                big = later[c].astype(BF16)
                g_pk = dot(jnp.concatenate([part[:, 192:256], unit], axis=1), big)
                g_v = dot_nt(part[:, :128], big[:64])
                parts.append(
                    grad + jnp.concatenate([g_pk, jnp.zeros((64, 64), F32), g_v], axis=1)
                )
        grad_t = jnp.concatenate(parts, axis=0).T
        nat_t = jnp.concatenate([n_ref[g, m, :, :192] for m in range(micro)], axis=0).astype(F32).T
        gmk = features_back_t(nat_t[:128], grad_t[:128]).astype(BF16)
        df_ref[0, g * 64 : (g + 1) * 64] = dot_nt(nat_t[128:].astype(BF16), gmk)
        keys.append(rotate_back_t(grad_t[128:192] + dot(f_ref[g], gmk), cos_t, sin_t))
        values.append(grad_t[192:256])
    gkv = jnp.concatenate(keys + values, axis=0).T.astype(BF16)
    gkv_ref[0] = gkv
    db_ref[...] = dot(u_ref[...].astype(F32).T[:32].astype(BF16), gkv)
    rank_grad = dot_nt(gkv, b_ref[0])

    @pl.when(pl.program_id(0) == 0)
    def _():
        acc_ref[...] = guq_ref[...] + rank_grad

    @pl.when(pl.program_id(0) > 0)
    def _():
        acc_ref[...] += rank_grad

    @pl.when(pl.program_id(0) == pl.num_programs(0) - 1)
    def _():
        gu_ref[...] = acc_ref[...].astype(BF16)
        dqkv_ref[...] = dot(acc_ref[...].T[:32].astype(BF16), h1_ref[...])


def table_kernel(heads_ref, dqkv_ref, dao_ref, dbq_ref, dbo_ref, dg1_ref, dg2_ref, out_ref):
    width = dqkv_ref.shape[1]
    gains = jnp.concatenate([dg1_ref[...], dg2_ref[...], jnp.zeros((6, width), F32)], axis=0)
    rows = jnp.concatenate(
        [dqkv_ref[:24], dao_ref[:8], dbq_ref[:8], dbo_ref[:8], gains, jnp.zeros((8, width), F32)],
        axis=0,
    )
    out_ref[...] = jnp.concatenate([heads_ref[...], rows.T], axis=1)


def out_kernel(depth, n_dp, place_ref, o_ref, ao_ref, bo_ref, x_ref, gain_ref, *refs):
    *h2_refs, acc_ref = refs
    *w_refs, x2_ref, uo_ref, r2_ref = h2_refs[:-2]
    h2_refs = h2_refs[-2:]
    rows = h2_refs[0].shape[0]
    uo = dot(o_ref[...], ao_ref[...]).astype(BF16)
    uo_ref[...] = uo
    for j in range(n_dp):
        cols = slice(j * depth, (j + 1) * depth)
        acc_ref[j] = x_ref[:, cols].astype(F32) + dot_nt(uo, bo_ref[cols])
    halves = w_refs[0].shape[2] // depth
    block = halves * depth
    for f, pieces in block_pieces(w_refs, place_ref, n_dp):
        for ref, start in pieces:
            for i in range(ref.shape[0]):
                total = None
                for a in range(halves):
                    e0 = f * block + a * depth
                    if not isinstance(f, int):
                        e0 = pl.multiple_of(e0, depth)
                    term = dot(o_ref[:, pl.ds(e0, depth)], ref[i, :, a * depth : (a + 1) * depth])
                    total = term if total is None else total + term
                acc_ref[start + i] += total
    squares = 0.0
    for j in range(n_dp):
        x2 = acc_ref[j]
        x2_ref[:, j * depth : (j + 1) * depth] = x2
        squares += jnp.sum(x2 * x2, axis=1, keepdims=True)
    r2 = lax.rsqrt(squares * (1.0 / (n_dp * depth)) + EPSILON)
    r2_ref[...] = r2
    for j in range(n_dp):
        cols = slice(j * depth, (j + 1) * depth)
        h2 = (acc_ref[j] * r2 * gain_ref[:, cols]).astype(BF16)
        for m, h2_ref in enumerate(h2_refs):
            h2_ref[:, cols] = h2[m * rows : (m + 1) * rows]


def go_kernel(depth, gb_ref, w_ref, ao_ref, guo_ref, o_ref, go_ref, dao_ref):
    groups = w_ref.shape[1]
    halves = w_ref.shape[3] // depth
    guo = guo_ref[...]
    low_rank = dot_nt(ao_ref[...], guo)
    for a in range(halves):
        total = low_rank[a * depth : (a + 1) * depth]
        for j in range(groups):
            total += dot_nt(
                w_ref[0, j, :, a * depth : (a + 1) * depth], gb_ref[:, j * depth : (j + 1) * depth]
            )
        go_ref[a * depth : (a + 1) * depth] = total.astype(BF16)
    dao_ref[...] = dot(guo.astype(F32).T[:16].astype(BF16), o_ref[...])


def gx_query_kernel(shards, gq_ref, wq_ref, u_ref, b_ref, out_ref, gu_ref, db_ref):
    total = dot_nt(gq_ref[0], wq_ref[0, 0])
    for f in range(1, shards):
        total += dot_nt(gq_ref[f], wq_ref[f, 0])
    out_ref[...] = total

    @pl.when(pl.program_id(0) == 0)
    def _():
        u_t = u_ref[...].astype(F32).T[:32].astype(BF16)
        cols = gq_ref.shape[2]
        rank_grad = 0.0
        for f in range(shards):
            rank_grad += dot_nt(gq_ref[f], b_ref[f])
            db_ref[:, f * cols : (f + 1) * cols] = dot(u_t, gq_ref[f])
        gu_ref[...] = rank_grad


def gx_kernel(shards, depth, part_ref, gkv_ref, wkv_ref, gu_ref, a_ref, x_ref, x_all_ref,
              gx2_ref, r1_ref, gain_ref, gx_ref, dg_ref, gh_all, dot_ref):
    j = pl.program_id(0)
    last = pl.num_programs(0) - 1

    @pl.when(j == 0)
    def _():
        dot_ref[...] = jnp.zeros_like(dot_ref)

    total = part_ref[...] + dot_nt(gu_ref[...], a_ref[...])
    for f in range(shards):
        total += dot_nt(gkv_ref[f], wkv_ref[f, 0])
    gh_all[j] = total
    hx = total * x_ref[...].astype(F32)
    dg_ref[...] = jnp.sum(hx * r1_ref[...], axis=0, keepdims=True)
    dot_ref[...] += jnp.sum(hx * gain_ref[0], axis=1, keepdims=True)

    @pl.when(j == last)
    def _():
        count = gh_all.shape[0]
        r1 = r1_ref[...]
        back = r1 * r1 * r1 * dot_ref[...] * (1.0 / (count * depth))
        for i in range(count):
            cols = slice(i * depth, (i + 1) * depth)
            gx_ref[:, cols] = (
                gx2_ref[:, cols]
                + r1 * gain_ref[i] * gh_all[i]
                - x_all_ref[:, cols].astype(F32) * back
            ).astype(BF16)


def pack_attention_kernel(wq_ref, wk_ref, wv_ref, wo_ref, qkv_ref, out_ref):
    depth, q_cols = wq_ref.shape
    qkv_ref[:, :q_cols] = wq_ref[...]
    qkv_ref[:, q_cols:] = jnp.concatenate([wk_ref[...], wv_ref[...]], axis=1)
    for a in range(wo_ref.shape[0] // depth):
        out_ref[:, a * depth : (a + 1) * depth] = wo_ref[a * depth : (a + 1) * depth]


def pack_ffn_kernel(cuts, wg_ref, wu_ref, wd_ref, *refs):
    for ref, start, stop in zip(refs, cuts, cuts[1:]):
        count = stop - start
        ref[:, :count] = wg_ref[:, start:stop]
        ref[:, count : 2 * count] = wu_ref[:, start:stop]
        step = min(256, count)
        for at in range(0, count, step):
            ref[:, 2 * count + at : 2 * count + at + step] = (
                wd_ref[start + at : start + at + step].astype(F32).T.astype(BF16)
            )


def joined(refs):
    own_a, own_b, x_a, y_a, y_b, x_b = refs
    left = own_a[0].astype(F32) + x_a[0].astype(F32) + y_a[...].astype(F32)
    right = own_b[0].astype(F32) + y_b[0].astype(F32) + x_b[...].astype(F32)
    return jnp.concatenate([left, right], axis=1)


def result_kernel(count, x2_ref, valid_ref, *refs):
    *parts, out_ref = refs
    total = joined(parts) if count == 6 else parts[0][...]
    out_ref[...] = jnp.where(valid_ref[...] > 0, x2_ref[...] + total, 0.0).astype(BF16)


def mid_back_kernel(count, x2_ref, r2_ref, gain_ref, gy_ref, uo_ref, bo_ref, *refs):
    gx2_ref, gb_ref, guo_ref, dg_ref, dbo_ref = refs[-5:]
    parts = refs[:count]
    gh = joined(parts) if count == 6 else parts[0][...]
    x2, r2 = x2_ref[...], r2_ref[...]
    gx = gh * x2
    scaled = gh * gain_ref[...]
    mean = jnp.mean(scaled * x2, axis=1, keepdims=True)
    gx2 = gy_ref[...].astype(F32) + r2 * scaled - x2 * (r2 * r2 * r2 * mean)
    gx2_ref[...] = gx2
    gb = gx2.astype(BF16)
    gb_ref[...] = gb
    guo_ref[...] = dot(gb, bo_ref[...]).astype(BF16)
    dg = jnp.sum(gx * r2, axis=0, keepdims=True)
    dbo = dot(uo_ref[...].astype(F32).T[:16].astype(BF16), gb)

    @pl.when(pl.program_id(0) == 0)
    def _():
        dg_ref[...] = dg
        dbo_ref[...] = dbo

    @pl.when(pl.program_id(0) > 0)
    def _():
        dg_ref[...] += dg
        dbo_ref[...] += dbo


def row_copies(refs, rows_ref, sems, r):
    tile, width = rows_ref.shape[1:]
    half_tile, half = tile // 2, width // 2
    if len(refs) == 1:
        parts = [(refs[0].at[r * tile : (r + 1) * tile], rows_ref.at[r])]
    elif r == 0:
        parts = [(refs[i], rows_ref.at[0, i * half_tile : (i + 1) * half_tile]) for i in range(2)]
    else:
        parts = [(refs[2], rows_ref.at[1, :half_tile])]
        parts += [
            (refs[3 + i], rows_ref.at[1, half_tile:, i * half : (i + 1) * half]) for i in range(2)
        ]
    return [
        pltpu.make_async_copy(source, target, sems.at[r, i])
        for i, (source, target) in enumerate(parts)
    ]


def store_rows(value_ref, refs):
    if len(refs) == 1:
        refs[0][...] = value_ref[...].astype(BF16)
        return
    send_x, keep_x, send_y, keep_y = refs
    count, half = value_ref.shape[0] // 2, value_ref.shape[1] // 2
    keep_x[0] = value_ref[:count, :half].astype(BF16)
    send_x[0] = value_ref[count:, :half].astype(BF16)
    for here, ref in enumerate((keep_y, send_y)):

        @pl.when(pl.program_id(0) == here)
        def _(ref=ref):
            ref[0] = value_ref[:count, half:].astype(BF16)
            ref[1] = value_ref[count:, half:].astype(BF16)


def ffn_kernel(pieces, carries, wg_ref, wu_ref, wd_ref, *refs):
    h2_refs, gy_refs = refs[:pieces], refs[pieces : 2 * pieces]
    carried = refs[2 * pieces : 2 * pieces + carries]
    *out_refs, h2_ref, gy_ref, out_acc, gh_acc, h2_sems, gy_sems = refs[2 * pieces + carries :]
    r, j = pl.program_id(0), pl.program_id(1)
    copies = [
        row_copies(h2_refs, h2_ref, h2_sems, tile) + row_copies(gy_refs, gy_ref, gy_sems, tile)
        for tile in range(2)
    ]

    @pl.when((r == 0) & (j == 0))
    def _():
        for copy in copies[0] + copies[1]:
            copy.start()
        for copy in copies[0]:
            copy.wait()

    @pl.when((r == 1) & (j == 0))
    def _():
        for copy in copies[1]:
            copy.wait()

    h2, gy = h2_ref[r], gy_ref[r]
    shape = (wg_ref.shape[0] * wg_ref.shape[1], wg_ref.shape[2])
    wg, wu, wd = wg_ref[...].reshape(shape), wu_ref[...].reshape(shape), wd_ref[...].reshape(shape)
    gate = dot(h2, wg)
    up = dot(h2, wu)
    g_hid = dot(gy, wd)
    sig = 1.0 / (1.0 + jnp.exp(-gate))
    silu = gate * sig
    hid = (silu * up).astype(BF16)
    g_gate = (g_hid * up * sig * (1.0 + gate * (1.0 - sig))).astype(BF16)
    g_up = (g_hid * silu).astype(BF16)

    @pl.when(j == 0)
    def _():
        out, gh = dot_nt(hid, wd), dot_nt(g_gate, wg) + dot_nt(g_up, wu)
        if carries:
            out += carried[0][...].astype(F32)
            gh += carried[1][...].astype(F32)
        out_acc[...] = out
        gh_acc[...] = gh

    @pl.when(j > 0)
    def _():
        out_acc[...] += dot_nt(hid, wd)
        gh_acc[...] += dot_nt(g_gate, wg) + dot_nt(g_up, wu)

    @pl.when(j == pl.num_programs(1) - 1)
    def _():
        half = len(out_refs) // 2
        store_rows(out_acc, out_refs[:half])
        store_rows(gh_acc, out_refs[half:])


def ffn(tile, split, h2, gy, weights, *carried):
    total = sum(part.size for part in h2) // h2[0].shape[1]
    width = h2[0].shape[1]
    groups, depth, cols = weights.shape
    tiles = cols // (3 * tile)
    pieces = len(h2)
    row_tile = total // 2
    row_spec = pl.BlockSpec((row_tile, width), lambda r, j: (r, 0))

    def weight_spec(kind):
        return pl.BlockSpec((groups, depth, tile), lambda r, j: (0, 0, kind * tiles + j))

    piece_specs = [pl.BlockSpec(memory_space=pl.ANY)] * pieces
    if split and pieces > 1:
        count, half = row_tile // 2, width // 2
        moving = pl.BlockSpec((1, count, half), lambda r, j: (r, 0, 0))
        fixed = pl.BlockSpec((2, count, half), lambda r, j: (0, 0, 0))
        out_specs = [moving, moving, fixed, fixed] * 2
        out_shape = [jax.ShapeDtypeStruct((2, count, half), BF16)] * 8
    else:
        out_specs = [row_spec, row_spec]
        out_shape = [jax.ShapeDtypeStruct((total, width), BF16)] * 2
    outs = pl.pallas_call(
        functools.partial(ffn_kernel, pieces, len(carried)),
        grid=(total // row_tile, tiles),
        in_specs=[weight_spec(0), weight_spec(1), weight_spec(2)]
        + piece_specs * 2
        + [row_spec] * len(carried),
        out_specs=out_specs,
        out_shape=out_shape,
        scratch_shapes=[pltpu.VMEM((2, row_tile, width), BF16)] * 2
        + [pltpu.VMEM((row_tile, width), F32)] * 2
        + [pltpu.SemaphoreType.DMA((2, 3))] * 2,
        compiler_params=params(60, ("arbitrary", "arbitrary")),
        cost_estimate=cost(4 * total * width * cols, 2 * width * cols * (total // row_tile) + 12 * total * width),
        name="feed_forward",
    )(weights, weights, weights, *h2, *gy, *carried)
    return (outs[: len(outs) // 2], outs[len(outs) // 2 :]) if split else outs


def gather_first(rows, size):
    if size != 4:
        return (lax.all_gather(rows, "fsdp", axis=0, tiled=True),)
    return rows, by_x(rows), by_y(rows)


def gather_second(*first):
    if len(first) == 1:
        return first
    rows, from_x, from_y = first
    half = rows.shape[1] // 2
    return rows, from_x, from_y, by_x(from_y[:, :half]), by_y(from_x[:, half:])


def scatter_first(*parts, size):
    if size != 4:
        (part,) = parts
        part = part.reshape(size, part.shape[0] // size, part.shape[1])
        return (lax.all_to_all(part, "fsdp", split_axis=0, concat_axis=0, tiled=True),)
    send_x, keep_x, send_y, keep_y = parts
    return keep_x, keep_y, by_x(send_x), by_y(send_y)


def pass_on_kernel(keep_x, from_x, keep_y, from_y, a_ref, b_ref):
    a_ref[...] = (keep_x[...].astype(F32) + from_x[...].astype(F32)).astype(BF16)
    b_ref[...] = (keep_y[...].astype(F32) + from_y[...].astype(F32)).astype(BF16)


def scatter_second(*first):
    if len(first) == 1:
        return [jnp.sum(first[0].astype(F32), axis=0)]
    keep_x, keep_y, from_x, from_y = first
    _, count, half = keep_x.shape
    second = pl.BlockSpec((None, count, half), lambda _: (1, 0, 0))
    a_pass, b_pass = pl.pallas_call(
        pass_on_kernel,
        grid=(1,),
        in_specs=[second] * 4,
        out_specs=[pl.BlockSpec((count, half), lambda _: (0, 0))] * 2,
        out_shape=[jax.ShapeDtypeStruct((count, half), BF16)] * 2,
        compiler_params=params(60),
        name="pass_on",
    )(keep_x, from_x, keep_y, from_y)
    return [keep_x, keep_y, from_x, by_y(a_pass), from_y, by_x(b_pass)]


def term_specs(terms, row_tile, width):
    full = pl.BlockSpec((row_tile, width), lambda r: (r, 0))
    if len(terms) == 1:
        return [full]
    half = width // 2
    row = pl.BlockSpec((row_tile, half), lambda r: (r, 0))
    first = pl.BlockSpec((1, row_tile, half), lambda r: (0, r, 0))
    return [first, first, first, row, first, row]


def pair_swap(part):
    return lax.ppermute(part, "dp", [(i, i ^ 1) for i in range(lax.axis_size("dp"))])


def columns_share(block, size, group):
    half = block.shape[0] // 2
    return block if size != 4 else lax.dynamic_slice_in_dim(block, group % 2 * half, half, 0)


def columns_first(mine, size):
    if size != 4:
        return (lax.all_gather(mine, "fsdp", axis=0, tiled=False),)
    return by_x(mine), by_y(mine)


def columns_second(*first):
    if len(first) == 1:
        return first
    from_x, from_y = first
    share = from_x.shape[0] // 2
    return (
        from_x, from_y, by_x(from_y[:share]), by_y(from_x[share:]),
        pair_swap(from_x), pair_swap(from_y),
    )


def columns_third(block, *second):
    if len(second) == 1:
        return [second[0][f] for f in range(second[0].shape[0])]
    from_x, from_y, diagonal_x, diagonal_y, other_x, other_y = second
    return [
        block, from_x, from_y, diagonal_x, diagonal_y,
        other_x, other_y, pair_swap(diagonal_x), pair_swap(diagonal_y),
    ]


def assembled(pieces, group, shard):
    if len(pieces) != 9:
        return jnp.stack(pieces)
    block = pieces[0]
    half = block.shape[0] // 2
    core = group % 2
    out = jnp.broadcast_to(block[None], (4,) + block.shape)

    def put(out, part, f, at):
        return lax.dynamic_update_slice(out, part[None], (f, at, 0, 0))

    masks = ((1, 0), (2, 0), (3, 0), (3, half // 2))
    for side, at in ((pieces[1:5], core * half), (pieces[5:], (1 - core) * half)):
        for part, (mask, offset) in zip(side, masks):
            out = put(out, part, shard ^ mask, at + offset)
    return out


def shifted(array, size, direction):
    moved = []
    for step in range(2, size):
        if direction > 0:
            perm = [(i, i + step) for i in range(size - step)]
        else:
            perm = [(i + step, i) for i in range(size - step)]
        moved.append(lax.ppermute(array, "fsdp", perm))
    return moved


def deal_out(rows):
    count, width = rows.shape
    groups = lax.axis_size("dp")
    pieces = rows.reshape(groups, count // groups, width)
    return lax.all_to_all(pieces, "dp", split_axis=0, concat_axis=0, tiled=True)


def reorder_kernel(at_ref, in_ref, out_ref):
    for j in range(out_ref.shape[0]):
        out_ref[j] = in_ref[at_ref[j]]


def reordered(spread, order):
    return pl.pallas_call(
        reorder_kernel,
        in_specs=[pl.BlockSpec(memory_space=pltpu.SMEM), pl.BlockSpec(memory_space=pltpu.VMEM)],
        out_specs=pl.BlockSpec(memory_space=pltpu.VMEM),
        out_shape=jax.ShapeDtypeStruct(spread.shape, spread.dtype),
        compiler_params=pltpu.CompilerParams(vmem_limit_bytes=60 * MIB),
        name="reorder",
    )(order, spread)


def deal_in(ordered):
    groups, share, width = ordered.shape
    settled = lax.all_to_all(ordered, "dp", split_axis=0, concat_axis=0, tiled=True)
    return settled.reshape(groups * share, width)


def halved(table):
    n_dp, n_f = lax.axis_size("dp"), lax.axis_size("fsdp")
    dp_bits, f_bits = n_dp.bit_length() - 1, n_f.bit_length() - 1
    bits = [("dp", b) for b in range(dp_bits)][::-1] + [("fsdp", b) for b in range(f_bits)][::-1]
    left = table.reshape((2,) * len(bits) + table.shape[1:])
    order = [("dp", 0)] + [("fsdp", b) for b in range(f_bits)] + [("dp", b) for b in range(1, dp_bits)]
    for axis, bit in order:
        at = bits.index((axis, bit))
        bits.pop(at)
        mine = (lax.axis_index(axis) >> bit) & 1
        keep = lax.dynamic_index_in_dim(left, mine, at, keepdims=False)
        send = lax.dynamic_index_in_dim(left, 1 - mine, at, keepdims=False).astype(BF16)
        perm = [(i, i ^ (1 << bit)) for i in range(lax.axis_size(axis))]
        left = keep + lax.ppermute(send, axis, perm).astype(F32)
    return left


def shards(
    inputs, cotangent, lengths, dealing, wq, wk, wv, wo, wg, wu, wd,
    down_ad, up_qo, up_kv, fmap_q, fmap_k, gains,
):
    n_dp = lax.axis_size("dp")
    n_f = lax.axis_size("fsdp")
    group = lax.axis_index("dp")
    quarter = lax.axis_index("fsdp")
    micro, rows, width = inputs.shape[1:]
    total = micro * rows
    depth = wq.shape[0]
    q_cols, k_cols = wq.shape[1], wk.shape[1]
    kv_heads = k_cols // HEAD_SIZE
    heads = q_cols // HEAD_SIZE
    halves = wo.shape[0] // depth
    n_all = n_dp * n_f
    x = inputs[0].reshape(total, width)

    small_parts = [down_ad, up_qo, up_kv, fmap_q, fmap_k, gains]
    flat = jnp.concatenate([part.reshape(-1) for part in small_parts])
    small_rows = -(-flat.shape[0] // (16 * 128)) * 16
    flat = jnp.pad(flat, (0, small_rows * 128 - flat.shape[0])).reshape(1, small_rows, 128)
    small = lax.all_gather(flat.reshape(small_rows, 128), "dp", axis=0, tiled=False)
    small = lax.all_gather(small, "fsdp", axis=0, tiled=False)
    small = small.transpose(1, 0, 2, 3).reshape(n_all, small_rows * 128)
    at = 0
    fetched = []
    for part in small_parts:
        fetched.append(
            small[:, at : at + part.size].reshape((n_all * part.shape[0],) + part.shape[1:])
        )
        at += part.size
    down_ad, up_qo, up_kv, fmap_q, fmap_k, gains = fetched

    pack_cols = q_cols + 2 * k_cols
    w_qkv, w_out = pl.pallas_call(
        pack_attention_kernel,
        out_shape=[
            jax.ShapeDtypeStruct((depth, pack_cols), BF16),
            jax.ShapeDtypeStruct((depth, q_cols), BF16),
        ],
        compiler_params=pltpu.CompilerParams(vmem_limit_bytes=60 * MIB),
        name="pack_attention",
    )(wq, wk, wv, wo)
    w_qkv = lax.all_gather(w_qkv, "dp", axis=0, tiled=False)
    w_out = lax.all_gather(w_out, "dp", axis=0, tiled=False)
    near, spread = together(
        (functools.partial(columns_first, size=n_f), columns_share(w_qkv, n_f, group)),
        (deal_out, after(cotangent[0].reshape(total, width), small)),
    )
    share_micro = group * (total // n_dp) // rows
    order = lax.dynamic_index_in_dim(dealing, share_micro, 0, keepdims=False)

    gain_one = gains[:, 0].astype(F32)
    gain_two = gains[:, 1].astype(F32)

    hidden = wg.shape[1]
    tile = hidden // 4
    cuts = (0, 3 * tile, hidden)
    w_ffn = pl.pallas_call(
        functools.partial(pack_ffn_kernel, cuts),
        out_shape=[
            jax.ShapeDtypeStruct((depth, 3 * (stop - start)), BF16)
            for start, stop in zip(cuts, cuts[1:])
        ],
        compiler_params=pltpu.CompilerParams(vmem_limit_bytes=60 * MIB),
        name="pack_feed_forward",
    )(wg, wu, wd)
    positions = quarter * rows + jnp.arange(rows, dtype=jnp.int32)
    seq_len = lax.dynamic_index_in_dim(lengths, group, 0, keepdims=False)
    valid = (positions[None, :] < seq_len[:, None]).reshape(total, 1)

    xf = x.astype(F32)
    r1 = lax.rsqrt(jnp.mean(xf * xf, axis=-1, keepdims=True) + EPSILON)
    h1 = (xf * r1 * gain_one).astype(BF16)
    rank = ADAPTER_RANK
    lanes = RANK_LANES
    a_qkv = jnp.pad(down_ad[:, : 3 * rank], ((0, 0), (0, lanes - 3 * rank)))
    a_o = jnp.pad(down_ad[:, 3 * rank :], ((0, 0), (0, lanes - rank)))
    u = dot(h1, a_qkv).astype(BF16)
    b_q = up_qo[:, :rank].reshape(n_f, q_cols, rank)
    b_k = up_kv[:, :rank].reshape(n_f, k_cols, rank)
    b_v = up_kv[:, rank:].reshape(n_f, k_cols, rank)
    b_o = jnp.pad(up_qo[:, rank:], ((0, 0), (0, lanes - rank)))

    def placed(block, at):
        return jnp.pad(block.transpose(0, 2, 1), ((0, 0), (at, lanes - at - rank), (0, 0)))

    b_q_t = placed(b_q, 0)
    b_kv_t = jnp.concatenate([placed(b_k, rank), placed(b_v, 2 * rank)], axis=2)
    fq = fmap_q.reshape(H, HEAD_SIZE, HEAD_SIZE)
    fk = fmap_k.reshape(KEY_VALUE_HEADS, HEAD_SIZE, HEAD_SIZE)
    fq_t = jnp.concatenate([fq.transpose(0, 2, 1), -fq.transpose(0, 2, 1)], axis=1)
    fk_t = jnp.concatenate([fk.transpose(0, 2, 1), -fk.transpose(0, 2, 1)], axis=1)
    cos_t, sin_t = rope_tables_t(jnp.tile(positions, micro))
    pairs = rows // 128
    prepared = (h1, u, a_qkv, a_o, b_q_t, b_kv_t, b_o, fq, fk, fq_t, fk_t, cos_t, sin_t)
    inverse = jnp.argsort(dealing, axis=1).astype(jnp.int32)
    prepared += (inverse,)
    second, out_near, cot, prepared = together(
        (columns_second, *near),
        (functools.partial(columns_first, size=n_f), columns_share(w_out, n_f, group)),
        (lambda spread, order: deal_in(reordered(spread, order)), spread, order),
        (lambda *arrays: arrays, *prepared),
    )
    h1, u, a_qkv, a_o, b_q_t, b_kv_t, b_o, fq, fk, fq_t, fk_t, cos_t, sin_t, inverse = prepared
    fetched_ffn = [lax.all_gather(after(w_ffn[0], cot), "dp", axis=0, tiled=False)]
    (qkv_pieces,) = together((columns_third, w_qkv, *second))

    place = jnp.stack([quarter, group % 2]).astype(jnp.int32)
    smem = pl.BlockSpec(memory_space=pltpu.SMEM)
    vmem = pl.BlockSpec(memory_space=pltpu.VMEM)

    def columns(pieces, size, at):
        return [
            pl.BlockSpec(part.shape[:2] + (size,), lambda _: (0, 0, at), pipeline_mode=pl.Buffered(1))
            for part in pieces
        ]

    def key_values(h1, u, *pieces):
        return pl.pallas_call(
            functools.partial(kv_kernel, kv_heads, micro, depth, n_dp),
            grid=(1,),
            in_specs=[smem] + [vmem] * 6 + columns(pieces, 2 * k_cols, q_cols // (2 * k_cols)),
            out_specs=[vmem] * 3,
            out_shape=[
                jax.ShapeDtypeStruct((KEY_VALUE_HEADS, micro, rows, 256), BF16),
                jax.ShapeDtypeStruct((KEY_VALUE_HEADS, micro, AUG, 128), BF16),
                jax.ShapeDtypeStruct((KEY_VALUE_HEADS, micro, 112, 256), BF16),
            ],
            compiler_params=params(40),
            cost_estimate=cost(4 * total * width * k_cols * n_f, 2 * (total * width + 2 * width * k_cols * n_f), 128 * 8 * total),
            name="key_value",
        )(place, h1, u, b_kv_t, cos_t, sin_t, fk_t, *pieces)

    def queries(h1, u, *pieces):
        return pl.pallas_call(
            functools.partial(q_kernel, heads, depth, n_dp),
            grid=(1,),
            in_specs=[smem] + [vmem] * 6 + columns(pieces, q_cols, 0),
            out_specs=[vmem, vmem],
            out_shape=[
                jax.ShapeDtypeStruct((H * 64, total), BF16),
                jax.ShapeDtypeStruct((H * 128, total), BF16),
            ],
            compiler_params=params(40),
            cost_estimate=cost(2 * total * width * q_cols * n_f, 2 * (total * width + width * q_cols * n_f + 3 * total * 2048), 128 * 32 * total),
            name="query",
        )(place, h1, u, b_q_t, cos_t, sin_t, fq_t, *pieces)

    forward_one = [(i, i + 1) for i in range(n_f - 1)]
    backward_one = [(i + 1, i) for i in range(n_f - 1)]

    gy_both = jnp.where(valid, cot, jnp.zeros_like(cot))
    gy = [gy_both[m * rows : (m + 1) * rows] for m in range(micro)]
    gather = functools.partial(gather_first, size=n_f)
    (kv_natural, totals, message), out_second = together(
        (key_values, h1, u, *qkv_pieces), (columns_second, *out_near)
    )

    def send_on(message, totals):
        return lax.ppermute(message, "fsdp", forward_one), shifted(totals, n_f, 1)

    (q_rot, q_feat), (message, bases) = together(
        (queries, h1, u, *qkv_pieces), (send_on, message, totals)
    )
    part = after(w_ffn[1], q_rot)
    fetched_ffn.append(lax.all_gather(part, "dp", axis=0, tiled=False))
    w_ffn = fetched_ffn

    has_prev = (quarter > 0).astype(jnp.int32).reshape(1)
    g4 = REPEAT * 64
    prev_spec = smem
    n_spec = pl.BlockSpec((1, micro, rows, 256), lambda g: (g, 0, 0, 0))
    message_spec = pl.BlockSpec((1, micro, 112, 256), lambda g: (g, 0, 0, 0))
    back_spec = pl.BlockSpec((1, micro, 64 + AUG, 256), lambda g: (g, 0, 0, 0))
    state_spec = pl.BlockSpec((1, micro, pairs, 2 * AUG, 128), lambda g: (g, 0, 0, 0, 0))
    head_spec = pl.BlockSpec((g4, total), lambda g: (g, 0))
    feat_spec = pl.BlockSpec((2 * g4, total), lambda g: (g, 0))
    den_spec = pl.BlockSpec((1, 8, total), lambda g: (g, 0, 0))
    base_spec = pl.BlockSpec((1, micro, AUG, 128), lambda g: (g, 0, 0, 0))
    attend_flops = H * total * 2 * (192 * 64 + 128 * 128 + 160 * 128 + 192 * 64)
    attend = pl.pallas_call(
        functools.partial(attend_kernel, micro),
        grid=(KEY_VALUE_HEADS,),
        in_specs=[
            prev_spec,
            n_spec,
            message_spec,
            head_spec,
            feat_spec,
        ]
        + [base_spec] * (n_f - 2),
        out_specs=[pl.BlockSpec((total, g4), lambda g: (0, g)), head_spec, den_spec, state_spec],
        out_shape=[
            jax.ShapeDtypeStruct((total, H * 64), BF16),
            jax.ShapeDtypeStruct((H * 64, total), BF16),
            jax.ShapeDtypeStruct((KEY_VALUE_HEADS, 8, total), F32),
            jax.ShapeDtypeStruct((KEY_VALUE_HEADS, micro, pairs, 2 * AUG, 128), BF16),
        ],
        compiler_params=params(60),
        cost_estimate=cost(attend_flops, 14 * MIB, 128 * H * total),
        name="attend",
    )
    (o, o_t, den, states), gy_first, out_pieces = together(
        (attend, has_prev, kv_natural, message, q_rot, q_feat, *bases),
        (gather, gy[0]),
        (columns_third, w_out, *out_second),
    )
    project_out = pl.pallas_call(
        functools.partial(out_kernel, depth, n_dp),
        grid=(1,),
        in_specs=[smem] + [vmem] * 5 + columns(out_pieces, q_cols, 0),
        out_specs=[vmem] * (3 + micro),
        out_shape=[
            jax.ShapeDtypeStruct((total, width), F32),
            jax.ShapeDtypeStruct((total, lanes), BF16),
            jax.ShapeDtypeStruct((total, 1), F32),
        ]
        + [jax.ShapeDtypeStruct((rows, width), BF16)] * micro,
        scratch_shapes=[pltpu.VMEM((n_dp, total, depth), F32)],
        compiler_params=params(60),
        cost_estimate=cost(2 * total * width * H * 64, 20 * MIB),
        name="output_projection",
    )
    (x2, uo, r2, *h2), gy_zero = together(
        (project_out, place, o, a_o, b_o, x, gain_two.reshape(1, width), *out_pieces),
        (gather_second, *gy_first),
    )
    gather = functools.partial(gather_first, size=n_f)

    def assemble(*pieces):
        return assembled(pieces, group, quarter)

    h2_first, w_qkv = together((gather, h2[0]), (assemble, *qkv_pieces))
    h2_zero, w_out = together((gather_second, *h2_first), (assemble, *out_pieces))

    def piece(array, m):
        return array[m * rows : (m + 1) * rows]

    row_tile = min(128, rows)

    def finish(m, terms):
        return pl.pallas_call(
            functools.partial(result_kernel, len(terms)),
            grid=(rows // row_tile,),
            in_specs=[
                pl.BlockSpec((row_tile, width), lambda r: (m * (rows // row_tile) + r, 0)),
                pl.BlockSpec((row_tile, 1), lambda r: (m * (rows // row_tile) + r, 0)),
            ]
            + term_specs(terms, row_tile, width),
            out_specs=pl.BlockSpec((row_tile, width), lambda r: (r, 0)),
            out_shape=jax.ShapeDtypeStruct((rows, width), BF16),
            compiler_params=params(60),
            cost_estimate=cost(4 * rows * width, 10 * rows * width),
            name="result",
        )(x2, valid_rows, *terms)

    def mid_back(m, terms, gy, *whole_arrays):
        here = pl.BlockSpec((row_tile, width), lambda r: (m * (rows // row_tile) + r, 0))
        thin = pl.BlockSpec((row_tile, lanes), lambda r: (m * (rows // row_tile) + r, 0))
        count = 6 + len(terms)
        return pl.pallas_call(
            functools.partial(mid_back_kernel, len(terms)),
            grid=(rows // row_tile,),
            in_specs=[
                here,
                pl.BlockSpec((row_tile, 1), lambda r: (m * (rows // row_tile) + r, 0)),
                whole((1, width)),
                pl.BlockSpec((row_tile, width), lambda r: (r, 0)),
                thin,
                whole((width, lanes)),
            ]
            + term_specs(terms, row_tile, width)
            + [pl.BlockSpec(memory_space=pl.ANY)] * len(whole_arrays),
            out_specs=[here, here, thin, whole((1, width)), whole((16, width))],
            out_shape=[
                jax.ShapeDtypeStruct((total, width), F32),
                jax.ShapeDtypeStruct((total, width), BF16),
                jax.ShapeDtypeStruct((total, lanes), BF16),
                jax.ShapeDtypeStruct((1, width), F32),
                jax.ShapeDtypeStruct((16, width), F32),
            ],
            input_output_aliases={count + i: i for i in range(len(whole_arrays))},
            compiler_params=params(60),
            cost_estimate=cost(20 * rows * width, 16 * rows * width),
            name="mid_back",
        )(x2, r2, gain_two.reshape(1, width), gy, uo, b_o, *terms, *whole_arrays)

    valid_rows = valid.astype(jnp.int32)
    def feed(split):
        def run(h2, gy, *carried):
            return ffn(tile, split, h2, gy, w_ffn[1 if split else 0], *carried)

        return run

    scatter = functools.partial(scatter_first, size=n_f)
    head_zero, h2_first, gy_first = together(
        (feed(False), h2_zero, gy_zero), (gather, h2[1]), (gather, gy[1])
    )
    (down_zero, gh_zero), h2_one, gy_one = together(
        (feed(True), h2_zero, gy_zero, *head_zero),
        (gather_second, *h2_first),
        (gather_second, *gy_first),
    )
    head_one, gh_zero_terms, down_zero_terms = together(
        (feed(False), h2_one, gy_one), (scatter, *gh_zero), (scatter, *down_zero)
    )
    (down_one, gh_one), gh_zero_terms, down_zero_terms = together(
        (feed(True), h2_one, gy_one, *head_one),
        (scatter_second, *gh_zero_terms),
        (scatter_second, *down_zero_terms),
    )

    go_back = pl.pallas_call(
        functools.partial(go_kernel, depth),
        grid=(n_f,),
        in_specs=[
            whole((total, width)),
            pl.BlockSpec((1, n_dp, depth, q_cols), lambda f: (f, 0, 0, 0)),
            pl.BlockSpec((q_cols, lanes), lambda f: (f, 0)),
            whole((total, lanes)),
            pl.BlockSpec((total, q_cols), lambda f: (0, f)),
        ],
        out_specs=[
            pl.BlockSpec((q_cols, total), lambda f: (f, 0)),
            pl.BlockSpec((16, q_cols), lambda f: (0, f)),
        ],
        out_shape=[
            jax.ShapeDtypeStruct((H * 64, total), BF16),
            jax.ShapeDtypeStruct((16, H * 64), F32),
        ],
        compiler_params=params(60),
        cost_estimate=cost(2 * total * width * H * 64, 12 * MIB),
        name="output_projection_back",
    )

    attend_back = pl.pallas_call(
        functools.partial(attend_back_kernel, micro),
        grid=(KEY_VALUE_HEADS,),
        in_specs=[
            prev_spec,
            n_spec,
            message_spec,
            state_spec,
            head_spec,
            feat_spec,
            head_spec,
            head_spec,
            den_spec,
            pl.BlockSpec((REPEAT, 64, 64), lambda g: (g, 0, 0)),
            whole((32, total)),
            whole((32, total)),
        ],
        out_specs=[
            pl.BlockSpec((1, total, g4), lambda g: (g * g4 // q_cols, 0, g % (q_cols // g4))),
            pl.BlockSpec((1, g4, 64), lambda g: (g, 0, 0)),
            n_spec,
            state_spec,
            back_spec,
            base_spec,
        ],
        out_shape=[
            jax.ShapeDtypeStruct((n_f, total, q_cols), BF16),
            jax.ShapeDtypeStruct((KEY_VALUE_HEADS, g4, 64), F32),
            jax.ShapeDtypeStruct((KEY_VALUE_HEADS, micro, rows, 256), F32),
            jax.ShapeDtypeStruct((KEY_VALUE_HEADS, micro, pairs, 2 * AUG, 128), F32),
            jax.ShapeDtypeStruct((KEY_VALUE_HEADS, micro, 64 + AUG, 256), BF16),
            jax.ShapeDtypeStruct((KEY_VALUE_HEADS, micro, AUG, 128), BF16),
        ],
        scratch_shapes=[pltpu.VMEM((g4, total), F32), pltpu.VMEM((g4, total), BF16)],
        compiler_params=params(60),
        cost_estimate=cost(3 * attend_flops, 24 * MIB, 128 * H * total),
        name="attend_back",
    )
    gh_one_terms, zero, result_zero = together(
        (scatter, *gh_one),
        (functools.partial(mid_back, 0), gh_zero_terms, gy[0]),
        (functools.partial(finish, 0), down_zero_terms),
    )
    (gh_one_terms,) = together((scatter_second, *gh_one_terms))

    def norm_to_output(gh_one, gy_one, *zero):
        gx2, gb, guo, *one = mid_back(1, gh_one, gy_one, *zero[:3])
        go_t, d_ao_t = go_back(gb, w_out, a_o, guo, o)
        return gx2, go_t, d_ao_t, zero[3] + one[0], zero[4] + one[1]

    (gx2, go_t, d_ao_t, dg2, d_bo_t), down_one_terms = together(
        (norm_to_output, gh_one_terms, gy[1], *zero), (scatter, *down_one)
    )
    back, down_one_terms, spread_zero = together(
        (attend_back, has_prev, kv_natural, message, states, q_rot, q_feat, go_t, o_t, den, fq, cos_t, sin_t),
        (scatter_second, *down_one_terms),
        (deal_out, result_zero),
    )
    gq, d_fq, g_keys, g_states, g_message, g_total = back

    query_part = pl.pallas_call(
        functools.partial(gx_query_kernel, n_f),
        grid=(n_dp,),
        in_specs=[
            whole((n_f, total, q_cols)),
            pl.BlockSpec((n_f, 1, depth, q_cols), lambda j: (0, j, 0, 0)),
            whole((total, lanes)),
            whole((n_f, lanes, q_cols)),
        ],
        out_specs=[
            pl.BlockSpec((total, depth), lambda j: (0, j)),
            whole((total, lanes)),
            whole((32, H * 64)),
        ],
        out_shape=[
            jax.ShapeDtypeStruct((total, width), F32),
            jax.ShapeDtypeStruct((total, lanes), F32),
            jax.ShapeDtypeStruct((32, H * 64), F32),
        ],
        compiler_params=params(60),
        cost_estimate=cost(2 * total * width * 2048, 16 * MIB),
        name="query_input_gradient",
    )

    def exchange(g_message, g_total):
        return lax.ppermute(g_message, "fsdp", backward_one), shifted(g_total, n_f, -1)

    (gh_q, gu_q, d_bq_t), (g_message, g_next), out_zero, result_one = together(
        (query_part, gq, w_qkv, u, b_q_t),
        (exchange, g_message, g_total),
        (lambda spread, order: deal_in(reordered(spread, order)), spread_zero, inverse[0]),
        (functools.partial(finish, 1), down_one_terms),
    )

    next_spec = pl.BlockSpec((kv_heads, micro, AUG, 128), lambda f: (f, 0, 0, 0))
    kv_back = pl.pallas_call(
        functools.partial(kv_back_kernel, kv_heads, micro),
        grid=(n_f,),
        in_specs=[
            pl.BlockSpec((kv_heads, micro, rows, 256), lambda f: (f, 0, 0, 0)),
            pl.BlockSpec((kv_heads, micro, 64 + AUG, 256), lambda f: (f, 0, 0, 0)),
            pl.BlockSpec((kv_heads, micro, rows, 256), lambda f: (f, 0, 0, 0)),
            pl.BlockSpec((kv_heads, micro, pairs, 2 * AUG, 128), lambda f: (f, 0, 0, 0, 0)),
            pl.BlockSpec((kv_heads, 64, 64), lambda f: (f, 0, 0)),
            whole((32, total)),
            whole((32, total)),
            whole((total, lanes)),
            pl.BlockSpec((1, lanes, 2 * k_cols), lambda f: (f, 0, 0)),
            whole((total, lanes)),
            whole((total, width)),
        ]
        + [next_spec] * (n_f - 2),
        out_specs=[
            pl.BlockSpec((1, total, 2 * k_cols), lambda f: (f, 0, 0)),
            pl.BlockSpec((1, k_cols, 64), lambda f: (f, 0, 0)),
            whole((total, lanes)),
            pl.BlockSpec((None, 32, 2 * k_cols), lambda f: (f, 0, 0)),
            whole((32, width)),
        ],
        out_shape=[
            jax.ShapeDtypeStruct((n_f, total, 2 * k_cols), BF16),
            jax.ShapeDtypeStruct((n_f, k_cols, 64), F32),
            jax.ShapeDtypeStruct((total, lanes), BF16),
            jax.ShapeDtypeStruct((n_f, 32, 2 * k_cols), F32),
            jax.ShapeDtypeStruct((32, width), F32),
        ],
        scratch_shapes=[pltpu.VMEM((total, lanes), F32)],
        compiler_params=params(60),
        cost_estimate=cost(8 * total * 128 * 128, 8 * MIB),
        name="key_value_back",
    )
    input_back = pl.pallas_call(
        functools.partial(gx_kernel, n_f, depth),
        grid=(n_dp,),
        in_specs=[
            pl.BlockSpec((total, depth), lambda j: (0, j)),
            whole((n_f, total, 2 * k_cols)),
            pl.BlockSpec((n_f, 1, depth, 2 * k_cols), lambda j: (0, j, 0, q_cols // (2 * k_cols))),
            whole((total, lanes)),
            pl.BlockSpec((depth, lanes), lambda j: (j, 0)),
            pl.BlockSpec((total, depth), lambda j: (0, j)),
            whole((total, width)),
            whole((total, width)),
            whole((total, 1)),
            whole((n_dp, 1, depth)),
        ],
        out_specs=[whole((total, width)), pl.BlockSpec((1, depth), lambda j: (0, j))],
        out_shape=[
            jax.ShapeDtypeStruct((total, width), BF16),
            jax.ShapeDtypeStruct((1, width), F32),
        ],
        scratch_shapes=[pltpu.VMEM((n_dp, total, depth), F32), pltpu.VMEM((total, 1), F32)],
        compiler_params=params(60),
        cost_estimate=cost(2 * total * width * 1024, 30 * MIB),
        name="input_gradient",
    )
    def heads_to_input(g_keys, g_message, g_next, gu_q, gh_q):
        gkv, d_fk, gu, d_bkv_t, d_qkv_t = kv_back(
            g_keys, g_message, kv_natural, g_states, fk, cos_t, sin_t, u, b_kv_t, gu_q, h1,
            *g_next,
        )
        gx, dg1 = input_back(
            gh_q, gkv, w_qkv, gu, a_qkv, x, x, gx2, r1, gain_one.reshape(n_dp, 1, depth)
        )
        return gx, dg1, d_fk, d_bkv_t, d_qkv_t

    (gx, dg1, d_fk, d_bkv_t, d_qkv_t), spread_one = together(
        (heads_to_input, g_keys, g_message, g_next, gu_q, gh_q),
        (deal_out, result_one),
    )

    wide = pl.pallas_call(
        table_kernel,
        out_shape=jax.ShapeDtypeStruct((width, lanes), F32),
        compiler_params=pltpu.CompilerParams(vmem_limit_bytes=60 * MIB),
        name="table",
    )(d_fq.reshape(H * 64, 64), d_qkv_t, d_ao_t, d_bq_t, d_bo_t, dg1, dg2)
    kv_rows = KEY_VALUE_HEADS * 64
    d_bk = d_bkv_t[:, rank : 2 * rank, :k_cols].transpose(0, 2, 1).reshape(kv_rows, rank)
    d_bv = d_bkv_t[:, 2 * rank : 3 * rank, k_cols:].transpose(0, 2, 1).reshape(kv_rows, rank)
    narrow = jnp.concatenate(
        [d_fk.reshape(kv_rows, 64), d_bk, d_bv, jnp.zeros((kv_rows, lanes - 80), F32)], axis=1
    )
    wide = wide.reshape(n_all, width // n_all, lanes)
    narrow = narrow.reshape(n_all, kv_rows // n_all, lanes)
    table = jnp.concatenate([wide, narrow], axis=1)
    table, out_one = together(
        (halved, table), (lambda spread, order: deal_in(reordered(spread, order)), spread_one, inverse[1])
    )
    output = [out_zero, out_one]
    wide, narrow = table[: width // n_all], table[width // n_all :]
    shares = (
        wide[:, 64:96],
        wide[:, 96:112],
        narrow[:, 64:80],
        wide[:, :64],
        narrow[:, :64],
        wide[:, 112:114],
    )
    held = jnp.broadcast_to(output[0][None], (micro, rows, width))
    held = lax.dynamic_update_slice(held, output[1][None], (1, 0, 0))
    return (held[None], gx.reshape(1, micro, rows, width), *shares)


def solution(mesh):
    every = ("dp", "fsdp")
    blocks = P("dp", None, "fsdp", None)
    in_specs = (
        blocks,
        blocks,
        P(),
        P(),
        P("dp", "fsdp"),
        P("dp", "fsdp"),
        P("dp", "fsdp"),
        P("fsdp", "dp"),
        P("dp", "fsdp"),
        P("dp", "fsdp"),
        P("fsdp", "dp"),
    ) + (P(every, None),) * 6
    out_specs = (blocks, blocks) + (P(every, None),) * 6
    return jax.shard_map(shards, mesh=mesh, in_specs=in_specs, out_specs=out_specs, check_vma=False)
```
